32 devices in a mesh: regions: 2 (over y), gz: 8 (over z, x), gy: 2 (over core).
Axes of the slice: x: 2, y: 2, z: 4, core: 2. Of those that a mesh axis runs over, the one named last changes fastest.
Arguments:
- iterate: float32 [16, 32, 128, 256], P(None, ('regions', 'gz'), 'gy'), parts along dimension 1, may hold values from -6 to 6
- residual: float32 [16, 32, 128, 256], P(None, ('regions', 'gz'), 'gy'), parts along dimension 1, may hold values from -16 to 16
- labels: int32 [32, 128, 256], P(('regions', 'gz'), 'gy'), parts along dimension 0, may hold values from 0 to 7
- boundary: int32 [32, 128, 256], P(('regions', 'gz'), 'gy'), parts along dimension 0, may hold values 0 or 1
Outputs:
- iterate_out: float32 [16, 32, 128, 256], P(None, ('regions', 'gz'), 'gy'), parts along dimension 1
- residual_out: float32 [16, 32, 128, 256], P(None, ('regions', 'gz'), 'gy'), parts along dimension 1
The draws below stay inside these ranges and needn't reach their ends.
There are 2 independent parts, one for each index of `regions`. The reference program is written for one: setup_inputs(seed, part) draws one part's arguments, and reference() takes and returns one part's arrays. A program takes and returns all parts, laid end to end along the dimension named above; each array names one. Nothing has to cross between parts.
All inputs are finite; a program needn't handle non-finite values. No bound on the sum of `boundary` on one device may be relied on, other than what follows from the above.
Results may differ from the reference program's by a relative error of at most 0.0003.
Values sent between devices are 32-bit elements; how exact they have to be, the bound alone decides.
No kernel may reach another device: no remote copies, remote signals or barrier semaphores. Data moves between devices by JAX's collectives and lax.ppermute only.
A program may use at most 128 MiB of HBM per device.

```python
import math
import jax
import jax.numpy as jnp
from jax import lax

RHS = 16
NCLASS = 8
ITERS = 3
NX = 256
NZ = 16
NY = 128


def draw_residual(key, part):
    base_key = jax.random.fold_in(key, 7)
    scale_key, random_key = jax.random.split(base_key, 2)
    column_scale = jnp.exp(jax.random.uniform(scale_key, (RHS,), jnp.float32, math.log(0.3), math.log(3.0)))
    depth_pos = jnp.arange(NZ, dtype=jnp.float32) / max(NZ - 1, 1)
    depth_scale = jnp.exp((depth_pos - 0.5) * math.log(3.0))
    random_part = jax.random.normal(random_key, (RHS, NZ, NY, NX), jnp.float32)
    values = column_scale[:, None, None, None] * depth_scale[None, :, None, None] * random_part
    return jnp.clip(values, -16.0, 16.0)


def touch_ends(array, own_key, smallest, high):
    shape = array.shape
    index_at = [jax.random.randint(jax.random.fold_in(own_key, axis), (), 0, shape[axis]) for axis in range(len(shape))]
    array = array.at[tuple(index_at)].set(smallest)
    longest = shape.index(max(shape))
    index_at[longest] = (index_at[longest] + 1) % shape[longest]
    return array.at[tuple(index_at)].set(high)


def levels(own_key, dims, cuts, least, largest):
    def one(dim, parts):
        draws = jax.random.uniform(jax.random.fold_in(jax.random.fold_in(own_key, 6), dim), (parts,), jnp.float32, least / len(cuts), largest / len(cuts))
        return jnp.repeat(jnp.exp(draws), dims[dim] // parts).reshape((-1,) + (1,) * (len(dims) - dim - 1))

    level = one(*cuts[0])
    for cut in cuts[1:]:
        level = level * one(*cut)
    return level


def gaussian(own_key, extent, deviation, reach, cuts=(), held_as=jnp.bfloat16):
    factor_of = levels(own_key, extent, cuts, -0.22, 0.18) if cuts else 1.0
    drawn = jax.random.normal(own_key, extent, jnp.float32) * deviation * factor_of
    return jnp.minimum(jnp.maximum(drawn, -reach), reach).astype(held_as)


def setup_inputs(seed: int = 0, part: int = 0) -> dict:
    key_of = jax.random.split(jax.random.key(seed), 5)
    own_keys = jax.random.split(jax.random.fold_in(key_of[4], part), 5)
    iterate = gaussian(own_keys[0], (RHS, NZ, NY, NX), 1.0, 6.0, ((1, 8), (2, 2)), jnp.float32)
    residual = draw_residual(jax.random.fold_in(jax.random.fold_in(key_of[4], part), 71), part)
    labels = touch_ends(jax.random.randint(own_keys[2], (NZ, NY, NX), 0, NCLASS), jax.random.fold_in(own_keys[2], 1), 0, NCLASS - 1).astype(jnp.int32)
    boundary = touch_ends((jax.random.randint(own_keys[3], (NZ, NY, NX), 0, 8) < 1).astype(jnp.int32), jax.random.fold_in(own_keys[3], 1), 0, 1)
    return {"iterate": iterate, "residual": residual, "labels": labels, "boundary": boundary}


contrast_log = 4.0 * math.log(10.0)
highest = lax.Precision.HIGHEST

def shift_cells(block, forward):
    widths = [(0, 0)] * (block.ndim - 1)
    if forward:
        return jnp.pad(block[..., 1:], widths + [(0, 1)])
    return jnp.pad(block[..., :-1], widths + [(1, 0)])

def neighbors(extended):
    center = extended[..., 1:-1, 1:-1, :]
    beside = [extended[..., 2:, 1:-1, :], extended[..., :-2, 1:-1, :], extended[..., 1:-1, 2:, :], extended[..., 1:-1, :-2, :], shift_cells(center, True), shift_cells(center, False)]
    return (center, beside)

def couplings_of(extended):
    coef_center, coef_beside = neighbors(extended[0])
    inner_center, inner_beside = neighbors(extended[1])
    diagonal = jnp.zeros_like(coef_center)
    offsets = []
    for neighbor_coef, neighbor_inner in zip(coef_beside, inner_beside):
        face_coef = jnp.where(neighbor_coef > 0.0, 2.0 * coef_center * neighbor_coef / (coef_center + neighbor_coef), coef_center)
        diagonal = diagonal + face_coef
        offsets.append(inner_center * face_coef * neighbor_inner)
    diagonal = inner_center * diagonal + (1.0 - inner_center)
    return (diagonal, offsets)

def apply_operator(diagonal, offsets, extended):
    center, beside = neighbors(extended)
    coupled = offsets[0] * beside[0]
    for weight, values in zip(offsets[1:], beside[1:]):
        coupled = coupled + weight * values
    return diagonal * center - coupled

def cell_fields(labels, boundary):
    coef = jnp.exp(labels.astype(jnp.float32) * (contrast_log / (NCLASS - 1)))
    interior = (1 - boundary).astype(jnp.float32)
    return jnp.stack([coef, interior])

def gram(left_block, right_block):
    left_flat = left_block.reshape(left_block.shape[0], -1)
    right_flat = right_block.reshape(right_block.shape[0], -1)
    return lax.dot_general(left_flat, right_flat, (((1,), (1,)), ((), ())), precision=highest)

def combine(block, weights):
    flat = block.reshape(block.shape[0], -1)
    mixed = lax.dot_general(weights, flat, (((0,), (0,)), ((), ())), precision=highest)
    return mixed.reshape(block.shape)

def spd_solve(matrix, right):
    factor = jnp.linalg.cholesky(matrix)
    return jax.scipy.linalg.cho_solve((factor, True), right)

def reference(iterate, residual, labels, boundary):
    fields = cell_fields(labels, boundary)
    extended = jnp.pad(fields, ((0, 0), (1, 1), (1, 1), (0, 0)))
    diagonal, offsets = couplings_of(extended)
    inverse_diag = 1.0 / diagonal
    scaled = inverse_diag * residual
    direction = scaled
    summed_rho = gram(residual, scaled)
    for iteration in range(ITERS):
        direction_ext = jnp.pad(direction, ((0, 0), (1, 1), (1, 1), (0, 0)))
        image = apply_operator(diagonal, offsets, direction_ext)
        curvature = gram(direction, image)
        step_size = spd_solve(curvature, summed_rho)
        iterate = iterate + combine(direction, step_size)
        residual = residual - combine(image, step_size)
        if iteration + 1 < ITERS:
            scaled = inverse_diag * residual
            next_rho = gram(residual, scaled)
            momentum = spd_solve(summed_rho, next_rho)
            direction = scaled + combine(direction, momentum)
            summed_rho = next_rho
    return (iterate, residual)
```

```python
import math
from functools import partial

import jax
import jax.numpy as jnp
from jax import lax
from jax.experimental import pallas as pl
from jax.experimental.pallas import tpu as pltpu
from jax.sharding import PartitionSpec as P

NCLASS = 8
ITERS = 3
REACH = ITERS

contrast_log = 4.0 * math.log(10.0)
highest = lax.Precision.HIGHEST
f32 = jnp.float32
bf16 = jnp.bfloat16


def shifted(block, axis, step):
    count = lax.axis_size(axis)
    pairs = [(i, i + step) for i in range(count) if 0 <= i + step < count]
    return lax.ppermute(block, axis, pairs)


def with_rows(block, dim, width):
    size = block.shape[dim]
    head = lax.slice_in_dim(block, 0, width, axis=dim)
    tail = lax.slice_in_dim(block, size - width, size, axis=dim)
    return jnp.concatenate(
        [shifted(tail, "gy", 1), block, shifted(head, "gy", -1)], axis=dim
    )


def all_sum(values, axes):
    for axis in axes:
        count = lax.axis_size(axis)
        if count & (count - 1):
            values = lax.psum(values, axis)
            continue
        step = 1
        while step < count:
            values = values + lax.ppermute(values, axis, [(i, i ^ step) for i in range(count)])
            step *= 2
    return values


def face_of(center, beside):
    return jnp.where(beside > 0.0, 2.0 * center * beside / (center + beside), center)


def symmetric_operator(coef, inner):
    def pad_x(a, forward):
        return jnp.pad(a[..., 1:], ((0, 0), (0, 0), (0, 1))) if forward else jnp.pad(a[..., :-1], ((0, 0), (0, 0), (1, 0)))

    center = coef[1:-1, 1:-1]
    here = inner[1:-1, 1:-1]
    total = jnp.zeros_like(center)
    for beside in (
        coef[2:, 1:-1], coef[:-2, 1:-1], coef[1:-1, 2:], coef[1:-1, :-2], pad_x(center, True), pad_x(center, False)
    ):
        total = total + face_of(center, beside)
    diagonal = here * total + (1.0 - here)
    root = jnp.sqrt(diagonal)
    inverse = 1.0 / root
    masked = here * inverse

    def coupling(a, b, ma, mb):
        return ma * face_of(a, b) * mb

    along_x = coupling(center, pad_x(center, True), masked, pad_x(masked, True))
    along_y = coupling(center[:, :-1], center[:, 1:], masked[:, :-1], masked[:, 1:])
    along_z = coupling(center[:-1], center[1:], masked[:-1], masked[1:])
    return root, inverse, along_x, along_y, along_z


def powers_kernel(
    rows, lo2, lo1, own, hi1, hi2, inverse, sx, sy, sz, moments, split, u0, u1, u2, u3
):
    first = REACH
    scaled = (u0, u1, u2, u3)
    pieces = [(lo2, 0), (lo1, 0), (lo1, 1), (own, 0), (own, 1), (hi1, 0), (hi1, 1), (hi2, 0)]
    depth = own.shape[0]
    planes = len(pieces)

    def distance(plane):
        return max(first - plane, plane - (first + depth - 1), 0)

    for plane, (piece, index) in enumerate(pieces):
        reach = REACH - distance(plane)

        def scale_row(y, carry, plane=plane, piece=piece, index=index):
            u0[plane, y] = piece[index, y] * inverse[plane, pl.ds(y, 1), :]
            return carry

        lax.fori_loop(first - reach, first + rows + reach, scale_row, 0, unroll=2)

    for power in range(1, REACH + 1):
        src, dst = scaled[power - 1], scaled[power]
        for plane in range(planes):
            reach = REACH - power - distance(plane)
            if reach < 0:
                continue

            def apply_row(y, carry, plane=plane, src=src, dst=dst):
                here = src[plane, y]
                ahead = sx[plane, pl.ds(y, 1), :]
                width = here.shape[-1]
                total = ahead * pltpu.roll(here, width - 1, 1) + pltpu.roll(ahead * here, 1, 1)
                total += sy[plane, pl.ds(y, 1), :] * src[plane, y + 1]
                total += sy[plane, pl.ds(y - 1, 1), :] * src[plane, y - 1]
                total += sz[plane, pl.ds(y, 1), :] * src[plane + 1, y]
                total += sz[plane - 1, pl.ds(y, 1), :] * src[plane - 1, y]
                dst[plane, y] = total
                return carry

            lax.fori_loop(first - reach, first + rows + reach, apply_row, 0, unroll=2)

    rhs = own.shape[2]
    height = rhs * (REACH + 1)

    def gram_rows(block, total):
        plane = block // (rows // 4)
        start = (block % (rows // 4)) * 4
        parts = []
        for j in range(4):
            stack = jnp.concatenate([u[plane + first, start + j + first] for u in scaled], axis=0)
            high = stack.astype(bf16)
            low = (stack - high.astype(f32)).astype(bf16)
            both = jnp.concatenate([high, low], axis=0)
            split[plane, start + j] = both
            parts.append(both)
        wide = jnp.concatenate(parts, axis=1)
        return total + lax.dot_general(wide, wide, (((1,), (1,)), ((), ())), preferred_element_type=f32)

    gram = lax.fori_loop(0, depth * rows // 4, gram_rows, jnp.zeros((2 * height, 2 * height), f32))
    gram = gram[:height] + gram[height:]
    gram = gram[:, :height] + gram[:, height:]
    blocks = []
    for power in range(2 * REACH):
        i = power // 2
        j = power - i
        blocks.append(gram[i * rhs : (i + 1) * rhs, j * rhs : (j + 1) * rhs])
    blocks.append(jnp.zeros((rhs, moments.shape[1] - rhs * len(blocks)), f32))
    moments[...] = jnp.concatenate(blocks, axis=1)


def eliminate(stacked, size):
    lane = lax.broadcasted_iota(jnp.int32, (1, size), 1)
    for k in range(size):
        row = stacked[k : k + 1, :]
        column = stacked[:, k : k + 1] * (1.0 / stacked[k : k + 1, k : k + 1])
        stacked = jnp.where(lane == k, column, stacked - column * row)
    return stacked[size:]


def mixing(moments, rhs):
    width = moments.shape[1]
    lane = lax.broadcasted_iota(jnp.int32, (rhs, width), 1)

    def hankel(first, degree):
        rows = []
        for i in range(degree):
            shifted_by = (i + first) * rhs
            rows.append(pltpu.roll(moments, width - shifted_by, 1) if shifted_by else moments)
        rows.append(jnp.zeros((width - degree * rhs, width), f32))
        return jnp.concatenate(rows, axis=0)

    def product(a, b):
        return jnp.dot(a, b, precision=highest, preferred_element_type=f32)

    def quadratic(coefs, matrix):
        return lax.dot_general(
            product(coefs, matrix), coefs, (((1,), (1,)), ((), ())), precision=highest, preferred_element_type=f32
        )

    plain = hankel(0, REACH)
    energy = plain - hankel(1, REACH)
    eye = (lax.broadcasted_iota(jnp.int32, (rhs, rhs), 0) == lax.broadcasted_iota(jnp.int32, (rhs, rhs), 1)).astype(f32)
    direction = (lax.broadcasted_iota(jnp.int32, (rhs, width), 0) == lane).astype(f32)
    residual = direction
    solution_part = jnp.zeros((rhs, width), f32)
    rho = moments[:, :rhs]
    for iteration in range(ITERS):
        curvature = rho - moments[:, rhs : 2 * rhs] if iteration == 0 else quadratic(direction, energy)
        step = eliminate(jnp.concatenate([curvature, rho], axis=0), rhs)
        solution_part = solution_part + product(step, direction)
        image = direction - pltpu.roll(direction, rhs, 1)
        residual = residual - product(step, image)
        if iteration + 1 < ITERS:
            following = quadratic(residual, plain)
            inverse = eliminate(jnp.concatenate([rho, eye], axis=0), rhs)
            direction = residual + product(product(following, inverse), direction)
            rho = following
    return solution_part, residual


def outputs_kernel(moments, split, inverse, root, iterate, iterate_out, residual_out, coefs):
    rhs = iterate.shape[0]
    height = rhs * (REACH + 1)
    rows = split.shape[1]

    @pl.when((pl.program_id(0) == 0) & (pl.program_id(1) == 0))
    def _():
        solution_part, residual = mixing(moments[...], rhs)
        both = jnp.concatenate([solution_part[:, :height], residual[:, :height]], axis=0)
        high = both.astype(bf16).astype(f32)
        stacked = jnp.concatenate([high, both - high], axis=0)
        coefs[...] = jnp.concatenate([stacked, stacked], axis=1).astype(bf16)

    wide = jnp.concatenate([split[0, j] for j in range(rows)], axis=1)
    mixed = jnp.dot(coefs[...], wide, preferred_element_type=f32)
    mixed = mixed[: 2 * rhs] + mixed[2 * rhs :]
    nx = split.shape[-1]
    by_row = jnp.stack([mixed[:, j * nx : (j + 1) * nx] for j in range(rows)], axis=0)
    by_rhs = pltpu.einshape("abc->bac", by_row)
    iterate_out[:, 0] = iterate[:, 0] + by_rhs[:rhs] * inverse[...]
    residual_out[:, 0] = by_rhs[rhs:] * root[...]


def on_device(iterate, residual, labels, boundary):
    rhs, depth, rows, nx = residual.shape
    assert depth == 2 and REACH == 3
    coef = jnp.exp(labels.astype(f32) * (contrast_log / (NCLASS - 1)))
    inner = (1 - boundary).astype(f32)

    fields = with_rows(jnp.stack([coef, inner]), 2, REACH + 1)
    own = with_rows(jnp.transpose(residual, (1, 2, 0, 3)), 1, REACH)

    field_lo1 = shifted(fields, "gz", 1)
    field_hi1 = shifted(fields, "gz", -1)
    field_lo2 = shifted(fields, "gz", 2)
    field_hi2 = shifted(fields, "gz", -2)
    lo1 = shifted(own, "gz", 1)
    hi1 = shifted(own, "gz", -1)
    lo2 = shifted(own[1:], "gz", 2)
    hi2 = shifted(own[:1], "gz", -2)

    fields = jnp.concatenate([field_lo2, field_lo1, fields, field_hi1, field_hi2], axis=1)
    root, inverse, sx, sy, sz = symmetric_operator(fields[0], fields[1])

    planes = depth + 2 * REACH
    extended = rows + 2 * REACH
    vmem = pl.BlockSpec(memory_space=pltpu.VMEM)
    moments, split = pl.pallas_call(
        partial(powers_kernel, rows),
        out_shape=(
            jax.ShapeDtypeStruct((rhs, 128), f32),
            jax.ShapeDtypeStruct((depth, rows, 2 * rhs * (REACH + 1), nx), bf16),
        ),
        in_specs=[vmem] * 9,
        out_specs=(vmem, vmem),
        scratch_shapes=[pltpu.VMEM((planes, extended, rhs, nx), f32)] * 3
        + [pltpu.VMEM((planes, extended, rhs, nx), f32)],
        compiler_params=pltpu.CompilerParams(vmem_limit_bytes=62 * 2**20),
    )(lo2, lo1, own, hi1, hi2, inverse, sx, sy, sz)

    moments = all_sum(moments, ("gy", "gz"))

    inverse = inverse[REACH : REACH + depth, REACH : REACH + rows]
    root = root[REACH : REACH + depth, REACH : REACH + rows]
    tile = 8
    plane_rows = pl.BlockSpec((rhs, 1, tile, nx), lambda z, y: (0, z, y, 0))
    cell_rows = pl.BlockSpec((None, tile, nx), lambda z, y: (z, y, 0))
    return pl.pallas_call(
        outputs_kernel,
        grid=(depth, rows // tile),
        out_shape=(jax.ShapeDtypeStruct(iterate.shape, f32), jax.ShapeDtypeStruct(residual.shape, f32)),
        in_specs=[
            pl.BlockSpec((rhs, 128), lambda z, y: (0, 0)),
            pl.BlockSpec((1, tile) + split.shape[2:], lambda z, y: (z, y, 0, 0)),
            cell_rows,
            cell_rows,
            plane_rows,
        ],
        out_specs=(plane_rows, plane_rows),
        scratch_shapes=[pltpu.VMEM((4 * rhs, 2 * rhs * (REACH + 1)), bf16)],
        compiler_params=pltpu.CompilerParams(vmem_limit_bytes=32 * 2**20),
    )(moments, split, inverse, root, iterate)


def solution(mesh):
    placed = (
        P(None, ("regions", "gz"), "gy", None),
        P(None, ("regions", "gz"), "gy", None),
        P(("regions", "gz"), "gy", None),
        P(("regions", "gz"), "gy", None),
    )
    return jax.shard_map(
        on_device,
        mesh=mesh,
        in_specs=placed,
        out_specs=(P(None, ("regions", "gz"), "gy", None), P(None, ("regions", "gz"), "gy", None)),
        check_vma=False,
    )
```

```python
import math
from functools import partial

import jax
import jax.numpy as jnp
from jax import lax
from jax.experimental import pallas as pl
from jax.experimental.pallas import tpu as pltpu
from jax.sharding import PartitionSpec as P

NCLASS = 8
ITERS = 3
REACH = ITERS

contrast_log = 4.0 * math.log(10.0)
highest = lax.Precision.HIGHEST
f32 = jnp.float32
bf16 = jnp.bfloat16


def moved(block, axis, pairs):
    return lax.ppermute(block, axis, pairs)


def shifted(block, axis, step):
    count = lax.axis_size(axis)
    return moved(block, axis, [(i, i + step) for i in range(count) if 0 <= i + step < count])


def swapped(block):
    return moved(block, "gz", [(i, i ^ 1) for i in range(lax.axis_size("gz"))])


def relayed(block):
    count = lax.axis_size("gz")
    steps = [(i, i + 2 - 4 * (i % 2)) for i in range(count)]
    return moved(block, "gz", [(i, j) for i, j in steps if 0 <= j < count])


def rows_beside(before, after):
    count = lax.axis_size("gy")
    if count != 2:
        return shifted(after, "gy", 1), shifted(before, "gy", -1)
    second = lax.axis_index("gy") == 1
    other = moved(jnp.where(second, before, after), "gy", [(0, 1), (1, 0)])
    zero = jnp.zeros_like(other)
    return jnp.where(second, other, zero), jnp.where(second, zero, other)


def all_sum(values, axes):
    for axis in axes:
        count = lax.axis_size(axis)
        if count & (count - 1):
            values = lax.psum(values, axis)
            continue
        step = 1
        while step < count:
            values = values + lax.ppermute(values, axis, [(i, i ^ step) for i in range(count)])
            step *= 2
    return values


def face_of(center, beside):
    return jnp.where(beside > 0.0, 2.0 * center * beside / (center + beside), center)


def symmetric_operator(coef, inner):
    def pad_x(a, forward):
        return jnp.pad(a[..., 1:], ((0, 0), (0, 0), (0, 1))) if forward else jnp.pad(a[..., :-1], ((0, 0), (0, 0), (1, 0)))

    center = coef[1:-1, 1:-1]
    here = inner[1:-1, 1:-1]
    total = jnp.zeros_like(center)
    for beside in (
        coef[2:, 1:-1], coef[:-2, 1:-1], coef[1:-1, 2:], coef[1:-1, :-2], pad_x(center, True), pad_x(center, False)
    ):
        total = total + face_of(center, beside)
    diagonal = here * total + (1.0 - here)
    root = jnp.sqrt(diagonal)
    inverse = 1.0 / root
    masked = here * inverse

    def coupling(a, b, ma, mb):
        return ma * face_of(a, b) * mb

    along_x = coupling(center, pad_x(center, True), masked, pad_x(masked, True))
    along_y = coupling(center[:, :-1], center[:, 1:], masked[:, :-1], masked[:, 1:])
    along_z = coupling(center[:-1], center[1:], masked[:-1], masked[1:])
    return root, inverse, along_x, along_y, along_z


def row_blocks(start, stop, body, size=8):
    blocks = -(-(stop - start) // size)

    def step(block, carry):
        body(jnp.minimum(start + block * size, stop - size))
        return carry

    lax.fori_loop(0, blocks, step, 0)


def powers_kernel(
    rows, lo3, lo2, lo1, own, hi1, hi2, hi3, inverse, sx, sy, sz, moments, split, u0, u1, u2, u3
):
    first = REACH
    scaled = (u0, u1, u2, u3)
    pieces = [(lo3, 0), (lo2, 0), (lo1, 0), (own, 0), (own, 1), (hi1, 0), (hi2, 0), (hi3, 0)]
    depth = own.shape[0]
    planes = len(pieces)

    def distance(plane):
        return max(first - plane, plane - (first + depth - 1), 0)

    for plane, (piece, index) in enumerate(pieces):
        reach = REACH - distance(plane)
        margin = (piece.shape[1] - rows) // 2

        def scale_rows(y, plane=plane, piece=piece, index=index, margin=margin):
            for j in range(8):
                u0[plane, y + j] = piece[index, y + (j + margin - first)] * inverse[plane, pl.ds(y + j, 1), :]

        row_blocks(first - reach, first + rows + reach, scale_rows)

    for power in range(1, REACH + 1):
        src, dst = scaled[power - 1], scaled[power]
        for plane in range(planes):
            reach = REACH - power - distance(plane)
            if reach < 0:
                continue

            def apply_rows(start, plane=plane, src=src, dst=dst):
                for j in range(8):
                    y = start + j
                    here = src[plane, y]
                    ahead = sx[plane, pl.ds(y, 1), :]
                    width = here.shape[-1]
                    total = ahead * pltpu.roll(here, width - 1, 1) + pltpu.roll(ahead * here, 1, 1)
                    total += sy[plane, pl.ds(y, 1), :] * src[plane, y + 1]
                    total += sy[plane, pl.ds(y - 1, 1), :] * src[plane, y - 1]
                    total += sz[plane, pl.ds(y, 1), :] * src[plane + 1, y]
                    total += sz[plane - 1, pl.ds(y, 1), :] * src[plane - 1, y]
                    dst[plane, y] = total

            row_blocks(first - reach, first + rows + reach, apply_rows)

    rhs = own.shape[2]
    height = rhs * (REACH + 1)

    def gram_rows(block, total):
        plane = block // (rows // 4)
        start = (block % (rows // 4)) * 4
        parts = []
        for j in range(4):
            stack = jnp.concatenate([u[plane + first, start + j + first] for u in scaled], axis=0)
            high = stack.astype(bf16)
            low = (stack - high.astype(f32)).astype(bf16)
            both = jnp.concatenate([high, low], axis=0)
            split[plane, start + j] = both
            parts.append(both)
        wide = jnp.concatenate(parts, axis=1)
        return total + lax.dot_general(wide, wide, (((1,), (1,)), ((), ())), preferred_element_type=f32)

    gram = lax.fori_loop(0, depth * rows // 4, gram_rows, jnp.zeros((2 * height, 2 * height), f32))
    gram = gram[:height] + gram[height:]
    gram = gram[:, :height] + gram[:, height:]
    blocks = []
    for power in range(2 * REACH):
        i = power // 2
        j = power - i
        blocks.append(gram[i * rhs : (i + 1) * rhs, j * rhs : (j + 1) * rhs])
    blocks.append(jnp.zeros((rhs, moments.shape[1] - rhs * len(blocks)), f32))
    moments[...] = jnp.concatenate(blocks, axis=1)


def eliminate(stacked, size):
    lane = lax.broadcasted_iota(jnp.int32, (1, size), 1)
    for k in range(size):
        row = stacked[k : k + 1, :]
        column = stacked[:, k : k + 1] * (1.0 / stacked[k : k + 1, k : k + 1])
        stacked = jnp.where(lane == k, column, stacked - column * row)
    return stacked[size:]


def mixing(moments, rhs):
    width = moments.shape[1]
    lane = lax.broadcasted_iota(jnp.int32, (rhs, width), 1)

    def hankel(first, degree):
        rows = []
        for i in range(degree):
            shifted_by = (i + first) * rhs
            rows.append(pltpu.roll(moments, width - shifted_by, 1) if shifted_by else moments)
        rows.append(jnp.zeros((width - degree * rhs, width), f32))
        return jnp.concatenate(rows, axis=0)

    def product(a, b):
        return jnp.dot(a, b, precision=highest, preferred_element_type=f32)

    def quadratic(coefs, matrix):
        return lax.dot_general(
            product(coefs, matrix), coefs, (((1,), (1,)), ((), ())), precision=highest, preferred_element_type=f32
        )

    plain = hankel(0, REACH)
    energy = plain - hankel(1, REACH)
    eye = (lax.broadcasted_iota(jnp.int32, (rhs, rhs), 0) == lax.broadcasted_iota(jnp.int32, (rhs, rhs), 1)).astype(f32)
    direction = (lax.broadcasted_iota(jnp.int32, (rhs, width), 0) == lane).astype(f32)
    residual = direction
    solution_part = jnp.zeros((rhs, width), f32)
    rho = moments[:, :rhs]
    for iteration in range(ITERS):
        curvature = rho - moments[:, rhs : 2 * rhs] if iteration == 0 else quadratic(direction, energy)
        step = eliminate(jnp.concatenate([curvature, rho], axis=0), rhs)
        solution_part = solution_part + product(step, direction)
        image = direction - pltpu.roll(direction, rhs, 1)
        residual = residual - product(step, image)
        if iteration + 1 < ITERS:
            following = quadratic(residual, plain)
            inverse = eliminate(jnp.concatenate([rho, eye], axis=0), rhs)
            direction = residual + product(product(following, inverse), direction)
            rho = following
    return solution_part, residual


def outputs_kernel(moments, split, inverse, root, iterate, iterate_out, residual_out, coefs):
    rhs = iterate.shape[0]
    height = rhs * (REACH + 1)
    rows = split.shape[1]

    @pl.when((pl.program_id(0) == 0) & (pl.program_id(1) == 0))
    def _():
        solution_part, residual = mixing(moments[...], rhs)
        both = jnp.concatenate([solution_part[:, :height], residual[:, :height]], axis=0)
        high = both.astype(bf16).astype(f32)
        stacked = jnp.concatenate([high, both - high], axis=0)
        coefs[...] = jnp.concatenate([stacked, stacked], axis=1).astype(bf16)

    wide = jnp.concatenate([split[0, j] for j in range(rows)], axis=1)
    mixed = jnp.dot(coefs[...], wide, preferred_element_type=f32)
    mixed = mixed[: 2 * rhs] + mixed[2 * rhs :]
    nx = split.shape[-1]
    by_row = jnp.stack([mixed[:, j * nx : (j + 1) * nx] for j in range(rows)], axis=0)
    by_rhs = pltpu.einshape("abc->bac", by_row)
    iterate_out[:, 0] = iterate[:, 0] + by_rhs[:rhs] * inverse[...]
    residual_out[:, 0] = by_rhs[rhs:] * root[...]


def on_device(iterate, residual, labels, boundary):
    rhs, depth, rows, nx = residual.shape
    assert depth == 2 and REACH == 3
    coef = jnp.exp(labels.astype(f32) * (contrast_log / (NCLASS - 1)))
    inner = (1 - boundary).astype(f32)

    fields = jnp.stack([coef, inner])
    own = jnp.transpose(residual, (1, 2, 0, 3))
    odd = lax.axis_index("gz") % 2 == 1

    wide = REACH + 1

    ends = [
        jnp.concatenate([own[:, a:b].reshape(-1, nx), fields[:, :, c:d].reshape(-1, nx)], axis=0)
        for a, b, c, d in ((0, REACH, 0, wide), (rows - REACH, rows, rows - wide, rows))
    ]
    cut = depth * REACH * rhs
    sides = [
        (side[:cut].reshape(depth, REACH, rhs, nx), side[cut:].reshape(2, depth, wide, nx))
        for side in rows_beside(*ends)
    ]
    fields = jnp.concatenate([sides[0][1], fields, sides[1][1]], axis=2)
    core = own
    own = jnp.concatenate([sides[0][0], own, sides[1][0]], axis=1)
    sent = own[:, 1:-1]

    field_pair = swapped(fields)
    field_lo2 = shifted(fields, "gz", 2)
    field_hi2 = shifted(fields, "gz", -2)
    lo3 = shifted(core[1:], "gz", 2)
    hi3 = shifted(core[:1], "gz", -2)
    pair2 = swapped(jnp.where(odd, sent[1:], sent[:1]))
    pair1 = swapped(jnp.where(odd, sent[:1], sent[1:]))
    field_far = relayed(field_pair)
    far1 = relayed(pair2)
    far2 = relayed(pair1)
    field_lo1 = jnp.where(odd, field_pair, field_far)
    field_hi1 = jnp.where(odd, field_far, field_pair)
    lo1 = jnp.where(odd, pair1, far1)
    lo2 = jnp.where(odd, pair2, far2)
    hi1 = jnp.where(odd, far1, pair1)
    hi2 = jnp.where(odd, far2, pair2)

    fields = jnp.concatenate([field_lo2, field_lo1, fields, field_hi1, field_hi2], axis=1)
    root, inverse, sx, sy, sz = symmetric_operator(fields[0], fields[1])

    planes = depth + 2 * REACH
    extended = rows + 2 * REACH
    vmem = pl.BlockSpec(memory_space=pltpu.VMEM)
    moments, split = pl.pallas_call(
        partial(powers_kernel, rows),
        out_shape=(
            jax.ShapeDtypeStruct((rhs, 128), f32),
            jax.ShapeDtypeStruct((depth, rows, 2 * rhs * (REACH + 1), nx), bf16),
        ),
        in_specs=[vmem] * 11,
        out_specs=(vmem, vmem),
        scratch_shapes=[pltpu.VMEM((planes, extended, rhs, nx), f32)] * 3
        + [pltpu.VMEM((planes, extended, rhs, nx), f32)],
        compiler_params=pltpu.CompilerParams(vmem_limit_bytes=62 * 2**20),
    )(lo3, lo2, lo1, own, hi1, hi2, hi3, inverse, sx, sy, sz)

    moments = all_sum(moments, ("gy", "gz"))

    inverse = inverse[REACH : REACH + depth, REACH : REACH + rows]
    root = root[REACH : REACH + depth, REACH : REACH + rows]
    tile = 8
    plane_rows = pl.BlockSpec((rhs, 1, tile, nx), lambda z, y: (0, z, y, 0))
    cell_rows = pl.BlockSpec((None, tile, nx), lambda z, y: (z, y, 0))
    return pl.pallas_call(
        outputs_kernel,
        grid=(depth, rows // tile),
        out_shape=(jax.ShapeDtypeStruct(iterate.shape, f32), jax.ShapeDtypeStruct(residual.shape, f32)),
        in_specs=[
            pl.BlockSpec((rhs, 128), lambda z, y: (0, 0)),
            pl.BlockSpec((1, tile) + split.shape[2:], lambda z, y: (z, y, 0, 0)),
            cell_rows,
            cell_rows,
            plane_rows,
        ],
        out_specs=(plane_rows, plane_rows),
        scratch_shapes=[pltpu.VMEM((4 * rhs, 2 * rhs * (REACH + 1)), bf16)],
        compiler_params=pltpu.CompilerParams(vmem_limit_bytes=32 * 2**20),
    )(moments, split, inverse, root, iterate)


def solution(mesh):
    placed = (
        P(None, ("regions", "gz"), "gy", None),
        P(None, ("regions", "gz"), "gy", None),
        P(("regions", "gz"), "gy", None),
        P(("regions", "gz"), "gy", None),
    )
    return jax.shard_map(
        on_device,
        mesh=mesh,
        in_specs=placed,
        out_specs=(P(None, ("regions", "gz"), "gy", None), P(None, ("regions", "gz"), "gy", None)),
        check_vma=False,
    )
```

```python
import math
from functools import partial

import jax
import jax.numpy as jnp
from jax import lax
from jax.experimental import pallas as pl
from jax.experimental.pallas import tpu as pltpu
from jax.sharding import PartitionSpec as P

NCLASS = 8
ITERS = 3
REACH = ITERS

contrast_log = 4.0 * math.log(10.0)
highest = lax.Precision.HIGHEST
f32 = jnp.float32
bf16 = jnp.bfloat16


def moved(block, axis, pairs):
    return lax.ppermute(block, axis, pairs)


def shifted(block, axis, step):
    count = lax.axis_size(axis)
    return moved(block, axis, [(i, i + step) for i in range(count) if 0 <= i + step < count])


def swapped(block):
    return moved(block, "gz", [(i, i ^ 1) for i in range(lax.axis_size("gz"))])


def relayed(block, back=False):
    count = lax.axis_size("gz")
    steps = [(i, i + 2 - 4 * (i % 2)) for i in range(count)]
    pairs = [(i, j) for i, j in steps if 0 <= j < count]
    return moved(block, "gz", [(j, i) for i, j in pairs] if back else pairs)


def after(value, *earlier):
    return lax.optimization_barrier((value,) + earlier)[0]


def rows_beside(before, after):
    count = lax.axis_size("gy")
    if count != 2:
        return shifted(after, "gy", 1), shifted(before, "gy", -1)
    second = lax.axis_index("gy") == 1
    other = moved(jnp.where(second, before, after), "gy", [(0, 1), (1, 0)])
    zero = jnp.zeros_like(other)
    return jnp.where(second, other, zero), jnp.where(second, zero, other)


def all_sum(values, axes):
    for axis in axes:
        count = lax.axis_size(axis)
        if count & (count - 1):
            values = lax.psum(values, axis)
            continue
        step = 1
        while step < count:
            values = values + lax.ppermute(values, axis, [(i, i ^ step) for i in range(count)])
            step *= 2
    return values


def face_of(center, beside):
    return jnp.where(beside > 0.0, 2.0 * center * beside / (center + beside), center)


def symmetric_operator(coef, inner):
    def pad_x(a, forward):
        return jnp.pad(a[..., 1:], ((0, 0), (0, 0), (0, 1))) if forward else jnp.pad(a[..., :-1], ((0, 0), (0, 0), (1, 0)))

    center = coef[1:-1, 1:-1]
    here = inner[1:-1, 1:-1]
    total = jnp.zeros_like(center)
    for beside in (
        coef[2:, 1:-1], coef[:-2, 1:-1], coef[1:-1, 2:], coef[1:-1, :-2], pad_x(center, True), pad_x(center, False)
    ):
        total = total + face_of(center, beside)
    diagonal = here * total + (1.0 - here)
    root = jnp.sqrt(diagonal)
    inverse = 1.0 / root
    masked = here * inverse

    def coupling(a, b, ma, mb):
        return ma * face_of(a, b) * mb

    along_x = coupling(center, pad_x(center, True), masked, pad_x(masked, True))
    along_y = coupling(center[:, :-1], center[:, 1:], masked[:, :-1], masked[:, 1:])
    along_z = coupling(center[:-1], center[1:], masked[:-1], masked[1:])
    return root, inverse, along_x, along_y, along_z


def row_blocks(start, stop, body, size=8):
    blocks = -(-(stop - start) // size)

    def step(block, carry):
        body(jnp.minimum(start + block * size, stop - size))
        return carry

    lax.fori_loop(0, blocks, step, 0)


def apply_rows(operator, plane, start, before, here, after, size=8):
    sx, sy, sz = operator
    out = []
    for j in range(size):
        y = start + j
        ref, index = here
        center = ref[index, y]
        ahead = sx[plane, pl.ds(y, 1), :]
        width = center.shape[-1]
        total = ahead * pltpu.roll(center, width - 1, 1) + pltpu.roll(ahead * center, 1, 1)
        total += sy[plane, pl.ds(y, 1), :] * ref[index, y + 1]
        total += sy[plane, pl.ds(y - 1, 1), :] * ref[index, y - 1]
        total += sz[plane, pl.ds(y, 1), :] * after[0][after[1], y]
        total += sz[plane - 1, pl.ds(y, 1), :] * before[0][before[1], y]
        out.append(total)
    return out


def spread(plane, depth=2):
    return max(REACH - plane, plane - (REACH + depth - 1), 0)


def scale_plane(rows, plane, piece, inverse, dst):
    reach = REACH - spread(plane)
    ref, index = piece
    out, place = dst
    shift = (ref.shape[1] - rows) // 2 - REACH

    def body(y):
        for j in range(8):
            out[place, y + j] = ref[index, y + (j + shift)] * inverse[plane, pl.ds(y + j, 1), :]

    row_blocks(REACH - reach, REACH + rows + reach, body)


def apply_plane(rows, power, plane, operator, fields):
    reach = REACH - power - spread(plane)
    src = [fields[power - 1, plane + offset] for offset in (-1, 0, 1)]
    out, place = fields[power, plane]

    def body(y):
        for j, values in enumerate(apply_rows(operator, plane, y, *src)):
            out[place, y + j] = values

    row_blocks(REACH - reach, REACH + rows + reach, body)


LATE = 1


def early_kernel(rows, far3, far1, own, near1, near2, near3, inverse, sx, sy, sz, u0_out, u1_out, u2_out, u0, u1):
    operator = (sx, sy, sz)
    fields = {(0, plane): (u0_out, plane) for plane in range(5)}
    fields.update({(0, plane): (u0, plane - 5) for plane in range(5, 8)})
    fields.update({(1, 3): (u1_out, 0), (1, 4): (u1_out, 1), (1, 5): (u1, 0), (1, 6): (u1, 1)})
    fields.update({(2, 4): (u2_out, 0), (2, 5): (u2_out, 1)})
    pieces = {0: (far3, 0), 2: (far1, 0), 3: (own, 0), 4: (own, 1), 5: (near1, 0), 6: (near2, 0), 7: (near3, 0)}
    for plane, piece in pieces.items():
        scale_plane(rows, plane, piece, inverse, fields[0, plane])
    for power, plane in ((1, 3), (1, 4), (1, 5), (1, 6), (2, 4), (2, 5)):
        apply_plane(rows, power, plane, operator, fields)


def late_kernel(rows, far2a, far2b, u0_in, u1_in, u2_in, inverse, sx, sy, sz, moments, split, u0, u1, u2):
    operator = (sx, sy, sz)
    fields = {(0, plane): (u0_in, plane) for plane in range(5)}
    fields[0, LATE] = (u0, 0)
    fields.update({(1, 1): (u1, 0), (1, 2): (u1, 1), (1, 3): (u1_in, 0), (1, 4): (u1_in, 1)})
    fields.update({(2, 2): (u2, 0), (2, 3): (u2, 1), (2, 4): (u2_in, 0), (2, 5): (u2_in, 1)})

    reach = REACH - spread(LATE)
    shift = (far2a.shape[1] - rows) // 2 - REACH
    part = far2a.shape[2]

    def scale(y):
        for j in range(8):
            factor = inverse[LATE, pl.ds(y + j, 1), :]
            u0[0, y + j, :part] = far2a[0, y + (j + shift)] * factor
            u0[0, y + j, part:] = far2b[0, y + (j + shift)] * factor

    row_blocks(REACH - reach, REACH + rows + reach, scale)
    for power, plane in ((1, 1), (1, 2), (2, 2), (2, 3)):
        apply_plane(rows, power, plane, operator, fields)

    rhs = u0.shape[2]
    height = rhs * (REACH + 1)
    gram = jnp.zeros((2 * height, 2 * height), f32)
    for plane in range(2):
        level = plane + REACH

        def gram_rows(block, total, plane=plane, level=level):
            start = block * 8
            y = start + REACH
            last = apply_rows(operator, level, y, *[fields[2, level + offset] for offset in (-1, 0, 1)])
            parts = []
            for j in range(8):
                lower = [fields[power, level] for power in range(REACH)]
                stack = jnp.concatenate([ref[index, y + j] for ref, index in lower] + [last[j]], axis=0)
                high = stack.astype(bf16)
                low = (stack - high.astype(f32)).astype(bf16)
                both = jnp.concatenate([high, low], axis=0)
                split[plane, start + j] = both
                parts.append(both)
            wide = jnp.concatenate(parts, axis=1)
            return total + lax.dot_general(wide, wide, (((1,), (1,)), ((), ())), preferred_element_type=f32)

        gram = lax.fori_loop(0, rows // 8, gram_rows, gram)
    gram = gram[:height] + gram[height:]
    gram = gram[:, :height] + gram[:, height:]
    blocks = []
    for power in range(2 * REACH):
        i = power // 2
        j = power - i
        blocks.append(gram[i * rhs : (i + 1) * rhs, j * rhs : (j + 1) * rhs])
    blocks.append(jnp.zeros((rhs, moments.shape[1] - rhs * len(blocks)), f32))
    moments[...] = jnp.concatenate(blocks, axis=1)


def eliminate(stacked, size):
    lane = lax.broadcasted_iota(jnp.int32, (1, size), 1)
    for k in range(size):
        row = stacked[k : k + 1, :]
        column = stacked[:, k : k + 1] * (1.0 / stacked[k : k + 1, k : k + 1])
        stacked = jnp.where(lane == k, column, stacked - column * row)
    return stacked[size:]


def mixing(moments, rhs):
    width = moments.shape[1]
    lane = lax.broadcasted_iota(jnp.int32, (rhs, width), 1)

    def hankel(first, degree):
        rows = []
        for i in range(degree):
            shifted_by = (i + first) * rhs
            rows.append(pltpu.roll(moments, width - shifted_by, 1) if shifted_by else moments)
        rows.append(jnp.zeros((width - degree * rhs, width), f32))
        return jnp.concatenate(rows, axis=0)

    def product(a, b):
        return jnp.dot(a, b, precision=highest, preferred_element_type=f32)

    def quadratic(coefs, matrix):
        return lax.dot_general(
            product(coefs, matrix), coefs, (((1,), (1,)), ((), ())), precision=highest, preferred_element_type=f32
        )

    plain = hankel(0, REACH)
    energy = plain - hankel(1, REACH)
    eye = (lax.broadcasted_iota(jnp.int32, (rhs, rhs), 0) == lax.broadcasted_iota(jnp.int32, (rhs, rhs), 1)).astype(f32)
    direction = (lax.broadcasted_iota(jnp.int32, (rhs, width), 0) == lane).astype(f32)
    residual = direction
    solution_part = jnp.zeros((rhs, width), f32)
    rho = moments[:, :rhs]
    for iteration in range(ITERS):
        curvature = rho - moments[:, rhs : 2 * rhs] if iteration == 0 else quadratic(direction, energy)
        step = eliminate(jnp.concatenate([curvature, rho], axis=0), rhs)
        solution_part = solution_part + product(step, direction)
        image = direction - pltpu.roll(direction, rhs, 1)
        residual = residual - product(step, image)
        if iteration + 1 < ITERS:
            following = quadratic(residual, plain)
            inverse = eliminate(jnp.concatenate([rho, eye], axis=0), rhs)
            direction = residual + product(product(following, inverse), direction)
            rho = following
    return solution_part, residual


def outputs_kernel(odd, moments, split, inverse, root, iterate, iterate_out, residual_out, coefs):
    rhs = iterate.shape[0]
    height = rhs * (REACH + 1)
    rows = split.shape[1]

    @pl.when((pl.program_id(0) == 0) & (pl.program_id(1) == 0))
    def _():
        solution_part, residual = mixing(moments[...], rhs)
        both = jnp.concatenate([solution_part[:, :height], residual[:, :height]], axis=0)
        high = both.astype(bf16).astype(f32)
        stacked = jnp.concatenate([high, both - high], axis=0)
        coefs[...] = jnp.concatenate([stacked, stacked], axis=1).astype(bf16)

    wide = jnp.concatenate([split[0, j] for j in range(rows)], axis=1)
    mixed = jnp.dot(coefs[...], wide, preferred_element_type=f32)
    mixed = mixed[: 2 * rhs] + mixed[2 * rhs :]
    nx = split.shape[-1]
    by_row = jnp.stack([mixed[:, j * nx : (j + 1) * nx] for j in range(rows)], axis=0)
    by_rhs = pltpu.einshape("abc->bac", by_row)
    iterate_out[:, 0] = iterate[:, 0] + by_rhs[:rhs] * inverse[...]
    residual_out[:, 0] = by_rhs[rhs:] * root[...]


def on_device(iterate, residual, labels, boundary):
    rhs, depth, rows, nx = residual.shape
    assert depth == 2 and REACH == 3 and lax.axis_size("gz") % 2 == 0
    half = rhs // 2
    odd = lax.axis_index("gz") % 2 == 1

    def mirrored(block, dim):
        return jnp.where(odd, jnp.flip(block, dim), block)

    cells = jnp.stack([labels, boundary])
    cells = mirrored(cells, 1)
    coef = jnp.exp(cells[0].astype(f32) * (contrast_log / (NCLASS - 1)))
    inner = (1 - cells[1]).astype(f32)
    fields = jnp.stack([coef, inner])
    field_pair = swapped(fields)
    field_far = relayed(jnp.concatenate([coef, inner[1:]], axis=0))
    field_near = relayed(jnp.concatenate([coef, inner[:1]], axis=0), back=True)

    own = mirrored(jnp.transpose(residual, (1, 2, 0, 3)), 0)
    core = after(own, field_far, field_near)
    far3 = relayed(core[1:])
    near3 = relayed(core[:1], back=True)
    before, behind = rows_beside(own[:, :REACH], own[:, -REACH:])
    own = jnp.concatenate([before, own, behind], axis=1)
    sent = after(own, field_pair)[:, 1:-1]
    near2 = swapped(sent[:1])
    field_relay = relayed(field_pair)
    sent = after(sent, field_relay)
    near1a = swapped(sent[1:, :, :half])
    near1b = swapped(sent[1:, :, half:])
    far1 = relayed(near2)
    far2a = relayed(near1a)
    far2b = relayed(near1b)
    near1 = jnp.concatenate([near1a, near1b], axis=2)

    none = jnp.zeros_like(coef[:1])
    coef = jnp.concatenate(
        [
            field_far[:2], field_relay[0, 1:], field_relay[0, :1], coef,
            field_pair[0, 1:], field_pair[0, :1], field_near[:2],
        ],
        axis=0,
    )
    inner = jnp.concatenate(
        [
            none, field_far[2:], field_relay[1, 1:], field_relay[1, :1], inner,
            field_pair[1, 1:], field_pair[1, :1], field_near[2:], none,
        ],
        axis=0,
    )
    fields = jnp.stack([coef, inner])
    wide = REACH + 1
    before, behind = rows_beside(fields[:, :, :wide], fields[:, :, -wide:])
    fields = jnp.concatenate([before, fields, behind], axis=2)
    root, inverse, sx, sy, sz = symmetric_operator(fields[0], fields[1])

    extended = rows + 2 * REACH
    vmem = pl.BlockSpec(memory_space=pltpu.VMEM)

    def planes(count):
        return (count, extended, rhs, nx)

    u0, u1, u2 = pl.pallas_call(
        partial(early_kernel, rows),
        out_shape=tuple(jax.ShapeDtypeStruct(planes(count), f32) for count in (5, 2, 2)),
        in_specs=[vmem] * 10,
        out_specs=(vmem,) * 3,
        scratch_shapes=[pltpu.VMEM(planes(count), f32) for count in (3, 2)],
        compiler_params=pltpu.CompilerParams(vmem_limit_bytes=40 * 2**20),
        cost_estimate=pl.CostEstimate(flops=0, bytes_accessed=50 * 2**20, transcendentals=0),
    )(far3, far1, own, near1, near2, near3, inverse, sx, sy, sz)

    moments, split = pl.pallas_call(
        partial(late_kernel, rows),
        out_shape=(
            jax.ShapeDtypeStruct((rhs, 128), f32),
            jax.ShapeDtypeStruct((depth, rows, 2 * rhs * (REACH + 1), nx), bf16),
        ),
        in_specs=[vmem] * 9,
        out_specs=(vmem, vmem),
        scratch_shapes=[pltpu.VMEM(planes(count), f32) for count in (1, 2, 2)],
        compiler_params=pltpu.CompilerParams(vmem_limit_bytes=40 * 2**20),
        cost_estimate=pl.CostEstimate(flops=0, bytes_accessed=50 * 2**20, transcendentals=0),
    )(far2a, far2b, u0, u1, u2, inverse, sx, sy, sz)

    moments = all_sum(moments, ("gy", "gz"))

    inverse = inverse[REACH : REACH + depth, REACH : REACH + rows]
    root = root[REACH : REACH + depth, REACH : REACH + rows]
    tile = 8
    plane_rows = pl.BlockSpec((rhs, 1, tile, nx), lambda z, y, odd: (0, jnp.bitwise_xor(z, odd[0]), y, 0))
    cell_rows = pl.BlockSpec((None, tile, nx), lambda z, y, odd: (z, y, 0))
    return pl.pallas_call(
        outputs_kernel,
        out_shape=(jax.ShapeDtypeStruct(iterate.shape, f32), jax.ShapeDtypeStruct(residual.shape, f32)),
        grid_spec=pltpu.PrefetchScalarGridSpec(
            num_scalar_prefetch=1,
            grid=(depth, rows // tile),
            in_specs=[
                pl.BlockSpec((rhs, 128), lambda z, y, odd: (0, 0)),
                pl.BlockSpec((1, tile) + split.shape[2:], lambda z, y, odd: (z, y, 0, 0)),
                cell_rows,
                cell_rows,
                plane_rows,
            ],
            out_specs=(plane_rows, plane_rows),
            scratch_shapes=[pltpu.VMEM((4 * rhs, 2 * rhs * (REACH + 1)), bf16)],
        ),
        compiler_params=pltpu.CompilerParams(vmem_limit_bytes=32 * 2**20),
    )(odd.astype(jnp.int32).reshape(1), moments, split, inverse, root, iterate)


def solution(mesh):
    placed = (
        P(None, ("regions", "gz"), "gy", None),
        P(None, ("regions", "gz"), "gy", None),
        P(("regions", "gz"), "gy", None),
        P(("regions", "gz"), "gy", None),
    )
    return jax.shard_map(
        on_device,
        mesh=mesh,
        in_specs=placed,
        out_specs=(P(None, ("regions", "gz"), "gy", None), P(None, ("regions", "gz"), "gy", None)),
        check_vma=False,
    )
```

```python
import math
from functools import partial

import jax
import jax.numpy as jnp
from jax import lax
from jax.experimental import pallas as pl
from jax.experimental.pallas import tpu as pltpu
from jax.sharding import PartitionSpec as P

NCLASS = 8
ITERS = 3
REACH = ITERS

contrast_log = 4.0 * math.log(10.0)
highest = lax.Precision.HIGHEST
f32 = jnp.float32
bf16 = jnp.bfloat16


def moved(block, axis, pairs):
    return lax.ppermute(block, axis, pairs)


def shifted(block, axis, step):
    count = lax.axis_size(axis)
    return moved(block, axis, [(i, i + step) for i in range(count) if 0 <= i + step < count])


def swapped(block):
    return moved(block, "gz", [(i, i ^ 1) for i in range(lax.axis_size("gz"))])


def swapped_far(block):
    count = lax.axis_size("gz")
    steps = [(i, i - 1 + 2 * (i % 2)) for i in range(count)]
    return moved(block, "gz", [(i, j) for i, j in steps if 0 <= j < count])


def relayed(block, back=False):
    count = lax.axis_size("gz")
    steps = [(i, i + 2 - 4 * (i % 2)) for i in range(count)]
    pairs = [(i, j) for i, j in steps if 0 <= j < count]
    return moved(block, "gz", [(j, i) for i, j in pairs] if back else pairs)


def after(value, *earlier):
    here = True
    for block in earlier:
        here = here & (block[(0,) * block.ndim] >= jnp.finfo(f32).min)
    return jnp.where(here, value, 0.0)


def rows_beside(before, after):
    count = lax.axis_size("gy")
    if count != 2:
        return shifted(after, "gy", 1), shifted(before, "gy", -1)
    second = lax.axis_index("gy") == 1
    other = moved(jnp.where(second, before, after), "gy", [(0, 1), (1, 0)])
    zero = jnp.zeros_like(other)
    return jnp.where(second, other, zero), jnp.where(second, zero, other)


def all_sum(values, axes):
    for axis in axes:
        count = lax.axis_size(axis)
        if count & (count - 1):
            values = lax.psum(values, axis)
            continue
        step = 1
        while step < count:
            values = values + lax.ppermute(values, axis, [(i, i ^ step) for i in range(count)])
            step *= 2
    return values


def face_of(center, beside):
    return jnp.where(beside > 0.0, 2.0 * center * beside / (center + beside), center)


def symmetric_operator(coef, inner):
    def pad_x(a, forward):
        return jnp.pad(a[..., 1:], ((0, 0), (0, 0), (0, 1))) if forward else jnp.pad(a[..., :-1], ((0, 0), (0, 0), (1, 0)))

    center = coef[1:-1, 1:-1]
    here = inner[1:-1, 1:-1]
    total = jnp.zeros_like(center)
    for beside in (
        coef[2:, 1:-1], coef[:-2, 1:-1], coef[1:-1, 2:], coef[1:-1, :-2], pad_x(center, True), pad_x(center, False)
    ):
        total = total + face_of(center, beside)
    diagonal = here * total + (1.0 - here)
    root = jnp.sqrt(diagonal)
    inverse = 1.0 / root
    masked = here * inverse

    def coupling(a, b, ma, mb):
        return ma * face_of(a, b) * mb

    along_x = coupling(center, pad_x(center, True), masked, pad_x(masked, True))
    along_y = coupling(center[:, :-1], center[:, 1:], masked[:, :-1], masked[:, 1:])
    along_z = coupling(center[:-1], center[1:], masked[:-1], masked[1:])
    return root, inverse, along_x, along_y, along_z


def row_blocks(start, stop, body, size=8):
    blocks = -(-(stop - start) // size)

    def step(block, carry):
        body(jnp.minimum(start + block * size, stop - size))
        return carry

    lax.fori_loop(0, blocks, step, 0)


def apply_rows(operator, plane, start, before, here, after, size=8):
    sx, sy, sz = operator
    ref, index = here
    out = []
    last, center = ref[index, start - 1], ref[index, start]
    below = sy[plane, pl.ds(start - 1, 1), :]
    width = center.shape[-1]
    for j in range(size):
        y = start + j
        following = ref[index, y + 1]
        above = sy[plane, pl.ds(y, 1), :]
        ahead = sx[plane, pl.ds(y, 1), :]
        total = ahead * pltpu.roll(center, width - 1, 1) + pltpu.roll(ahead * center, 1, 1)
        total += above * following + below * last
        total += sz[plane, pl.ds(y, 1), :] * after[0][after[1], y]
        total += sz[plane - 1, pl.ds(y, 1), :] * before[0][before[1], y]
        out.append(total)
        last, center, below = center, following, above
    return out


def spread(plane, depth=2):
    return max(REACH - plane, plane - (REACH + depth - 1), 0)


def scale_plane(rows, plane, piece, inverse, dst):
    reach = REACH - spread(plane)
    ref, index = piece
    out, place = dst
    shift = (ref.shape[1] - rows) // 2 - REACH

    def body(y):
        for j in range(8):
            out[place, y + j] = ref[index, y + (j + shift)] * inverse[plane, pl.ds(y + j, 1), :]

    row_blocks(REACH - reach, REACH + rows + reach, body)


def apply_plane(rows, power, plane, operator, fields):
    reach = REACH - power - spread(plane)
    src = [fields[power - 1, plane + offset] for offset in (-1, 0, 1)]
    out, place = fields[power, plane]

    def body(y):
        for j, values in enumerate(apply_rows(operator, plane, y, *src)):
            out[place, y + j] = values

    row_blocks(REACH - reach, REACH + rows + reach, body)


LATE = 1


def halves(blocks):
    stack = jnp.concatenate(blocks, axis=0)
    high = stack.astype(bf16)
    low = (stack - high.astype(f32)).astype(bf16)
    return jnp.concatenate([high, low], axis=0)


def inner_products(left, right):
    return lax.dot_general(left, right, (((1,), (1,)), ((), ())), preferred_element_type=f32)


def whole(gram, left, right):
    gram = gram[:left] + gram[left : 2 * left]
    return gram[:, :right] + gram[:, right : 2 * right]


def early_kernel(
    rows, far3, far1, own, near1, near2, near3, inverse, sx, sy, sz,
    u0_out, u1_out, u2_out, split, moments, u0, u1,
):
    operator = (sx, sy, sz)
    fields = {(0, plane): (u0_out, plane) for plane in range(5)}
    fields.update({(0, plane): (u0, plane - 5) for plane in range(5, 8)})
    fields.update({(1, 3): (u1_out, 0), (1, 4): (u1_out, 1), (1, 5): (u1, 0), (1, 6): (u1, 1)})
    fields.update({(2, 4): (u2_out, 0), (2, 5): (u2_out, 1)})
    pieces = {0: (far3, 0), 2: (far1, 0), 3: (own, 0), 4: (own, 1), 5: (near1, 0), 6: (near2, 0), 7: (near3, 0)}
    for plane, piece in pieces.items():
        scale_plane(rows, plane, piece, inverse, fields[0, plane])
    for power, plane in ((1, 3), (1, 4), (1, 5), (1, 6), (2, 4), (2, 5)):
        apply_plane(rows, power, plane, operator, fields)

    rhs = u0.shape[2]
    gram = jnp.zeros((4 * rhs, 4 * rhs), f32)
    for plane in range(2):

        def gram_rows(block, total, plane=plane):
            parts = []
            for j in range(8):
                y = block * 8 + j
                sources = [fields[power, plane + REACH] for power in range(2)]
                both = halves([ref[index, y + REACH] for ref, index in sources])
                split[plane, y] = both
                parts.append(both)
            wide = jnp.concatenate(parts, axis=1)
            return total + inner_products(wide, wide)

        gram = lax.fori_loop(0, rows // 8, gram_rows, gram)
    gram = whole(gram, 2 * rhs, 2 * rhs)
    moments[:, : 2 * rhs] = gram[:rhs]
    moments[:, 2 * rhs : 3 * rhs] = gram[rhs:, rhs:]


def late_kernel(
    rows, far2a, far2b, u0_in, u1_in, u2_in, split_in, moments_in, inverse, sx, sy, sz, moments, split, u0, u1, u2
):
    operator = (sx, sy, sz)
    fields = {(0, plane): (u0_in, plane) for plane in range(5)}
    fields[0, LATE] = (u0, 0)
    fields.update({(1, 1): (u1, 0), (1, 2): (u1, 1), (1, 3): (u1_in, 0), (1, 4): (u1_in, 1)})
    fields.update({(2, 2): (u2, 0), (2, 3): (u2, 1), (2, 4): (u2_in, 0), (2, 5): (u2_in, 1)})

    reach = REACH - spread(LATE)
    shift = (far2a.shape[1] - rows) // 2 - REACH
    part = far2a.shape[2]

    def scale(y):
        for j in range(8):
            factor = inverse[LATE, pl.ds(y + j, 1), :]
            u0[0, y + j, :part] = far2a[0, y + (j + shift)] * factor
            u0[0, y + j, part:] = far2b[0, y + (j + shift)] * factor

    row_blocks(REACH - reach, REACH + rows + reach, scale)
    for power, plane in ((1, 1), (1, 2), (2, 2), (2, 3)):
        apply_plane(rows, power, plane, operator, fields)

    rhs = u0.shape[2]
    gram = jnp.zeros((6 * rhs, 2 * rhs), f32)
    for plane in range(2):
        level = plane + REACH

        def gram_rows(block, total, plane=plane, level=level):
            start = block * 8
            y = start + REACH
            last = apply_rows(operator, level, y, *[fields[2, level + offset] for offset in (-1, 0, 1)])
            left, right = [], []
            for j in range(8):
                ref, index = fields[2, level]
                both = halves([ref[index, y + j], last[j]])
                split[plane, start + j] = both
                first = [split_in[plane, start + j, part * rhs : (part + 1) * rhs] for part in (1, 3)]
                left.append(jnp.concatenate(first + [both], axis=0))
                right.append(jnp.concatenate([both[:rhs], both[2 * rhs : 3 * rhs]], axis=0))
            return total + inner_products(jnp.concatenate(left, axis=1), jnp.concatenate(right, axis=1))

        gram = lax.fori_loop(0, rows // 8, gram_rows, gram)
    gram = gram[:, :rhs] + gram[:, rhs:]
    blocks = [gram[part * rhs : (part + 1) * rhs] for part in range(6)]
    moments[:, : 3 * rhs] = moments_in[:, : 3 * rhs]
    moments[:, 3 * rhs : 4 * rhs] = blocks[0] + blocks[1]
    moments[:, 4 * rhs : 5 * rhs] = blocks[2] + blocks[4]
    moments[:, 5 * rhs : 6 * rhs] = blocks[3] + blocks[5]
    moments[:, 6 * rhs :] = jnp.zeros((rhs, moments.shape[1] - 6 * rhs), f32)


def eliminate(stacked, size):
    lane = lax.broadcasted_iota(jnp.int32, (1, stacked.shape[1]), 1)
    done = 0
    for k in range(0, size, 2):
        if k - done == 8:
            stacked, done = stacked[8:], k
        at = k - done
        row0, row1 = stacked[at : at + 1, :], stacked[at + 1 : at + 2, :]
        col0, col1 = stacked[:, k : k + 1], stacked[:, k + 1 : k + 2]
        a, b = row0[:, k : k + 1], row0[:, k + 1 : k + 2]
        c, d = row1[:, k : k + 1], row1[:, k + 1 : k + 2]
        scale = 1.0 / (a * d - b * c)
        new0 = col0 * (d * scale) - col1 * (c * scale)
        new1 = col1 * (a * scale) - col0 * (b * scale)
        rest = stacked - new0 * row0 - new1 * row1
        stacked = jnp.where(lane == k, new0, jnp.where(lane == k + 1, new1, rest))
    return stacked[size - done :]


def mixing(moments, rhs):
    width = moments.shape[1]
    lane = lax.broadcasted_iota(jnp.int32, (rhs, width), 1)
    row = lax.broadcasted_iota(jnp.int32, (rhs, width), 0)
    size = REACH * rhs
    rolled = [moments] + [pltpu.roll(moments, width - i * rhs, 1) for i in range(1, REACH + 1)]
    energy = [rolled[i] - rolled[i + 1] for i in range(REACH)]
    solved = eliminate(jnp.concatenate(energy + [moments], axis=0), size)
    solved = jnp.where(lane < size, solved, 0.0)
    residual = (row == lane).astype(f32) - (solved - pltpu.roll(solved, rhs, 1))
    return solved, residual


def outputs_kernel(odd, moments, split01, split23, inverse, root, iterate, iterate_out, residual_out, coefs):
    rhs = iterate.shape[0]
    rows = split01.shape[1]

    @pl.when((pl.program_id(0) == 0) & (pl.program_id(1) == 0))
    def _():
        solved, residual = mixing(moments[...], rhs)
        both = jnp.concatenate([solved[:, : 4 * rhs], residual[:, : 4 * rhs]], axis=0)
        high = both.astype(bf16).astype(f32)
        stacked = jnp.concatenate([high, both - high], axis=0)
        pair01, pair23 = stacked[:, : 2 * rhs], stacked[:, 2 * rhs :]
        coefs[...] = jnp.concatenate([pair01, pair01, pair23, pair23], axis=1).astype(bf16)

    wide = jnp.concatenate(
        [jnp.concatenate([split01[0, j], split23[0, j]], axis=0) for j in range(rows)], axis=1
    )
    mixed = jnp.dot(coefs[...], wide, preferred_element_type=f32)
    mixed = mixed[: 2 * rhs] + mixed[2 * rhs :]
    nx = split01.shape[-1]
    by_row = jnp.stack([mixed[:, j * nx : (j + 1) * nx] for j in range(rows)], axis=0)
    by_rhs = pltpu.einshape("abc->bac", by_row)
    iterate_out[:, 0] = iterate[:, 0] + by_rhs[:rhs] * inverse[...]
    residual_out[:, 0] = by_rhs[rhs:] * root[...]


def on_device(iterate, residual, labels, boundary):
    rhs, depth, rows, nx = residual.shape
    assert depth == 2 and REACH == 3 and lax.axis_size("gz") % 2 == 0
    half = rhs // 2
    odd = lax.axis_index("gz") % 2 == 1

    def mirrored(block, dim):
        return jnp.where(odd, jnp.flip(block, dim), block)

    cells = jnp.stack([labels, boundary])
    cells = mirrored(cells, 1)
    coef = jnp.exp(cells[0].astype(f32) * (contrast_log / (NCLASS - 1)))
    inner = (1 - cells[1]).astype(f32)
    fields = jnp.stack([coef, inner])
    field_pair = swapped(fields)
    field_beyond = swapped_far(fields)

    own = mirrored(jnp.transpose(residual, (1, 2, 0, 3)), 0)
    before, behind = rows_beside(own[:, :REACH], own[:, -REACH:])
    def with_fields(plane, *cells):
        return jnp.concatenate([plane] + [block.reshape(-1, rhs, nx) for block in cells], axis=0)

    def without_fields(message):
        return message[None, :rows], message[rows:].reshape(-1, rows, nx)

    far3, field_far = without_fields(relayed(with_fields(own[1], coef, inner[1:])))
    near3, field_near = without_fields(relayed(with_fields(own[0], coef, inner[:1]), back=True))
    own = jnp.concatenate([before, own, behind], axis=1)
    sent = after(own, field_pair, field_beyond)[:, 1:-1]
    near2 = swapped(sent[:1])
    last = after(sent[1:], near2)
    near1a = swapped(last[:, :, :half])
    near1b = swapped(last[:, :, half:])
    far1 = relayed(near2)
    far2a = relayed(near1a)
    far2b = relayed(near1b)
    near1 = jnp.concatenate([near1a, near1b], axis=2)

    none = jnp.zeros_like(coef[:1])
    coef = jnp.concatenate(
        [
            field_far[:2], field_beyond[0, 1:], field_beyond[0, :1], coef,
            field_pair[0, 1:], field_pair[0, :1], field_near[:2],
        ],
        axis=0,
    )
    inner = jnp.concatenate(
        [
            none, field_far[2:], field_beyond[1, 1:], field_beyond[1, :1], inner,
            field_pair[1, 1:], field_pair[1, :1], field_near[2:], none,
        ],
        axis=0,
    )
    fields = jnp.stack([coef, inner])
    wide = REACH + 1
    before, behind = rows_beside(fields[:, :, :wide], fields[:, :, -wide:])
    fields = jnp.concatenate([before, fields, behind], axis=2)
    root, inverse, sx, sy, sz = symmetric_operator(fields[0], fields[1])

    extended = rows + 2 * REACH
    vmem = pl.BlockSpec(memory_space=pltpu.VMEM)

    def planes(count):
        return (count, extended, rhs, nx)

    spl = jax.ShapeDtypeStruct((depth, rows, 4 * rhs, nx), bf16)
    sums = jax.ShapeDtypeStruct((rhs, 128), f32)
    u0, u1, u2, split01, moments = pl.pallas_call(
        partial(early_kernel, rows),
        out_shape=tuple(jax.ShapeDtypeStruct(planes(count), f32) for count in (5, 2, 2)) + (spl, sums),
        in_specs=[vmem] * 10,
        out_specs=(vmem,) * 5,
        scratch_shapes=[pltpu.VMEM(planes(count), f32) for count in (3, 2)],
        compiler_params=pltpu.CompilerParams(vmem_limit_bytes=32 * 2**20),
        cost_estimate=pl.CostEstimate(flops=0, bytes_accessed=50 * 2**20, transcendentals=0),
    )(far3, far1, own, near1, near2, near3, inverse, sx, sy, sz)

    moments, split23 = pl.pallas_call(
        partial(late_kernel, rows),
        out_shape=(sums, spl),
        in_specs=[vmem] * 11,
        out_specs=(vmem, vmem),
        scratch_shapes=[pltpu.VMEM(planes(count), f32) for count in (1, 2, 2)],
        compiler_params=pltpu.CompilerParams(vmem_limit_bytes=32 * 2**20),
        cost_estimate=pl.CostEstimate(flops=0, bytes_accessed=50 * 2**20, transcendentals=0),
    )(far2a, far2b, u0, u1, u2, split01, moments, inverse, sx, sy, sz)

    moments = all_sum(moments, ("gy", "gz"))

    inverse = inverse[REACH : REACH + depth, REACH : REACH + rows]
    root = root[REACH : REACH + depth, REACH : REACH + rows]
    tile = 8
    plane_rows = pl.BlockSpec((rhs, 1, tile, nx), lambda z, y, odd: (0, jnp.bitwise_xor(z, odd[0]), y, 0))
    cell_rows = pl.BlockSpec((None, tile, nx), lambda z, y, odd: (z, y, 0))
    return pl.pallas_call(
        outputs_kernel,
        out_shape=(jax.ShapeDtypeStruct(iterate.shape, f32), jax.ShapeDtypeStruct(residual.shape, f32)),
        grid_spec=pltpu.PrefetchScalarGridSpec(
            num_scalar_prefetch=1,
            grid=(depth, rows // tile),
            in_specs=[
                pl.BlockSpec((rhs, 128), lambda z, y, odd: (0, 0)),
                *[pl.BlockSpec((1, tile) + spl.shape[2:], lambda z, y, odd: (z, y, 0, 0))] * 2,
                cell_rows,
                cell_rows,
                plane_rows,
            ],
            out_specs=(plane_rows, plane_rows),
            scratch_shapes=[pltpu.VMEM((4 * rhs, 8 * rhs), bf16)],
        ),
        compiler_params=pltpu.CompilerParams(vmem_limit_bytes=16 * 2**20),
    )(odd.astype(jnp.int32).reshape(1), moments, split01, split23, inverse, root, iterate)


def solution(mesh):
    placed = (
        P(None, ("regions", "gz"), "gy", None),
        P(None, ("regions", "gz"), "gy", None),
        P(("regions", "gz"), "gy", None),
        P(("regions", "gz"), "gy", None),
    )
    return jax.shard_map(
        on_device,
        mesh=mesh,
        in_specs=placed,
        out_specs=(P(None, ("regions", "gz"), "gy", None), P(None, ("regions", "gz"), "gy", None)),
        check_vma=False,
    )
```

```python
import math
from functools import partial

import jax
import jax.numpy as jnp
from jax import lax
from jax.experimental import pallas as pl
from jax.experimental.pallas import tpu as pltpu
from jax.sharding import PartitionSpec as P

NCLASS = 8
ITERS = 3
REACH = ITERS

contrast_log = 4.0 * math.log(10.0)
highest = lax.Precision.HIGHEST
f32 = jnp.float32
bf16 = jnp.bfloat16


def moved(block, axis, pairs):
    return lax.ppermute(block, axis, pairs)


def shifted(block, axis, step):
    count = lax.axis_size(axis)
    return moved(block, axis, [(i, i + step) for i in range(count) if 0 <= i + step < count])


def swapped(block):
    return moved(block, "gz", [(i, i ^ 1) for i in range(lax.axis_size("gz"))])


def relayed(block, back=False):
    count = lax.axis_size("gz")
    steps = [(i, i + 2 - 4 * (i % 2)) for i in range(count)]
    pairs = [(i, j) for i, j in steps if 0 <= j < count]
    return moved(block, "gz", [(j, i) for i, j in pairs] if back else pairs)


def rows_beside(before, after):
    count = lax.axis_size("gy")
    if count != 2:
        return shifted(after, "gy", 1), shifted(before, "gy", -1)
    second = lax.axis_index("gy") == 1
    other = moved(jnp.where(second, before, after), "gy", [(0, 1), (1, 0)])
    zero = jnp.zeros_like(other)
    return jnp.where(second, other, zero), jnp.where(second, zero, other)


def all_sum(values, axes):
    for axis in axes:
        count = lax.axis_size(axis)
        if count & (count - 1):
            values = lax.psum(values, axis)
            continue
        step = 1
        while step < count:
            values = values + lax.ppermute(values, axis, [(i, i ^ step) for i in range(count)])
            step *= 2
    return values


def face_of(center, beside):
    return jnp.where(beside > 0.0, 2.0 * center * beside / (center + beside), center)


def symmetric_operator(coef, inner):
    def pad_x(a, forward):
        return jnp.pad(a[..., 1:], ((0, 0), (0, 0), (0, 1))) if forward else jnp.pad(a[..., :-1], ((0, 0), (0, 0), (1, 0)))

    center = coef[1:-1, 1:-1]
    here = inner[1:-1, 1:-1]
    total = jnp.zeros_like(center)
    for beside in (
        coef[2:, 1:-1], coef[:-2, 1:-1], coef[1:-1, 2:], coef[1:-1, :-2], pad_x(center, True), pad_x(center, False)
    ):
        total = total + face_of(center, beside)
    diagonal = here * total + (1.0 - here)
    root = jnp.sqrt(diagonal)
    inverse = 1.0 / root
    masked = here * inverse

    def coupling(a, b, ma, mb):
        return ma * face_of(a, b) * mb

    along_x = coupling(center, pad_x(center, True), masked, pad_x(masked, True))
    along_y = coupling(center[:, :-1], center[:, 1:], masked[:, :-1], masked[:, 1:])
    along_z = coupling(center[:-1], center[1:], masked[:-1], masked[1:])
    return root, inverse, along_x, along_y, along_z


def row_blocks(start, stop, body, size=8):
    blocks = -(-(stop - start) // size)

    def step(block, carry):
        body(jnp.minimum(start + block * size, stop - size))
        return carry

    lax.fori_loop(0, blocks, step, 0)


def apply_rows(operator, plane, start, before, here, after, size=8):
    sx, sy, sz = operator
    ref, index = here
    out = []
    last, center = ref[index, start - 1], ref[index, start]
    below = sy[plane, pl.ds(start - 1, 1), :]
    width = center.shape[-1]
    for j in range(size):
        y = start + j
        following = ref[index, y + 1]
        above = sy[plane, pl.ds(y, 1), :]
        ahead = sx[plane, pl.ds(y, 1), :]
        total = ahead * pltpu.roll(center, width - 1, 1) + pltpu.roll(ahead * center, 1, 1)
        total += above * following + below * last
        total += sz[plane, pl.ds(y, 1), :] * after[0][after[1], y]
        total += sz[plane - 1, pl.ds(y, 1), :] * before[0][before[1], y]
        out.append(total)
        last, center, below = center, following, above
    return out


def spread(plane, depth=2):
    return max(REACH - plane, plane - (REACH + depth - 1), 0)


def scale_rows(plane, source, first, dst, start, count, inverse, part=slice(None)):
    out, place = dst

    def body(j, size=8):
        for i in range(size):
            out[place, start + j + i, part] = source[first + j + i] * inverse[plane, pl.ds(start + j + i, 1), :]

    if count < 8:
        body(0, count)
    else:
        row_blocks(0, count, body)


def apply_plane(rows, power, plane, operator, fields):
    reach = REACH - power - spread(plane)
    src = [fields[power - 1, plane + offset] for offset in (-1, 0, 1)]
    out, place = fields[power, plane]

    def body(y):
        for j, values in enumerate(apply_rows(operator, plane, y, *src)):
            out[place, y + j] = values

    row_blocks(REACH - reach, REACH + rows + reach, body)


LATE = 1
BESIDE = ((5, 0, 2), (6, 2, 1), (2, 3, 2))


def halves(blocks):
    stack = jnp.concatenate(blocks, axis=0)
    high = stack.astype(bf16)
    low = (stack - high.astype(f32)).astype(bf16)
    return jnp.concatenate([high, low], axis=0)


def inner_products(left, right):
    return lax.dot_general(left, right, (((1,), (1,)), ((), ())), preferred_element_type=f32)


def whole(gram, left, right):
    gram = gram[:left] + gram[left : 2 * left]
    return gram[:, :right] + gram[:, right : 2 * right]


def early_kernel(
    rows, far3, far1, own, own_before, own_behind, near1a, near1b, near2, near3, before, behind,
    inverse, sx, sy, sz, u0_out, u1_out, u2_out, split, moments, u0, u1,
):
    operator = (sx, sy, sz)
    fields = {(0, plane): (u0_out, index) for index, plane in enumerate((0, 2, 3))}
    fields.update({(0, plane): (u0, plane - 4) for plane in range(4, 8)})
    fields.update({(1, 3): (u1_out, 0), (1, 4): (u1_out, 1), (1, 5): (u1, 0), (1, 6): (u1, 1)})
    fields.update({(2, 4): (u2_out, 0), (2, 5): (u2_out, 1)})
    first, last = REACH, REACH + rows
    half = near1a.shape[1]
    for plane, source in ((0, far3), (2, far1), (3, own.at[0]), (4, own.at[1]), (6, near2), (7, near3)):
        scale_rows(plane, source, 0, fields[0, plane], first, rows, inverse)
    scale_rows(5, near1a, 0, fields[0, 5], first, rows, inverse, slice(0, half))
    scale_rows(5, near1b, 0, fields[0, 5], first, rows, inverse, slice(half, None))
    for plane in (3, 4):
        scale_rows(plane, own_before.at[plane - 3], 0, fields[0, plane], 0, REACH, inverse)
        scale_rows(plane, own_behind.at[plane - 3], 0, fields[0, plane], last, REACH, inverse)
    for plane, place, count in BESIDE:
        scale_rows(plane, before, place, fields[0, plane], first - count, count, inverse)
        scale_rows(plane, behind, place, fields[0, plane], last, count, inverse)
    for power, plane in ((1, 3), (1, 4), (1, 5), (1, 6), (2, 4), (2, 5)):
        apply_plane(rows, power, plane, operator, fields)

    rhs = u0.shape[2]
    gram = jnp.zeros((4 * rhs, 4 * rhs), f32)
    for plane in range(2):

        def gram_rows(block, total, plane=plane):
            parts = []
            for j in range(8):
                y = block * 8 + j
                sources = [fields[power, plane + REACH] for power in range(2)]
                both = halves([ref[index, y + REACH] for ref, index in sources])
                split[plane, y] = both
                parts.append(both)
            wide = jnp.concatenate(parts, axis=1)
            return total + inner_products(wide, wide)

        gram = lax.fori_loop(0, rows // 8, gram_rows, gram)
    gram = whole(gram, 2 * rhs, 2 * rhs)
    moments[:, : 2 * rhs] = gram[:rhs]
    moments[:, 2 * rhs : 3 * rhs] = gram[rhs:, rhs:]


def late_kernel(
    rows, far2a, far2b, u0_in, u1_in, u2_in, moments_in, inverse, sx, sy, sz, moments, split, u0, u1, u2
):
    operator = (sx, sy, sz)
    fields = {(0, plane): (u0_in, index) for index, plane in enumerate((0, 2, 3))}
    fields[0, LATE] = (u0, 0)
    fields.update({(1, 1): (u1, 0), (1, 2): (u1, 1), (1, 3): (u1_in, 0), (1, 4): (u1_in, 1)})
    fields.update({(2, 2): (u2, 0), (2, 3): (u2, 1), (2, 4): (u2_in, 0), (2, 5): (u2_in, 1)})
    first, last = REACH, REACH + rows
    half = far2a.shape[1]
    for source, part in ((far2a, slice(0, half)), (far2b, slice(half, None))):
        scale_rows(LATE, source, 0, fields[0, LATE], first, rows, inverse, part)
    for place, y in ((rows, first - 1), (rows + 2, last)):
        for index, part in enumerate((slice(0, half), slice(half, None))):
            scale_rows(LATE, far2b, place + index, fields[0, LATE], y, 1, inverse, part)
    for power, plane in ((1, 1), (1, 2), (2, 2), (2, 3)):
        apply_plane(rows, power, plane, operator, fields)

    rhs = u0.shape[2]
    gram = jnp.zeros((6 * rhs, 2 * rhs), f32)
    for plane in range(2):
        level = plane + REACH

        def gram_rows(block, total, plane=plane, level=level):
            start = block * 8
            y = start + REACH
            last = apply_rows(operator, level, y, *[fields[2, level + offset] for offset in (-1, 0, 1)])
            left, right = [], []
            for j in range(8):
                ref, index = fields[2, level]
                both = halves([ref[index, y + j], last[j]])
                split[plane, start + j] = both
                left.append(jnp.concatenate([halves([u1_in[plane, y + j]]), both], axis=0))
                right.append(jnp.concatenate([both[:rhs], both[2 * rhs : 3 * rhs]], axis=0))
            return total + inner_products(jnp.concatenate(left, axis=1), jnp.concatenate(right, axis=1))

        gram = lax.fori_loop(0, rows // 8, gram_rows, gram)
    gram = gram[:, :rhs] + gram[:, rhs:]
    blocks = [gram[part * rhs : (part + 1) * rhs] for part in range(6)]
    moments[:, : 3 * rhs] = moments_in[:, : 3 * rhs]
    moments[:, 3 * rhs : 4 * rhs] = blocks[0] + blocks[1]
    moments[:, 4 * rhs : 5 * rhs] = blocks[2] + blocks[4]
    moments[:, 5 * rhs : 6 * rhs] = blocks[3] + blocks[5]
    moments[:, 6 * rhs :] = jnp.zeros((rhs, moments.shape[1] - 6 * rhs), f32)


def eliminate(stacked, size):
    tiles, height, width = stacked.shape
    lane = lax.broadcasted_iota(jnp.int32, (height, width), 1)

    def everywhere(row):
        return jnp.broadcast_to(row, (height, width))

    for k in range(0, size, 2):
        if k and k % height == 0:
            stacked = stacked[1:]
        at = k % height
        row0, row1 = everywhere(stacked[0, at : at + 1]), everywhere(stacked[0, at + 1 : at + 2])
        col0 = jnp.broadcast_to(stacked[:, :, k : k + 1], stacked.shape)
        col1 = jnp.broadcast_to(stacked[:, :, k + 1 : k + 2], stacked.shape)
        a, c = everywhere(col0[0, at : at + 1]), everywhere(col0[0, at + 1 : at + 2])
        b, d = everywhere(col1[0, at : at + 1]), everywhere(col1[0, at + 1 : at + 2])
        scale = 1.0 / (a * d - b * c)
        first, second = lane == k, lane == k + 1
        mix0 = scale * jnp.where(first, -d, jnp.where(second, b, d * row0 - b * row1))
        mix1 = scale * jnp.where(first, c, jnp.where(second, -a, a * row1 - c * row0))
        rest = jnp.where((first | second)[None], 0.0, stacked)
        stacked = rest - col0 * mix0[None] - col1 * mix1[None]
    return stacked[1:]


def mixing(moments, rhs):
    width = moments.shape[1]
    lane = lax.broadcasted_iota(jnp.int32, (rhs, width), 1)
    row = lax.broadcasted_iota(jnp.int32, (rhs, width), 0)
    size = REACH * rhs
    rolled = [moments] + [pltpu.roll(moments, width - i * rhs, 1) for i in range(1, REACH + 1)]
    energy = [rolled[i] - rolled[i + 1] for i in range(REACH)]
    tiles = jnp.concatenate(energy + [moments], axis=0).reshape(-1, 8, width)
    solved = eliminate(tiles, size).reshape(rhs, width)
    solved = jnp.where(lane < size, solved, 0.0)
    residual = (row == lane).astype(f32) - (solved - pltpu.roll(solved, rhs, 1))
    return solved, residual


def outputs_kernel(odd, moments, split01, split23, inverse, root, iterate, iterate_out, residual_out, coefs):
    rhs = iterate.shape[0]
    rows = split01.shape[1]

    @pl.when((pl.program_id(0) == 0) & (pl.program_id(1) == 0))
    def _():
        solved, residual = mixing(moments[...], rhs)
        both = jnp.concatenate([solved[:, : 4 * rhs], residual[:, : 4 * rhs]], axis=0)
        high = both.astype(bf16).astype(f32)
        stacked = jnp.concatenate([high, both - high], axis=0)
        pair01, pair23 = stacked[:, : 2 * rhs], stacked[:, 2 * rhs :]
        coefs[...] = jnp.concatenate([pair01, pair01, pair23, pair23], axis=1).astype(bf16)

    wide = jnp.concatenate(
        [jnp.concatenate([split01[0, j], split23[0, j]], axis=0) for j in range(rows)], axis=1
    )
    mixed = jnp.dot(coefs[...], wide, preferred_element_type=f32)
    mixed = mixed[: 2 * rhs] + mixed[2 * rhs :]
    nx = split01.shape[-1]
    by_row = jnp.stack([mixed[:, j * nx : (j + 1) * nx] for j in range(rows)], axis=0)
    by_rhs = pltpu.einshape("abc->bac", by_row)
    iterate_out[:, 0] = iterate[:, 0] + by_rhs[:rhs] * inverse[...]
    residual_out[:, 0] = by_rhs[rhs:] * root[...]


def on_device(iterate, residual, labels, boundary):
    rhs, depth, rows, nx = residual.shape
    assert depth == 2 and REACH == 3 and lax.axis_size("gz") % 2 == 0
    half = rhs // 2
    odd = lax.axis_index("gz") % 2 == 1

    def mirrored(block, dim):
        return jnp.where(odd, jnp.flip(block, dim), block)

    cells = jnp.stack([labels, boundary])
    cells = mirrored(cells, 1)
    coef = jnp.exp(cells[0].astype(f32) * (contrast_log / (NCLASS - 1)))
    inner = (1 - cells[1]).astype(f32)
    fields = jnp.stack([coef, inner])
    own = mirrored(jnp.transpose(residual, (1, 2, 0, 3)), 0)

    def with_cells(plane, *cells):
        return jnp.concatenate([plane] + [block.reshape(-1, rhs, nx) for block in cells], axis=0)

    def cells_of(message):
        return message[rows:].reshape(-1, rows, nx)

    near2 = swapped(with_cells(own[0], fields))
    far3 = relayed(with_cells(own[1], coef, inner[1:]))
    near3 = relayed(with_cells(own[0], coef, inner[:1]), back=True)
    own_before, own_behind = rows_beside(own[:, :REACH], own[:, -REACH:])
    near1a = swapped(own[1, :, :half])
    edges = [own_before[1, -1:], own_behind[1, :1]]
    near1b = swapped(jnp.concatenate([own[1, :, half:]] + [edge.reshape(2, half, nx) for edge in edges], axis=0))
    far1 = relayed(near2)
    far2a = relayed(near1a)
    far2b = relayed(near1b)

    field_pair = cells_of(near2).reshape(2, depth, rows, nx)
    field_beyond = cells_of(far1).reshape(2, depth, rows, nx)
    field_far, field_near = cells_of(far3), cells_of(near3)
    none = jnp.zeros_like(coef[:1])
    coef = jnp.concatenate(
        [
            field_far[:2], field_beyond[0, 1:], field_beyond[0, :1], coef,
            field_pair[0, 1:], field_pair[0, :1], field_near[:2],
        ],
        axis=0,
    )
    inner = jnp.concatenate(
        [
            none, field_far[2:], field_beyond[1, 1:], field_beyond[1, :1], inner,
            field_pair[1, 1:], field_pair[1, :1], field_near[2:], none,
        ],
        axis=0,
    )
    fields = jnp.stack([coef, inner])
    wide = REACH + 1

    def edges_of(last):
        def cut(block, count, axis=0):
            low, high = (rows - count, rows) if last else (0, count)
            return lax.slice_in_dim(block, low, high, axis=axis)

        pair = jnp.concatenate([cut(near1a, 2), cut(near1b, 2)], axis=1)
        planes = jnp.concatenate([pair, cut(near2, 1), cut(far1, 2)], axis=0)
        return jnp.concatenate([planes.reshape(-1, nx), cut(fields, wide, 2).reshape(-1, nx)], axis=0)

    sides = rows_beside(edges_of(False), edges_of(True))
    count = sum(number for _, _, number in BESIDE) * rhs
    before, behind = [side[:count].reshape(-1, rhs, nx) for side in sides]
    fields_beside = [side[count:].reshape(2, -1, wide, nx) for side in sides]
    fields = jnp.concatenate([fields_beside[0], fields, fields_beside[1]], axis=2)
    root, inverse, sx, sy, sz = symmetric_operator(fields[0], fields[1])

    extended = rows + 2 * REACH
    vmem = pl.BlockSpec(memory_space=pltpu.VMEM)

    def planes(count):
        return (count, extended, rhs, nx)

    spl = jax.ShapeDtypeStruct((depth, rows, 4 * rhs, nx), bf16)
    sums = jax.ShapeDtypeStruct((rhs, 128), f32)
    u0, u1, u2, split01, moments = pl.pallas_call(
        partial(early_kernel, rows),
        out_shape=tuple(jax.ShapeDtypeStruct(planes(count), f32) for count in (3, 2, 2)) + (spl, sums),
        in_specs=[vmem] * 15,
        out_specs=(vmem,) * 5,
        scratch_shapes=[pltpu.VMEM(planes(count), f32) for count in (4, 2)],
        compiler_params=pltpu.CompilerParams(vmem_limit_bytes=32 * 2**20),
        cost_estimate=pl.CostEstimate(flops=0, bytes_accessed=50 * 2**20, transcendentals=0),
    )(
        far3, far1, own, own_before, own_behind, near1a, near1b, near2, near3, before, behind, inverse, sx, sy, sz
    )

    moments, split23 = pl.pallas_call(
        partial(late_kernel, rows),
        out_shape=(sums, spl),
        in_specs=[vmem] * 10,
        out_specs=(vmem, vmem),
        scratch_shapes=[pltpu.VMEM(planes(count), f32) for count in (1, 2, 2)],
        compiler_params=pltpu.CompilerParams(vmem_limit_bytes=32 * 2**20),
        cost_estimate=pl.CostEstimate(flops=0, bytes_accessed=50 * 2**20, transcendentals=0),
    )(far2a, far2b, u0, u1, u2, moments, inverse, sx, sy, sz)

    moments = all_sum(moments, ("gy", "gz"))

    inverse = inverse[REACH : REACH + depth, REACH : REACH + rows]
    root = root[REACH : REACH + depth, REACH : REACH + rows]
    tile = 8
    plane_rows = pl.BlockSpec((rhs, 1, tile, nx), lambda z, y, odd: (0, jnp.bitwise_xor(z, odd[0]), y, 0))
    cell_rows = pl.BlockSpec((None, tile, nx), lambda z, y, odd: (z, y, 0))
    return pl.pallas_call(
        outputs_kernel,
        out_shape=(jax.ShapeDtypeStruct(iterate.shape, f32), jax.ShapeDtypeStruct(residual.shape, f32)),
        grid_spec=pltpu.PrefetchScalarGridSpec(
            num_scalar_prefetch=1,
            grid=(depth, rows // tile),
            in_specs=[
                pl.BlockSpec((rhs, 128), lambda z, y, odd: (0, 0)),
                *[pl.BlockSpec((1, tile) + spl.shape[2:], lambda z, y, odd: (z, y, 0, 0))] * 2,
                cell_rows,
                cell_rows,
                plane_rows,
            ],
            out_specs=(plane_rows, plane_rows),
            scratch_shapes=[pltpu.VMEM((4 * rhs, 8 * rhs), bf16)],
        ),
        compiler_params=pltpu.CompilerParams(vmem_limit_bytes=16 * 2**20),
    )(odd.astype(jnp.int32).reshape(1), moments, split01, split23, inverse, root, iterate)


def solution(mesh):
    placed = (
        P(None, ("regions", "gz"), "gy", None),
        P(None, ("regions", "gz"), "gy", None),
        P(("regions", "gz"), "gy", None),
        P(("regions", "gz"), "gy", None),
    )
    return jax.shard_map(
        on_device,
        mesh=mesh,
        in_specs=placed,
        out_specs=(P(None, ("regions", "gz"), "gy", None), P(None, ("regions", "gz"), "gy", None)),
        check_vma=False,
    )
```

```python
import math
from functools import partial

import jax
import jax.numpy as jnp
from jax import lax
from jax.experimental import pallas as pl
from jax.experimental.pallas import tpu as pltpu
from jax.sharding import PartitionSpec as P

NCLASS = 8
ITERS = 3
REACH = ITERS

contrast_log = 4.0 * math.log(10.0)
highest = lax.Precision.HIGHEST
f32 = jnp.float32
bf16 = jnp.bfloat16


def moved(block, axis, pairs):
    return lax.ppermute(block, axis, pairs)


def shifted(block, axis, step):
    count = lax.axis_size(axis)
    return moved(block, axis, [(i, i + step) for i in range(count) if 0 <= i + step < count])


def swapped(block):
    return moved(block, "gz", [(i, i ^ 1) for i in range(lax.axis_size("gz"))])


def relayed(block, back=False):
    count = lax.axis_size("gz")
    steps = [(i, i + 2 - 4 * (i % 2)) for i in range(count)]
    pairs = [(i, j) for i, j in steps if 0 <= j < count]
    return moved(block, "gz", [(j, i) for i, j in pairs] if back else pairs)


def rows_beside(before, after):
    count = lax.axis_size("gy")
    if count != 2:
        return shifted(after, "gy", 1), shifted(before, "gy", -1)
    second = lax.axis_index("gy") == 1
    other = moved(jnp.where(second, before, after), "gy", [(0, 1), (1, 0)])
    zero = jnp.zeros_like(other)
    return jnp.where(second, other, zero), jnp.where(second, zero, other)


def all_sum(values, axes):
    for axis in axes:
        count = lax.axis_size(axis)
        if count & (count - 1):
            values = lax.psum(values, axis)
            continue
        step = 1
        while step < count:
            values = values + lax.ppermute(values, axis, [(i, i ^ step) for i in range(count)])
            step *= 2
    return values


def face_of(center, beside):
    return jnp.where(beside > 0.0, 2.0 * center * beside / (center + beside), center)


LATE = 1
BESIDE = ((5, 0, 2), (6, 2, 1), (2, 3, 2))
EDGES = 5
FIELDS = (
    ("far3", 0, None), ("far3", 1, 2), ("far1", 1, 3), ("far1", 0, 2), ("mine", 0, 2),
    ("mine", 1, 3), ("near2", 1, 3), ("near2", 0, 2), ("near3", 0, 2), ("near3", 1, None),
)
MARGIN = 8


def prepare_kernel(odd, residual, labels, boundary, mine, ahead):
    rhs, depth, rows, nx = residual.shape
    for place, out in ((0, mine), (1, ahead)):
        plane = jnp.bitwise_xor(place, odd[0])

        def turn(block, carry, plane=plane, out=out):
            rows_here = pl.ds(block * 8, 8)
            out[rows_here] = pltpu.einshape("abc->bac", residual[:, plane, rows_here, :])
            return carry

        lax.fori_loop(0, rows // 8, turn, 0)
        for part in range(rows // rhs):
            cells = pl.ds(part * rhs, rhs)
            coef = jnp.exp(labels[plane, cells, :].astype(f32) * (contrast_log / (NCLASS - 1)))
            inner = (1 - boundary[plane, cells, :]).astype(f32)
            count = rows // rhs
            for message in (mine, ahead):
                message[rows + place * count + part] = coef
            mine[rows + (2 + place) * count + part] = inner
            if place == 1:
                ahead[rows + 2 * count + part] = inner


def edges_kernel(rows, near1, near2, far1, far3, near3, mine, first, last):
    messages = {"near2": near2, "far1": far1, "far3": far3, "near3": near3, "mine": mine}
    rhs = mine.shape[1]
    count = rows // rhs
    for (_, place, number), source in zip(BESIDE, (near1, near2, far1)):
        first[place : place + number] = source[:number]
        last[place : place + number] = source[rows - number : rows]
    place = EDGES
    for name, *parts in FIELDS:
        for part in parts:
            if part is not None:
                start = rows + part * count
                first[place] = messages[name][start]
                last[place] = messages[name][start + count - 1]
                place += 1


def fill_cells(rows, messages, before, behind, coef, inner):
    place = EDGES
    for plane, (name, *parts) in enumerate(FIELDS):
        for part, out in zip(parts, (coef, inner)):
            if part is None:
                continue
            rhs = messages[name].shape[1]
            count = rows // rhs
            for block in range(count):
                out[plane, MARGIN + block * rhs : MARGIN + (block + 1) * rhs] = messages[name][
                    rows + part * count + block
                ]
            out[plane, :MARGIN] = before[place, rhs - MARGIN :]
            out[plane, MARGIN + rows :] = behind[place, :MARGIN]
            place += 1


def make_operator(coef, inner, inverse, sx, sy, sz, root, masked):
    planes, height, nx = inverse.shape
    lane = lax.broadcasted_iota(jnp.int32, (height, nx), 1)
    inside = lane < nx - 1

    def one_plane(plane, carry):
        here = coef[plane + 1]
        flag = inner[plane + 1]
        right = jnp.where(inside, pltpu.roll(here, nx - 1, 1), 0.0)
        left = jnp.where(lane > 0, pltpu.roll(here, 1, 1), 0.0)
        behind, before = pltpu.roll(here, height - 1, 0), pltpu.roll(here, 1, 0)
        along_x, along_y = face_of(here, right), face_of(here, behind)
        along_z = face_of(here, coef[plane + 2])
        total = along_x + jnp.where(left > 0.0, pltpu.roll(along_x, 1, 1), here)
        total += along_y + jnp.where(before > 0.0, pltpu.roll(along_y, 1, 0), here)
        total += along_z + face_of(here, coef[plane])
        diagonal = flag * total + (1.0 - flag)
        square = jnp.sqrt(diagonal)
        reciprocal = 1.0 / square
        root[plane] = square
        inverse[plane] = reciprocal
        scale = flag * reciprocal
        masked[plane] = scale
        sx[plane] = jnp.where(inside, scale * along_x * pltpu.roll(scale, nx - 1, 1), 0.0)
        sy[plane] = scale * along_y * pltpu.roll(scale, height - 1, 0)
        sz[plane] = scale * along_z
        return carry

    lax.fori_loop(0, planes, one_plane, 0)

    def next_plane(plane, carry):
        sz[plane] = sz[plane] * masked[plane + 1]
        return carry

    lax.fori_loop(0, planes - 1, next_plane, 0)


def cell_row(ref, plane, y):
    return ref[plane, pl.ds(y + (MARGIN - REACH), 1), :]


def row_blocks(start, stop, body, size=8):
    blocks = -(-(stop - start) // size)

    def step(block, carry):
        body(jnp.minimum(start + block * size, stop - size))
        return carry

    lax.fori_loop(0, blocks, step, 0)


def apply_rows(operator, plane, start, before, here, after, size=8):
    sx, sy, sz = operator
    ref, index = here
    out = []
    last, center = ref[index, start - 1], ref[index, start]
    below = cell_row(sy, plane, start - 1)
    width = center.shape[-1]
    for j in range(size):
        y = start + j
        following = ref[index, y + 1]
        above = cell_row(sy, plane, y)
        ahead = cell_row(sx, plane, y)
        total = ahead * pltpu.roll(center, width - 1, 1) + pltpu.roll(ahead * center, 1, 1)
        total += above * following + below * last
        total += cell_row(sz, plane, y) * after[0][after[1], y]
        total += cell_row(sz, plane - 1, y) * before[0][before[1], y]
        out.append(total)
        last, center, below = center, following, above
    return out


def spread(plane, depth=2):
    return max(REACH - plane, plane - (REACH + depth - 1), 0)


def scale_rows(plane, source, first, dst, start, count, inverse):
    out, place = dst

    def body(j, size=8):
        for i in range(size):
            out[place, start + j + i] = source[first + j + i] * cell_row(inverse, plane, start + j + i)

    if count < 8:
        body(0, count)
    else:
        row_blocks(0, count, body)


def apply_plane(rows, power, plane, operator, fields):
    reach = REACH - power - spread(plane)
    src = [fields[power - 1, plane + offset] for offset in (-1, 0, 1)]
    out, place = fields[power, plane]

    def body(y):
        for j, values in enumerate(apply_rows(operator, plane, y, *src)):
            out[place, y + j] = values

    row_blocks(REACH - reach, REACH + rows + reach, body)


def halves(blocks):
    stack = jnp.concatenate(blocks, axis=0)
    high = stack.astype(bf16)
    low = (stack - high.astype(f32)).astype(bf16)
    return jnp.concatenate([high, low], axis=0)


def inner_products(left, right):
    return lax.dot_general(left, right, (((1,), (1,)), ((), ())), preferred_element_type=f32)


def whole(gram, left, right):
    gram = gram[:left] + gram[left : 2 * left]
    return gram[:, :right] + gram[:, right : 2 * right]


def early_kernel(
    rows, far3, far1, mine, ahead, own_before, own_behind, near1, near2, near3, before, behind,
    inverse, sx, sy, sz, root, u0_out, u1_out, u2_out, split, moments, u0, u1, coef, inner, masked,
):
    messages = {"near2": near2, "far1": far1, "far3": far3, "near3": near3, "mine": mine}
    fill_cells(rows, messages, before, behind, coef, inner)
    make_operator(coef, inner, inverse, sx, sy, sz, root, masked)
    operator = (sx, sy, sz)
    fields = {(0, plane): (u0_out, index) for index, plane in enumerate((0, 2, 3))}
    fields.update({(0, plane): (u0, plane - 4) for plane in range(4, 8)})
    fields.update({(1, 3): (u1_out, 0), (1, 4): (u1_out, 1), (1, 5): (u1, 0), (1, 6): (u1, 1)})
    fields.update({(2, 4): (u2_out, 0), (2, 5): (u2_out, 1)})
    first, last = REACH, REACH + rows
    for plane, source in ((0, far3), (2, far1), (3, mine), (4, ahead), (5, near1), (6, near2), (7, near3)):
        scale_rows(plane, source, 0, fields[0, plane], first, rows, inverse)
    for plane in (3, 4):
        scale_rows(plane, own_before.at[plane - 3], 0, fields[0, plane], 0, REACH, inverse)
        scale_rows(plane, own_behind.at[plane - 3], 0, fields[0, plane], last, REACH, inverse)
    for plane, place, count in BESIDE:
        scale_rows(plane, before, place, fields[0, plane], first - count, count, inverse)
        scale_rows(plane, behind, place, fields[0, plane], last, count, inverse)
    for power, plane in ((1, 3), (1, 4), (1, 5), (1, 6), (2, 4), (2, 5)):
        apply_plane(rows, power, plane, operator, fields)

    rhs = u0.shape[2]
    gram = jnp.zeros((4 * rhs, 4 * rhs), f32)
    for plane in range(2):

        def gram_rows(block, total, plane=plane):
            parts = []
            for j in range(8):
                y = block * 8 + j
                sources = [fields[power, plane + REACH] for power in range(2)]
                both = halves([ref[index, y + REACH] for ref, index in sources])
                split[plane, y] = both
                parts.append(both)
            wide = jnp.concatenate(parts, axis=1)
            return total + inner_products(wide, wide)

        gram = lax.fori_loop(0, rows // 8, gram_rows, gram)
    gram = whole(gram, 2 * rhs, 2 * rhs)
    moments[:, : 2 * rhs] = gram[:rhs]
    moments[:, 2 * rhs : 3 * rhs] = gram[rhs:, rhs:]


def late_kernel(
    rows, far2, u0_in, u1_in, u2_in, moments_in, inverse, sx, sy, sz, moments, split, u0, u1, u2
):
    operator = (sx, sy, sz)
    fields = {(0, plane): (u0_in, index) for index, plane in enumerate((0, 2, 3))}
    fields[0, LATE] = (u0, 0)
    fields.update({(1, 1): (u1, 0), (1, 2): (u1, 1), (1, 3): (u1_in, 0), (1, 4): (u1_in, 1)})
    fields.update({(2, 2): (u2, 0), (2, 3): (u2, 1), (2, 4): (u2_in, 0), (2, 5): (u2_in, 1)})
    first, last = REACH, REACH + rows
    for place, start, count in ((0, first, rows), (rows, first - 1, 1), (rows + 1, last, 1)):
        scale_rows(LATE, far2, place, fields[0, LATE], start, count, inverse)
    for power, plane in ((1, 1), (1, 2), (2, 2), (2, 3)):
        apply_plane(rows, power, plane, operator, fields)

    rhs = u0.shape[2]
    gram = jnp.zeros((6 * rhs, 2 * rhs), f32)
    for plane in range(2):
        level = plane + REACH

        def gram_rows(block, total, plane=plane, level=level):
            start = block * 8
            y = start + REACH
            last = apply_rows(operator, level, y, *[fields[2, level + offset] for offset in (-1, 0, 1)])
            left, right = [], []
            for j in range(8):
                ref, index = fields[2, level]
                both = halves([ref[index, y + j], last[j]])
                split[plane, start + j] = both
                left.append(jnp.concatenate([halves([u1_in[plane, y + j]]), both], axis=0))
                right.append(jnp.concatenate([both[:rhs], both[2 * rhs : 3 * rhs]], axis=0))
            return total + inner_products(jnp.concatenate(left, axis=1), jnp.concatenate(right, axis=1))

        gram = lax.fori_loop(0, rows // 8, gram_rows, gram)
    gram = gram[:, :rhs] + gram[:, rhs:]
    blocks = [gram[part * rhs : (part + 1) * rhs] for part in range(6)]
    moments[:, : 3 * rhs] = moments_in[:, : 3 * rhs]
    moments[:, 3 * rhs : 4 * rhs] = blocks[0] + blocks[1]
    moments[:, 4 * rhs : 5 * rhs] = blocks[2] + blocks[4]
    moments[:, 5 * rhs : 6 * rhs] = blocks[3] + blocks[5]
    moments[:, 6 * rhs :] = jnp.zeros((rhs, moments.shape[1] - 6 * rhs), f32)


def eliminate(stacked, size):
    tiles, height, width = stacked.shape
    lane = lax.broadcasted_iota(jnp.int32, (height, width), 1)

    def everywhere(row):
        return jnp.broadcast_to(row, (height, width))

    for k in range(0, size, 2):
        if k and k % height == 0:
            stacked = stacked[1:]
        at = k % height
        row0, row1 = everywhere(stacked[0, at : at + 1]), everywhere(stacked[0, at + 1 : at + 2])
        col0 = jnp.broadcast_to(stacked[:, :, k : k + 1], stacked.shape)
        col1 = jnp.broadcast_to(stacked[:, :, k + 1 : k + 2], stacked.shape)
        a, c = everywhere(col0[0, at : at + 1]), everywhere(col0[0, at + 1 : at + 2])
        b, d = everywhere(col1[0, at : at + 1]), everywhere(col1[0, at + 1 : at + 2])
        scale = 1.0 / (a * d - b * c)
        first, second = lane == k, lane == k + 1
        mix0 = scale * jnp.where(first, -d, jnp.where(second, b, d * row0 - b * row1))
        mix1 = scale * jnp.where(first, c, jnp.where(second, -a, a * row1 - c * row0))
        rest = jnp.where((first | second)[None], 0.0, stacked)
        stacked = rest - col0 * mix0[None] - col1 * mix1[None]
    return stacked[1:]


def mixing(moments, rhs):
    width = moments.shape[1]
    lane = lax.broadcasted_iota(jnp.int32, (rhs, width), 1)
    row = lax.broadcasted_iota(jnp.int32, (rhs, width), 0)
    size = REACH * rhs
    rolled = [moments] + [pltpu.roll(moments, width - i * rhs, 1) for i in range(1, REACH + 1)]
    energy = [rolled[i] - rolled[i + 1] for i in range(REACH)]
    tiles = jnp.concatenate(energy + [moments], axis=0).reshape(-1, 8, width)
    solved = eliminate(tiles, size).reshape(rhs, width)
    solved = jnp.where(lane < size, solved, 0.0)
    residual = (row == lane).astype(f32) - (solved - pltpu.roll(solved, rhs, 1))
    return solved, residual


def outputs_kernel(odd, moments, split01, split23, inverse, root, iterate, iterate_out, residual_out, coefs):
    rhs = iterate.shape[0]
    rows = split01.shape[1]

    @pl.when((pl.program_id(0) == 0) & (pl.program_id(1) == 0))
    def _():
        solved, residual = mixing(moments[...], rhs)
        both = jnp.concatenate([solved[:, : 4 * rhs], residual[:, : 4 * rhs]], axis=0)
        high = both.astype(bf16).astype(f32)
        stacked = jnp.concatenate([high, both - high], axis=0)
        pair01, pair23 = stacked[:, : 2 * rhs], stacked[:, 2 * rhs :]
        coefs[...] = jnp.concatenate([pair01, pair01, pair23, pair23], axis=1).astype(bf16)

    wide = jnp.concatenate(
        [jnp.concatenate([split01[0, j], split23[0, j]], axis=0) for j in range(rows)], axis=1
    )
    mixed = jnp.dot(coefs[...], wide, preferred_element_type=f32)
    mixed = mixed[: 2 * rhs] + mixed[2 * rhs :]
    nx = split01.shape[-1]
    by_row = jnp.stack([mixed[:, j * nx : (j + 1) * nx] for j in range(rows)], axis=0)
    by_rhs = pltpu.einshape("abc->bac", by_row)
    iterate_out[:, 0] = iterate[:, 0] + by_rhs[:rhs] * inverse[...]
    residual_out[:, 0] = by_rhs[rhs:] * root[...]


def on_device(iterate, residual, labels, boundary):
    rhs, depth, rows, nx = residual.shape
    assert depth == 2 and REACH == 3 and rows % rhs == 0 and rhs % 8 == 0 and lax.axis_size("gz") % 2 == 0
    odd = (lax.axis_index("gz") % 2).astype(jnp.int32).reshape(1)
    vmem = pl.BlockSpec(memory_space=pltpu.VMEM)
    smem = pl.BlockSpec(memory_space=pltpu.SMEM)

    def array(*shape, dtype=f32):
        return jax.ShapeDtypeStruct(shape, dtype)

    def params(mib):
        return pltpu.CompilerParams(vmem_limit_bytes=mib * 2**20)

    count = rows // rhs
    mine, ahead = pl.pallas_call(
        prepare_kernel,
        out_shape=(array(rows + 4 * count, rhs, nx), array(rows + 3 * count, rhs, nx)),
        in_specs=[smem, vmem, vmem, vmem],
        out_specs=(vmem, vmem),
        compiler_params=params(16),
    )(odd, residual, labels, boundary)

    near2 = swapped(mine)
    far3 = relayed(ahead)
    near3 = relayed(mine, back=True)
    own_before, own_behind = rows_beside(
        jnp.stack([mine[:REACH], ahead[:REACH]]), jnp.stack([mine[rows - REACH : rows], ahead[rows - REACH : rows]])
    )
    last = jnp.concatenate([ahead[:rows], own_before[1, -1:], own_behind[1, :1]], axis=0)
    here = jnp.minimum(near2[0, 0, 0], far3[0, 0, 0]) >= jnp.finfo(f32).min
    near1 = swapped(jnp.where(here, last, 0.0))
    far1 = relayed(near2)
    far2 = relayed(near1)

    edges = EDGES + sum(part is not None for _, *parts in FIELDS for part in parts)
    before, behind = rows_beside(
        *pl.pallas_call(
            partial(edges_kernel, rows),
            out_shape=(array(edges, rhs, nx),) * 2,
            in_specs=[vmem] * 6,
            out_specs=(vmem, vmem),
            compiler_params=params(12),
        )(near1, near2, far1, far3, near3, mine)
    )

    def planes(number):
        return (number, rows + 2 * REACH, rhs, nx)

    cells = (depth + 2 * REACH, rows + 2 * MARGIN, nx)
    inverse, sx, sy, sz, root, u0, u1, u2, split01, moments = pl.pallas_call(
        partial(early_kernel, rows),
        out_shape=(array(*cells),) * 5
        + tuple(array(*planes(number)) for number in (3, 2, 2))
        + (array(depth, rows, 4 * rhs, nx, dtype=bf16), array(rhs, 128)),
        in_specs=[vmem] * 11,
        out_specs=(vmem,) * 10,
        scratch_shapes=[pltpu.VMEM(planes(number), f32) for number in (4, 2)]
        + [pltpu.VMEM((cells[0] + 2,) + cells[1:], f32)] * 2
        + [pltpu.VMEM(cells, f32)],
        compiler_params=params(24),
    )(far3, far1, mine, ahead, own_before, own_behind, near1, near2, near3, before, behind)

    moments, split23 = pl.pallas_call(
        partial(late_kernel, rows),
        out_shape=(array(rhs, 128), array(depth, rows, 4 * rhs, nx, dtype=bf16)),
        in_specs=[vmem] * 9,
        out_specs=(vmem, vmem),
        scratch_shapes=[pltpu.VMEM(planes(number), f32) for number in (1, 2, 2)],
        compiler_params=params(20),
    )(far2, u0, u1, u2, moments, inverse, sx, sy, sz)

    moments = all_sum(moments, ("gy", "gz"))

    tile = 8
    plane_rows = pl.BlockSpec((rhs, 1, tile, nx), lambda z, y, odd: (0, jnp.bitwise_xor(z, odd[0]), y, 0))
    cell_rows = pl.BlockSpec((None, tile, nx), lambda z, y, odd: (z + REACH, y + MARGIN // tile, 0))
    return pl.pallas_call(
        outputs_kernel,
        out_shape=(array(*iterate.shape), array(*residual.shape)),
        grid_spec=pltpu.PrefetchScalarGridSpec(
            num_scalar_prefetch=1,
            grid=(depth, rows // tile),
            in_specs=[
                pl.BlockSpec((rhs, 128), lambda z, y, odd: (0, 0)),
                *[pl.BlockSpec((1, tile, 4 * rhs, nx), lambda z, y, odd: (z, y, 0, 0))] * 2,
                cell_rows,
                cell_rows,
                plane_rows,
            ],
            out_specs=(plane_rows, plane_rows),
            scratch_shapes=[pltpu.VMEM((4 * rhs, 8 * rhs), bf16)],
        ),
        compiler_params=params(10),
    )(odd, moments, split01, split23, inverse, root, iterate)


def solution(mesh):
    placed = (
        P(None, ("regions", "gz"), "gy", None),
        P(None, ("regions", "gz"), "gy", None),
        P(("regions", "gz"), "gy", None),
        P(("regions", "gz"), "gy", None),
    )
    return jax.shard_map(
        on_device,
        mesh=mesh,
        in_specs=placed,
        out_specs=(P(None, ("regions", "gz"), "gy", None), P(None, ("regions", "gz"), "gy", None)),
        check_vma=False,
    )
```

```python
import math
from functools import partial

import jax
import jax.numpy as jnp
from jax import lax
from jax.experimental import pallas as pl
from jax.experimental.pallas import tpu as pltpu
from jax.sharding import PartitionSpec as P

NCLASS = 8
ITERS = 3
REACH = ITERS

contrast_log = 4.0 * math.log(10.0)
highest = lax.Precision.HIGHEST
f32 = jnp.float32
bf16 = jnp.bfloat16


def moved(block, axis, pairs):
    return lax.ppermute(block, axis, pairs)


def shifted(block, axis, step):
    count = lax.axis_size(axis)
    return moved(block, axis, [(i, i + step) for i in range(count) if 0 <= i + step < count])


def swapped(block):
    return moved(block, "gz", [(i, i ^ 1) for i in range(lax.axis_size("gz"))])


def relayed(block, back=False):
    count = lax.axis_size("gz")
    steps = [(i, i + 2 - 4 * (i % 2)) for i in range(count)]
    pairs = [(i, j) for i, j in steps if 0 <= j < count]
    return moved(block, "gz", [(j, i) for i, j in pairs] if back else pairs)


def rows_beside(before, after):
    count = lax.axis_size("gy")
    if count != 2:
        return shifted(after, "gy", 1), shifted(before, "gy", -1)
    second = lax.axis_index("gy") == 1
    other = moved(jnp.where(second, before, after), "gy", [(0, 1), (1, 0)])
    zero = jnp.zeros_like(other)
    return jnp.where(second, other, zero), jnp.where(second, zero, other)


def all_sum(values, axes):
    for axis in axes:
        count = lax.axis_size(axis)
        if count & (count - 1):
            values = lax.psum(values, axis)
            continue
        step = 1
        while step < count:
            values = values + lax.ppermute(values, axis, [(i, i ^ step) for i in range(count)])
            step *= 2
    return values


def face_of(center, beside):
    return jnp.where(beside > 0.0, 2.0 * center * beside / (center + beside), center)


LATE = 1
BESIDE = ((5, 0, 2), (6, 2, 1), (2, 3, 2))
EDGES = 5
FIELDS = (
    ("far3", 0, None), ("far3", 1, 2), ("far1", 1, 3), ("far1", 0, 2), ("mine", 0, 2),
    ("mine", 1, 3), ("near2", 1, 3), ("near2", 0, 2), ("near3", 0, 2), ("near3", 1, None),
)
MARGIN = 8


def prepare_kernel(
    odd, residual, labels, boundary, mine_a, mine_b, ahead, back, block, label_cells, boundary_cells, arrived
):
    rhs, depth, rows, nx = residual.shape
    half = rhs // 2
    copies = [
        pltpu.make_async_copy(labels, label_cells, arrived.at[0]),
        pltpu.make_async_copy(boundary, boundary_cells, arrived.at[1]),
    ] + [
        pltpu.make_async_copy(
            residual.at[:, jnp.bitwise_xor(place, odd[0])], block.at[place], arrived.at[2 + place]
        )
        for place in range(depth)
    ]
    for copy in copies:
        copy.start()
    for copy in copies[:2]:
        copy.wait()
    for place in range(depth):
        plane = jnp.bitwise_xor(place, odd[0])
        for message, order in ((mine_a, (0, 1, 2, 3)), (ahead, (0, 1, None, 2)), (back, (0, 1, 2, None))):
            size = message.shape[1]
            count = rows // size
            for part in range(count):
                cells = pl.ds(part * size, size)
                values = (
                    jnp.exp(label_cells[plane, cells, :].astype(f32) * (contrast_log / (NCLASS - 1))),
                    (1 - boundary_cells[plane, cells, :]).astype(f32),
                )
                for kind, value in enumerate(values):
                    at = order[2 * kind + place]
                    if at is not None:
                        message[rows + at * count + part] = value

    for place in range(depth):
        copies[2 + place].wait()

        def turn(group, carry, place=place):
            here = pl.ds(group * 8, 8)
            turned = pltpu.einshape("abc->bac", block[place, :, here, :])
            if place == 0:
                mine_a[here] = turned[:, :half]
                mine_b[here] = turned[:, half:]
                back[here] = turned
            else:
                ahead[here] = turned
            return carry

        lax.fori_loop(0, rows // 8, turn, 0)


def second_kernel(rows, ahead, own_before, own_behind, near2, out):
    del near2

    def copy_rows(y, size):
        for j in range(size):
            out[y + j] = ahead[y + j]

    row_blocks(0, rows, copy_rows, 16)
    out[rows] = own_before[1, REACH - 1]
    out[rows + 1] = own_behind[1, 0]


def field_edges_kernel(rows, near2, far1, far3, near3, mine, first, last):
    messages = {"near2": near2, "far1": far1, "far3": far3, "near3": near3, "mine": mine}
    place = 0
    for name, *parts in FIELDS:
        message = messages[name]
        size = message.shape[1]
        count = rows // size
        for part in parts:
            if part is not None:
                start = rows + part * count
                first[place] = message[start, :MARGIN]
                last[place] = message[start + count - 1, size - MARGIN :]
                place += 1


def edges_kernel(rows, near1, near2a, near2b, far1a, far1b, inverse, first, last):
    del inverse
    half = near2a.shape[1]
    for (_, place, number), sources in zip(BESIDE, ((near1,), (near2a, near2b), (far1a, far1b))):
        for index, source in enumerate(sources):
            part = slice(None) if len(sources) == 1 else slice(index * half, (index + 1) * half)
            first[place : place + number, part] = source[:number]
            last[place : place + number, part] = source[rows - number : rows]


def couplings_kernel(rows, far3, far1, mine, near2, near3, before, behind, inverse, sx, sy, sz, root, coef, inner, masked):
    messages = {"near2": near2, "far1": far1, "far3": far3, "near3": near3, "mine": mine}
    fill_cells(rows, messages, before, behind, coef, inner)
    make_operator(coef, inner, inverse, sx, sy, sz, root, masked)


def fill_cells(rows, messages, before, behind, coef, inner):
    place = 0
    for plane, (name, *parts) in enumerate(FIELDS):
        for part, out in zip(parts, (coef, inner)):
            if part is None:
                continue
            rhs = messages[name].shape[1]
            count = rows // rhs
            for block in range(count):
                out[plane, MARGIN + block * rhs : MARGIN + (block + 1) * rhs] = messages[name][
                    rows + part * count + block
                ]
            out[plane, :MARGIN] = before[place]
            out[plane, MARGIN + rows :] = behind[place]
            place += 1


def make_operator(coef, inner, inverse, sx, sy, sz, root, masked):
    planes, height, nx = inverse.shape
    lane = lax.broadcasted_iota(jnp.int32, (height, nx), 1)
    inside = lane < nx - 1

    def one_plane(plane, carry):
        here = coef[plane + 1]
        flag = inner[plane + 1]
        right = jnp.where(inside, pltpu.roll(here, nx - 1, 1), 0.0)
        left = jnp.where(lane > 0, pltpu.roll(here, 1, 1), 0.0)
        behind, before = pltpu.roll(here, height - 1, 0), pltpu.roll(here, 1, 0)
        along_x, along_y = face_of(here, right), face_of(here, behind)
        along_z = face_of(here, coef[plane + 2])
        total = along_x + jnp.where(left > 0.0, pltpu.roll(along_x, 1, 1), here)
        total += along_y + jnp.where(before > 0.0, pltpu.roll(along_y, 1, 0), here)
        total += along_z + face_of(here, coef[plane])
        diagonal = flag * total + (1.0 - flag)
        square = jnp.sqrt(diagonal)
        reciprocal = 1.0 / square
        root[plane] = square
        inverse[plane] = reciprocal
        scale = flag * reciprocal
        masked[plane] = scale
        sx[plane] = jnp.where(inside, scale * along_x * pltpu.roll(scale, nx - 1, 1), 0.0)
        sy[plane] = scale * along_y * pltpu.roll(scale, height - 1, 0)
        sz[plane] = scale * along_z
        return carry

    lax.fori_loop(0, planes, one_plane, 0)

    def next_plane(plane, carry):
        sz[plane] = sz[plane] * masked[plane + 1]
        return carry

    lax.fori_loop(0, planes - 1, next_plane, 0)


def cell_row(ref, plane, y):
    return ref[plane, pl.ds(y + (MARGIN - REACH), 1), :]


def row_blocks(start, stop, body, size):
    blocks = -(-(stop - start) // size)
    size = -(-(stop - start) // blocks)

    def step(block, carry):
        body(jnp.minimum(start + block * size, stop - size), size)
        return carry

    lax.fori_loop(0, blocks, step, 0)


def apply_rows(operator, plane, start, before, here, after, size):
    sx, sy, sz = operator
    ref, index = here
    out = []
    last, center = ref[index, start - 1], ref[index, start]
    below = cell_row(sy, plane, start - 1)
    width = center.shape[-1]
    for j in range(size):
        y = start + j
        following = ref[index, y + 1]
        above = cell_row(sy, plane, y)
        ahead = cell_row(sx, plane, y)
        total = ahead * pltpu.roll(center, width - 1, 1) + pltpu.roll(ahead * center, 1, 1)
        total += above * following + below * last
        total += cell_row(sz, plane, y) * after[0][after[1], y]
        total += cell_row(sz, plane - 1, y) * before[0][before[1], y]
        out.append(total)
        last, center, below = center, following, above
    return out


def spread(plane, depth=2):
    return max(REACH - plane, plane - (REACH + depth - 1), 0)


def scale_rows(plane, source, first, dst, start, count, inverse, part=slice(None)):
    out, place = dst

    def body(j, size):
        for i in range(size):
            out[place, start + j + i, part] = source[first + j + i] * cell_row(inverse, plane, start + j + i)

    if count < 8:
        body(0, count)
    else:
        row_blocks(0, count, body, 16)


def apply_plane(rows, power, plane, operator, fields):
    reach = REACH - power - spread(plane)
    src = [fields[power - 1, plane + offset] for offset in (-1, 0, 1)]
    out, place = fields[power, plane]

    def body(y, size):
        for j, values in enumerate(apply_rows(operator, plane, y, *src, size)):
            out[place, y + j] = values

    row_blocks(REACH - reach, REACH + rows + reach, body, 34)


def halves(blocks):
    stack = jnp.concatenate(blocks, axis=0)
    high = stack.astype(bf16)
    low = (stack - high.astype(f32)).astype(bf16)
    return jnp.concatenate([high, low], axis=0)


def inner_products(left, right):
    return lax.dot_general(left, right, (((1,), (1,)), ((), ())), preferred_element_type=f32)


def whole(gram, left, right):
    gram = gram[:left] + gram[left : 2 * left]
    return gram[:, :right] + gram[:, right : 2 * right]


def early_kernel(
    rows, far3, far1a, far1b, mine_a, mine_b, ahead, own_before, own_behind, near1, near2a, near2b, near3,
    before, behind, inverse, sx, sy, sz, u0_out, u1_out, u2_out, split, moments, u0, u1,
):
    operator = (sx, sy, sz)
    fields = {(0, plane): (u0_out, index) for index, plane in enumerate((0, 2, 3))}
    fields.update({(0, plane): (u0, plane - 4) for plane in range(4, 8)})
    fields.update({(1, 3): (u1_out, 0), (1, 4): (u1_out, 1), (1, 5): (u1, 0), (1, 6): (u1, 1)})
    fields.update({(2, 4): (u2_out, 0), (2, 5): (u2_out, 1)})
    first, last = REACH, REACH + rows
    half = mine_a.shape[1]
    for plane, source in ((0, far3), (4, ahead), (5, near1), (7, near3)):
        scale_rows(plane, source, 0, fields[0, plane], first, rows, inverse)
    for plane, sources in ((2, (far1a, far1b)), (3, (mine_a, mine_b)), (6, (near2a, near2b))):
        for source, part in zip(sources, (slice(0, half), slice(half, None))):
            scale_rows(plane, source, 0, fields[0, plane], first, rows, inverse, part)
    for plane in (3, 4):
        scale_rows(plane, own_before.at[plane - 3], 0, fields[0, plane], 0, REACH, inverse)
        scale_rows(plane, own_behind.at[plane - 3], 0, fields[0, plane], last, REACH, inverse)
    for plane, place, count in BESIDE:
        scale_rows(plane, before, place, fields[0, plane], first - count, count, inverse)
        scale_rows(plane, behind, place, fields[0, plane], last, count, inverse)
    for power, plane in ((1, 3), (1, 4), (1, 5), (1, 6), (2, 4), (2, 5)):
        apply_plane(rows, power, plane, operator, fields)

    rhs = u0.shape[2]
    gram = jnp.zeros((4 * rhs, 4 * rhs), f32)
    for plane in range(2):

        def gram_rows(block, total, plane=plane):
            for group in range(4):
                parts = []
                for j in range(4):
                    y = block * 16 + group * 4 + j
                    sources = [fields[power, plane + REACH] for power in range(2)]
                    both = halves([ref[index, y + REACH] for ref, index in sources])
                    split[plane, y] = both
                    parts.append(both)
                wide = jnp.concatenate(parts, axis=1)
                total = total + inner_products(wide, wide)
            return total

        gram = lax.fori_loop(0, rows // 16, gram_rows, gram)
    gram = whole(gram, 2 * rhs, 2 * rhs)
    moments[:, : 2 * rhs] = gram[:rhs]
    moments[:, 2 * rhs : 3 * rhs] = gram[rhs:, rhs:]


def late_kernel(
    rows, far2, u0_in, u1_in, u2_in, moments_in, inverse, sx, sy, sz, moments, split, u0, u1, u2
):
    operator = (sx, sy, sz)
    fields = {(0, plane): (u0_in, index) for index, plane in enumerate((0, 2, 3))}
    fields[0, LATE] = (u0, 0)
    fields.update({(1, 1): (u1, 0), (1, 2): (u1, 1), (1, 3): (u1_in, 0), (1, 4): (u1_in, 1)})
    fields.update({(2, 2): (u2, 0), (2, 3): (u2, 1), (2, 4): (u2_in, 0), (2, 5): (u2_in, 1)})
    first, last = REACH, REACH + rows
    for place, start, count in ((0, first, rows), (rows, first - 1, 1), (rows + 1, last, 1)):
        scale_rows(LATE, far2, place, fields[0, LATE], start, count, inverse)
    for power, plane in ((1, 1), (1, 2), (2, 2), (2, 3)):
        apply_plane(rows, power, plane, operator, fields)

    rhs = u0.shape[2]
    gram = jnp.zeros((6 * rhs, 2 * rhs), f32)
    for plane in range(2):
        level = plane + REACH

        def gram_rows(block, total, plane=plane, level=level):
            start = block * 16
            y = start + REACH
            last = apply_rows(operator, level, y, *[fields[2, level + offset] for offset in (-1, 0, 1)], 16)
            for group in range(4):
                left, right = [], []
                for j in range(group * 4, group * 4 + 4):
                    ref, index = fields[2, level]
                    both = halves([ref[index, y + j], last[j]])
                    split[plane, start + j] = both
                    left.append(jnp.concatenate([halves([u1_in[plane, y + j]]), both], axis=0))
                    right.append(jnp.concatenate([both[:rhs], both[2 * rhs : 3 * rhs]], axis=0))
                total = total + inner_products(jnp.concatenate(left, axis=1), jnp.concatenate(right, axis=1))
            return total

        gram = lax.fori_loop(0, rows // 16, gram_rows, gram)
    gram = gram[:, :rhs] + gram[:, rhs:]
    blocks = [gram[part * rhs : (part + 1) * rhs] for part in range(6)]
    moments[:, : 3 * rhs] = moments_in[:, : 3 * rhs]
    moments[:, 3 * rhs : 4 * rhs] = blocks[0] + blocks[1]
    moments[:, 4 * rhs : 5 * rhs] = blocks[2] + blocks[4]
    moments[:, 5 * rhs : 6 * rhs] = blocks[3] + blocks[5]
    moments[:, 6 * rhs :] = jnp.zeros((rhs, moments.shape[1] - 6 * rhs), f32)


def inverse_of_pair(a, b, c, d):
    scale = 1.0 / (a * d - b * c)
    return d * scale, -b * scale, -c * scale, a * scale


def times(p, q):
    a, b, c, d = p
    e, f, g, h = q
    return a * e + b * g, a * f + b * h, c * e + d * g, c * f + d * h


def inverse_of_four(m):
    p, q = (m[0][0], m[0][1], m[1][0], m[1][1]), (m[0][2], m[0][3], m[1][2], m[1][3])
    r, s = (m[2][0], m[2][1], m[3][0], m[3][1]), (m[2][2], m[2][3], m[3][2], m[3][3])
    inner = inverse_of_pair(*p)
    right, left = times(inner, q), times(r, inner)
    outer = inverse_of_pair(*[x - y for x, y in zip(s, times(r, right))])
    lower = [-x for x in times(outer, left)]
    upper = [-x for x in times(right, outer)]
    corner = [x - y for x, y in zip(inner, times(right, lower))]
    return (
        (corner[0], corner[1], upper[0], upper[1]),
        (corner[2], corner[3], upper[2], upper[3]),
        (lower[0], lower[1], outer[0], outer[1]),
        (lower[2], lower[3], outer[2], outer[3]),
    )


def eliminate(stacked, size):
    tiles, height, width = stacked.shape
    lane = lax.broadcasted_iota(jnp.int32, (height, width), 1)

    def everywhere(row):
        return jnp.broadcast_to(row, (height, width))

    for k in range(0, size, 4):
        if k and k % height == 0:
            stacked = stacked[1:]
        at = k % height
        rows = [everywhere(stacked[0, at + i : at + i + 1]) for i in range(4)]
        columns = [jnp.broadcast_to(stacked[:, :, k + i : k + i + 1], stacked.shape) for i in range(4)]
        block = [[everywhere(columns[j][0, at + i : at + i + 1]) for j in range(4)] for i in range(4)]
        inverse = inverse_of_four(block)
        pivots = (lane >= k) & (lane < k + 4)
        result = jnp.where(pivots[None], 0.0, stacked)
        for i in range(4):
            mix = (inverse[i][0] * rows[0] + inverse[i][1] * rows[1]) + (
                inverse[i][2] * rows[2] + inverse[i][3] * rows[3]
            )
            for j in range(4):
                mix = jnp.where(lane == k + j, -inverse[i][j], mix)
            result = result - columns[i] * mix[None]
        stacked = result
    return stacked[1:]


def mixing(moments, rhs):
    width = moments.shape[1]
    lane = lax.broadcasted_iota(jnp.int32, (rhs, width), 1)
    row = lax.broadcasted_iota(jnp.int32, (rhs, width), 0)
    size = REACH * rhs
    rolled = [moments] + [pltpu.roll(moments, width - i * rhs, 1) for i in range(1, REACH + 1)]
    energy = [rolled[i] - rolled[i + 1] for i in range(REACH)]
    tiles = jnp.concatenate(energy + [moments], axis=0).reshape(-1, 8, width)
    solved = eliminate(tiles, size).reshape(rhs, width)
    solved = jnp.where(lane < size, solved, 0.0)
    residual = (row == lane).astype(f32) - (solved - pltpu.roll(solved, rhs, 1))
    return solved, residual


def outputs_kernel(odd, moments, split01, split23, inverse, root, iterate, iterate_out, residual_out, coefs):
    rhs = iterate.shape[0]
    rows = split01.shape[1]

    @pl.when((pl.program_id(0) == 0) & (pl.program_id(1) == 0))
    def _():
        solved, residual = mixing(moments[...], rhs)
        both = jnp.concatenate([solved[:, : 4 * rhs], residual[:, : 4 * rhs]], axis=0)
        high = both.astype(bf16).astype(f32)
        stacked = jnp.concatenate([high, both - high], axis=0)
        pair01, pair23 = stacked[:, : 2 * rhs], stacked[:, 2 * rhs :]
        coefs[...] = jnp.concatenate([pair01, pair01, pair23, pair23], axis=1).astype(bf16)

    wide = jnp.concatenate(
        [jnp.concatenate([split01[0, j], split23[0, j]], axis=0) for j in range(rows)], axis=1
    )
    mixed = jnp.dot(coefs[...], wide, preferred_element_type=f32)
    mixed = mixed[: 2 * rhs] + mixed[2 * rhs :]
    nx = split01.shape[-1]
    by_row = jnp.stack([mixed[:, j * nx : (j + 1) * nx] for j in range(rows)], axis=0)
    by_rhs = pltpu.einshape("abc->bac", by_row)
    iterate_out[:, 0] = iterate[:, 0] + by_rhs[:rhs] * inverse[...]
    residual_out[:, 0] = by_rhs[rhs:] * root[...]


def on_device(iterate, residual, labels, boundary):
    rhs, depth, rows, nx = residual.shape
    assert depth == 2 and REACH == 3 and rows % rhs == 0 and rhs % 8 == 0 and lax.axis_size("gz") % 2 == 0
    odd = (lax.axis_index("gz") % 2).astype(jnp.int32).reshape(1)
    vmem = pl.BlockSpec(memory_space=pltpu.VMEM)
    smem = pl.BlockSpec(memory_space=pltpu.SMEM)

    def array(*shape, dtype=f32):
        return jax.ShapeDtypeStruct(shape, dtype)

    def params(mib):
        return pltpu.CompilerParams(vmem_limit_bytes=mib * 2**20)

    anywhere = pl.BlockSpec(memory_space=pl.ANY)

    half = rhs // 2
    wide = rows + 3 * rows // rhs
    mine_a, mine_b, ahead, back = pl.pallas_call(
        prepare_kernel,
        out_shape=(
            array(rows + 4 * rows // half, half, nx), array(rows, half, nx), array(wide, rhs, nx), array(wide, rhs, nx)
        ),
        in_specs=[smem] + [pl.BlockSpec(memory_space=pltpu.HBM)] * 3,
        out_specs=(vmem,) * 4,
        scratch_shapes=[
            pltpu.VMEM((depth, rhs, rows, nx), f32),
            pltpu.VMEM(labels.shape, jnp.int32),
            pltpu.VMEM(boundary.shape, jnp.int32),
            pltpu.SemaphoreType.DMA((2 + depth,)),
        ],
        compiler_params=params(55),
    )(odd, residual, labels, boundary)

    near2a = swapped(mine_a)
    far3 = relayed(ahead)
    near3 = relayed(back, back=True)
    near2b = swapped(mine_b)

    def both(first, last, second):
        return jnp.stack([jnp.concatenate([first[second], last[second]], axis=1), ahead[second]])

    own_before, own_behind = rows_beside(
        both(mine_a, mine_b, slice(0, REACH)), both(mine_a, mine_b, slice(rows - REACH, rows))
    )
    near1 = swapped(
        pl.pallas_call(
            partial(second_kernel, rows),
            out_shape=array(rows + 2, rhs, nx),
            in_specs=[vmem, vmem, vmem, anywhere],
            out_specs=vmem,
            compiler_params=params(8),
        )(ahead, own_before, own_behind, near2b)
    )
    far1a = relayed(near2a)
    far1b = relayed(near2b)
    far2 = relayed(near1)

    number = sum(part is not None for _, *parts in FIELDS for part in parts)
    fields_before, fields_behind = rows_beside(
        *pl.pallas_call(
            partial(field_edges_kernel, rows),
            out_shape=(array(number, MARGIN, nx),) * 2,
            in_specs=[vmem] * 5,
            out_specs=(vmem, vmem),
            compiler_params=params(8),
        )(near2a, far1a, far3, near3, mine_a)
    )
    cells = (depth + 2 * REACH, rows + 2 * MARGIN, nx)
    inverse, sx, sy, sz, root = pl.pallas_call(
        partial(couplings_kernel, rows),
        out_shape=(array(*cells),) * 5,
        in_specs=[vmem] * 7,
        out_specs=(vmem,) * 5,
        scratch_shapes=[pltpu.VMEM((cells[0] + 2,) + cells[1:], f32)] * 2 + [pltpu.VMEM(cells, f32)],
        compiler_params=params(14),
    )(far3, far1a, mine_a, near2a, near3, fields_before, fields_behind)

    before, behind = rows_beside(
        *pl.pallas_call(
            partial(edges_kernel, rows),
            out_shape=(array(EDGES, rhs, nx),) * 2,
            in_specs=[vmem] * 5 + [anywhere],
            out_specs=(vmem, vmem),
            compiler_params=params(8),
        )(near1, near2a, near2b, far1a, far1b, inverse)
    )

    def planes(number):
        return (number, rows + 2 * REACH, rhs, nx)

    u0, u1, u2, split01, moments = pl.pallas_call(
        partial(early_kernel, rows),
        out_shape=tuple(array(*planes(number)) for number in (3, 2, 2))
        + (array(depth, rows, 4 * rhs, nx, dtype=bf16), array(rhs, 128)),
        in_specs=[vmem] * 18,
        out_specs=(vmem,) * 5,
        scratch_shapes=[pltpu.VMEM(planes(number), f32) for number in (4, 2)],
        compiler_params=params(24),
    )(
        far3, far1a, far1b, mine_a, mine_b, ahead, own_before, own_behind, near1, near2a, near2b, near3,
        before, behind, inverse, sx, sy, sz,
    )

    moments, split23 = pl.pallas_call(
        partial(late_kernel, rows),
        out_shape=(array(rhs, 128), array(depth, rows, 4 * rhs, nx, dtype=bf16)),
        in_specs=[vmem] * 9,
        out_specs=(vmem, vmem),
        scratch_shapes=[pltpu.VMEM(planes(number), f32) for number in (1, 2, 2)],
        compiler_params=params(20),
    )(far2, u0, u1, u2, moments, inverse, sx, sy, sz)

    moments = all_sum(moments, ("gy", "gz"))

    tile = 8
    plane_rows = pl.BlockSpec((rhs, 1, tile, nx), lambda z, y, odd: (0, jnp.bitwise_xor(z, odd[0]), y, 0))
    cell_rows = pl.BlockSpec((None, tile, nx), lambda z, y, odd: (z + REACH, y + MARGIN // tile, 0))
    return pl.pallas_call(
        outputs_kernel,
        out_shape=(array(*iterate.shape), array(*residual.shape)),
        grid_spec=pltpu.PrefetchScalarGridSpec(
            num_scalar_prefetch=1,
            grid=(depth, rows // tile),
            in_specs=[
                pl.BlockSpec((rhs, 128), lambda z, y, odd: (0, 0)),
                *[pl.BlockSpec((1, tile, 4 * rhs, nx), lambda z, y, odd: (z, y, 0, 0))] * 2,
                cell_rows,
                cell_rows,
                plane_rows,
            ],
            out_specs=(plane_rows, plane_rows),
            scratch_shapes=[pltpu.VMEM((4 * rhs, 8 * rhs), bf16)],
        ),
        compiler_params=params(10),
    )(odd, moments, split01, split23, inverse, root, iterate)


def solution(mesh):
    placed = (
        P(None, ("regions", "gz"), "gy", None),
        P(None, ("regions", "gz"), "gy", None),
        P(("regions", "gz"), "gy", None),
        P(("regions", "gz"), "gy", None),
    )
    return jax.shard_map(
        on_device,
        mesh=mesh,
        in_specs=placed,
        out_specs=(P(None, ("regions", "gz"), "gy", None), P(None, ("regions", "gz"), "gy", None)),
        check_vma=False,
    )
```

```python
import math
from functools import partial

import jax
import jax.numpy as jnp
from jax import lax
from jax.experimental import pallas as pl
from jax.experimental.pallas import tpu as pltpu
from jax.sharding import PartitionSpec as P

NCLASS = 8
ITERS = 3
REACH = ITERS

contrast_log = 4.0 * math.log(10.0)
highest = lax.Precision.HIGHEST
f32 = jnp.float32
bf16 = jnp.bfloat16


def moved(block, axis, pairs):
    return lax.ppermute(block, axis, pairs)


def shifted(block, axis, step):
    count = lax.axis_size(axis)
    return moved(block, axis, [(i, i + step) for i in range(count) if 0 <= i + step < count])


def swapped(block):
    return moved(block, "gz", [(i, i ^ 1) for i in range(lax.axis_size("gz"))])


def relayed(block, back=False):
    count = lax.axis_size("gz")
    steps = [(i, i + 2 - 4 * (i % 2)) for i in range(count)]
    pairs = [(i, j) for i, j in steps if 0 <= j < count]
    return moved(block, "gz", [(j, i) for i, j in pairs] if back else pairs)


def rows_beside(before, after):
    count = lax.axis_size("gy")
    if count != 2:
        return shifted(after, "gy", 1), shifted(before, "gy", -1)
    second = lax.axis_index("gy") == 1
    other = moved(jnp.where(second, before, after), "gy", [(0, 1), (1, 0)])
    zero = jnp.zeros_like(other)
    return jnp.where(second, other, zero), jnp.where(second, zero, other)


def all_sum(values, axes):
    for axis in axes:
        count = lax.axis_size(axis)
        if count & (count - 1):
            values = lax.psum(values, axis)
            continue
        step = 1
        while step < count:
            values = values + lax.ppermute(values, axis, [(i, i ^ step) for i in range(count)])
            step *= 2
    return values


def face_of(center, beside):
    return jnp.where(beside > 0.0, 2.0 * center * beside / (center + beside), center)


LATE = 1
BESIDE = ((5, 0, 2), (6, 2, 1), (2, 3, 2))
EDGES = 5
FIELDS = (
    ("far3", 0, None), ("far3", 1, 2), ("far1", 1, 3), ("far1", 0, 2), ("mine", 0, 2),
    ("mine", 1, 3), ("near2", 1, 3), ("near2", 0, 2), ("near3", 0, 2), ("near3", 1, None),
)
MARGIN = 8


def prepare_kernel(
    odd, residual, labels, boundary, mine, ahead, first, last, block, label_cells, boundary_cells, arrived
):
    rhs, depth, rows, nx = residual.shape
    copies = [
        pltpu.make_async_copy(labels, label_cells, arrived.at[0]),
        pltpu.make_async_copy(boundary, boundary_cells, arrived.at[1]),
    ] + [
        pltpu.make_async_copy(
            residual.at[:, jnp.bitwise_xor(place, odd[0])], block.at[place], arrived.at[2 + place]
        )
        for place in range(depth)
    ]
    for copy in copies:
        copy.start()
    for copy in copies[:2]:
        copy.wait()
    count = rows // rhs
    for place in range(depth):
        plane = jnp.bitwise_xor(place, odd[0])
        for part in range(count):
            cells = pl.ds(part * rhs, rhs)
            coef = jnp.exp(label_cells[plane, cells, :].astype(f32) * (contrast_log / (NCLASS - 1)))
            inner = (1 - boundary_cells[plane, cells, :]).astype(f32)
            for message in (mine, ahead):
                message[rows + place * count + part] = coef
            mine[rows + (2 + place) * count + part] = inner
            if place == 1:
                ahead[rows + 2 * count + part] = inner

    for place, out in ((0, mine), (1, ahead)):
        copies[2 + place].wait()

        def turn(group, carry, place=place, out=out):
            here = pl.ds(group * 8, 8)
            out[here] = pltpu.einshape("abc->bac", block[place, :, here, :])
            return carry

        lax.fori_loop(0, rows // 8, turn, 0)
        first[place] = out[:REACH]
        last[place] = out[rows - REACH : rows]


def second_kernel(rows, ahead, own_before, own_behind, near2, far3, out):
    del near2, far3

    def copy_rows(y, size):
        for j in range(size):
            out[y + j] = ahead[y + j]

    row_blocks(0, rows, copy_rows, 16)
    out[rows] = own_before[1, REACH - 1]
    out[rows + 1] = own_behind[1, 0]


def edges_kernel(rows, near1, near2, far1, far3, near3, mine, first, last):
    messages = {"near2": near2, "far1": far1, "far3": far3, "near3": near3, "mine": mine}
    rhs = mine.shape[1]
    count = rows // rhs
    for (_, place, number), source in zip(BESIDE, (near1, near2, far1)):
        first[place : place + number] = source[:number]
        last[place : place + number] = source[rows - number : rows]
    place = EDGES
    for name, *parts in FIELDS:
        for part in parts:
            if part is not None:
                start = rows + part * count
                first[place, :MARGIN] = messages[name][start, :MARGIN]
                last[place, :MARGIN] = messages[name][start + count - 1, rhs - MARGIN :]
                place += 1
                first[place - 1, MARGIN:] = jnp.zeros_like(first[place - 1, MARGIN:])
                last[place - 1, MARGIN:] = jnp.zeros_like(last[place - 1, MARGIN:])


def fill_cells(rows, messages, before, behind, coef, inner):
    place = EDGES
    for plane, (name, *parts) in enumerate(FIELDS):
        for part, out in zip(parts, (coef, inner)):
            if part is None:
                continue
            rhs = messages[name].shape[1]
            count = rows // rhs
            for block in range(count):
                out[plane, MARGIN + block * rhs : MARGIN + (block + 1) * rhs] = messages[name][
                    rows + part * count + block
                ]
            out[plane, :MARGIN] = before[place, :MARGIN]
            out[plane, MARGIN + rows :] = behind[place, :MARGIN]
            place += 1


def make_operator(coef, inner, inverse, sx, sy, sz, root, masked):
    planes, height, nx = inverse.shape
    lane = lax.broadcasted_iota(jnp.int32, (height, nx), 1)
    inside = lane < nx - 1

    def one_plane(plane, carry):
        here = coef[plane + 1]
        flag = inner[plane + 1]
        right = jnp.where(inside, pltpu.roll(here, nx - 1, 1), 0.0)
        left = jnp.where(lane > 0, pltpu.roll(here, 1, 1), 0.0)
        behind, before = pltpu.roll(here, height - 1, 0), pltpu.roll(here, 1, 0)
        along_x, along_y = face_of(here, right), face_of(here, behind)
        along_z = face_of(here, coef[plane + 2])
        total = along_x + jnp.where(left > 0.0, pltpu.roll(along_x, 1, 1), here)
        total += along_y + jnp.where(before > 0.0, pltpu.roll(along_y, 1, 0), here)
        total += along_z + face_of(here, coef[plane])
        diagonal = flag * total + (1.0 - flag)
        square = jnp.sqrt(diagonal)
        reciprocal = 1.0 / square
        root[plane] = square
        inverse[plane] = reciprocal
        scale = flag * reciprocal
        masked[plane] = scale
        sx[plane] = jnp.where(inside, scale * along_x * pltpu.roll(scale, nx - 1, 1), 0.0)
        sy[plane] = scale * along_y * pltpu.roll(scale, height - 1, 0)
        sz[plane] = scale * along_z
        return carry

    lax.fori_loop(0, planes, one_plane, 0)

    def next_plane(plane, carry):
        sz[plane] = sz[plane] * masked[plane + 1]
        return carry

    lax.fori_loop(0, planes - 1, next_plane, 0)


def cell_row(ref, plane, y):
    return ref[plane, pl.ds(y + (MARGIN - REACH), 1), :]


def row_blocks(start, stop, body, size):
    blocks = -(-(stop - start) // size)
    size = -(-(stop - start) // blocks)

    def step(block, carry):
        body(jnp.minimum(start + block * size, stop - size), size)
        return carry

    lax.fori_loop(0, blocks, step, 0)


def apply_rows(operator, plane, start, before, here, after, size):
    sx, sy, sz = operator
    ref, index = here
    out = []
    last, center = ref[index, start - 1], ref[index, start]
    below = cell_row(sy, plane, start - 1)
    width = center.shape[-1]
    for j in range(size):
        y = start + j
        following = ref[index, y + 1]
        above = cell_row(sy, plane, y)
        ahead = cell_row(sx, plane, y)
        total = ahead * pltpu.roll(center, width - 1, 1) + pltpu.roll(ahead * center, 1, 1)
        total += above * following + below * last
        total += cell_row(sz, plane, y) * after[0][after[1], y]
        total += cell_row(sz, plane - 1, y) * before[0][before[1], y]
        out.append(total)
        last, center, below = center, following, above
    return out


def spread(plane, depth=2):
    return max(REACH - plane, plane - (REACH + depth - 1), 0)


def scale_rows(plane, source, first, dst, start, count, inverse):
    out, place = dst

    def body(j, size):
        for i in range(size):
            out[place, start + j + i] = source[first + j + i] * cell_row(inverse, plane, start + j + i)

    if count < 8:
        body(0, count)
    else:
        row_blocks(0, count, body, 16)


def apply_plane(rows, power, plane, operator, fields):
    reach = REACH - power - spread(plane)
    src = [fields[power - 1, plane + offset] for offset in (-1, 0, 1)]
    out, place = fields[power, plane]

    def body(y, size):
        for j, values in enumerate(apply_rows(operator, plane, y, *src, size)):
            out[place, y + j] = values

    row_blocks(REACH - reach, REACH + rows + reach, body, 34)


def halves(blocks):
    stack = jnp.concatenate(blocks, axis=0)
    high = stack.astype(bf16)
    low = (stack - high.astype(f32)).astype(bf16)
    return jnp.concatenate([high, low], axis=0)


def inner_products(left, right):
    return lax.dot_general(left, right, (((1,), (1,)), ((), ())), preferred_element_type=f32)


def whole(gram, left, right):
    gram = gram[:left] + gram[left : 2 * left]
    return gram[:, :right] + gram[:, right : 2 * right]


def early_kernel(
    rows, far3, far1, mine, ahead, own_before, own_behind, near1, near2, near3, before, behind,
    inverse, sx, sy, sz, root, u0_out, u1_out, u2_out, split, moments, u0, u1, coef, inner, masked,
):
    messages = {"near2": near2, "far1": far1, "far3": far3, "near3": near3, "mine": mine}
    fill_cells(rows, messages, before, behind, coef, inner)
    make_operator(coef, inner, inverse, sx, sy, sz, root, masked)
    operator = (sx, sy, sz)
    fields = {(0, plane): (u0_out, index) for index, plane in enumerate((0, 2, 3))}
    fields.update({(0, plane): (u0, plane - 4) for plane in range(4, 8)})
    fields.update({(1, 3): (u1_out, 0), (1, 4): (u1_out, 1), (1, 5): (u1, 0), (1, 6): (u1, 1)})
    fields.update({(2, 4): (u2_out, 0), (2, 5): (u2_out, 1)})
    first, last = REACH, REACH + rows
    for plane, source in ((0, far3), (2, far1), (3, mine), (4, ahead), (5, near1), (6, near2), (7, near3)):
        scale_rows(plane, source, 0, fields[0, plane], first, rows, inverse)
    for plane in (3, 4):
        scale_rows(plane, own_before.at[plane - 3], 0, fields[0, plane], 0, REACH, inverse)
        scale_rows(plane, own_behind.at[plane - 3], 0, fields[0, plane], last, REACH, inverse)
    for plane, place, count in BESIDE:
        scale_rows(plane, before, place, fields[0, plane], first - count, count, inverse)
        scale_rows(plane, behind, place, fields[0, plane], last, count, inverse)
    for power, plane in ((1, 3), (1, 4), (1, 5), (1, 6), (2, 4), (2, 5)):
        apply_plane(rows, power, plane, operator, fields)

    rhs = u0.shape[2]
    gram = jnp.zeros((4 * rhs, 4 * rhs), f32)
    for plane in range(2):

        def gram_rows(block, total, plane=plane):
            for group in range(4):
                parts = []
                for j in range(4):
                    y = block * 16 + group * 4 + j
                    sources = [fields[power, plane + REACH] for power in range(2)]
                    both = halves([ref[index, y + REACH] for ref, index in sources])
                    split[plane, y] = both
                    parts.append(both)
                wide = jnp.concatenate(parts, axis=1)
                total = total + inner_products(wide, wide)
            return total

        gram = lax.fori_loop(0, rows // 16, gram_rows, gram)
    gram = whole(gram, 2 * rhs, 2 * rhs)
    moments[:, : 2 * rhs] = gram[:rhs]
    moments[:, 2 * rhs : 3 * rhs] = gram[rhs:, rhs:]


def late_kernel(
    rows, far2, u0_in, u1_in, u2_in, moments_in, inverse, sx, sy, sz, moments, split, u0, u1, u2
):
    operator = (sx, sy, sz)
    fields = {(0, plane): (u0_in, index) for index, plane in enumerate((0, 2, 3))}
    fields[0, LATE] = (u0, 0)
    fields.update({(1, 1): (u1, 0), (1, 2): (u1, 1), (1, 3): (u1_in, 0), (1, 4): (u1_in, 1)})
    fields.update({(2, 2): (u2, 0), (2, 3): (u2, 1), (2, 4): (u2_in, 0), (2, 5): (u2_in, 1)})
    first, last = REACH, REACH + rows
    for place, start, count in ((0, first, rows), (rows, first - 1, 1), (rows + 1, last, 1)):
        scale_rows(LATE, far2, place, fields[0, LATE], start, count, inverse)
    for power, plane in ((1, 1), (1, 2), (2, 2), (2, 3)):
        apply_plane(rows, power, plane, operator, fields)

    rhs = u0.shape[2]
    gram = jnp.zeros((6 * rhs, 2 * rhs), f32)
    for plane in range(2):
        level = plane + REACH

        def gram_rows(block, total, plane=plane, level=level):
            start = block * 16
            y = start + REACH
            last = apply_rows(operator, level, y, *[fields[2, level + offset] for offset in (-1, 0, 1)], 16)
            for group in range(4):
                left, right = [], []
                for j in range(group * 4, group * 4 + 4):
                    ref, index = fields[2, level]
                    both = halves([ref[index, y + j], last[j]])
                    split[plane, start + j] = both
                    left.append(jnp.concatenate([halves([u1_in[plane, y + j]]), both], axis=0))
                    right.append(jnp.concatenate([both[:rhs], both[2 * rhs : 3 * rhs]], axis=0))
                total = total + inner_products(jnp.concatenate(left, axis=1), jnp.concatenate(right, axis=1))
            return total

        gram = lax.fori_loop(0, rows // 16, gram_rows, gram)
    gram = gram[:, :rhs] + gram[:, rhs:]
    blocks = [gram[part * rhs : (part + 1) * rhs] for part in range(6)]
    moments[:, : 3 * rhs] = moments_in[:, : 3 * rhs]
    moments[:, 3 * rhs : 4 * rhs] = blocks[0] + blocks[1]
    moments[:, 4 * rhs : 5 * rhs] = blocks[2] + blocks[4]
    moments[:, 5 * rhs : 6 * rhs] = blocks[3] + blocks[5]
    moments[:, 6 * rhs :] = jnp.zeros((rhs, moments.shape[1] - 6 * rhs), f32)


def inverse_of_pair(a, b, c, d):
    scale = 1.0 / (a * d - b * c)
    return d * scale, -b * scale, -c * scale, a * scale


def times(p, q):
    a, b, c, d = p
    e, f, g, h = q
    return a * e + b * g, a * f + b * h, c * e + d * g, c * f + d * h


def inverse_of_four(m):
    p, q = (m[0][0], m[0][1], m[1][0], m[1][1]), (m[0][2], m[0][3], m[1][2], m[1][3])
    r, s = (m[2][0], m[2][1], m[3][0], m[3][1]), (m[2][2], m[2][3], m[3][2], m[3][3])
    inner = inverse_of_pair(*p)
    right, left = times(inner, q), times(r, inner)
    outer = inverse_of_pair(*[x - y for x, y in zip(s, times(r, right))])
    lower = [-x for x in times(outer, left)]
    upper = [-x for x in times(right, outer)]
    corner = [x - y for x, y in zip(inner, times(right, lower))]
    return (
        (corner[0], corner[1], upper[0], upper[1]),
        (corner[2], corner[3], upper[2], upper[3]),
        (lower[0], lower[1], outer[0], outer[1]),
        (lower[2], lower[3], outer[2], outer[3]),
    )


def eliminate(stacked, size):
    tiles, height, width = stacked.shape
    lane = lax.broadcasted_iota(jnp.int32, (height, width), 1)

    def everywhere(row):
        return jnp.broadcast_to(row, (height, width))

    for k in range(0, size, 4):
        if k and k % height == 0:
            stacked = stacked[1:]
        at = k % height
        rows = [everywhere(stacked[0, at + i : at + i + 1]) for i in range(4)]
        columns = [jnp.broadcast_to(stacked[:, :, k + i : k + i + 1], stacked.shape) for i in range(4)]
        block = [[everywhere(columns[j][0, at + i : at + i + 1]) for j in range(4)] for i in range(4)]
        inverse = inverse_of_four(block)
        pivots = (lane >= k) & (lane < k + 4)
        result = jnp.where(pivots[None], 0.0, stacked)
        for i in range(4):
            mix = (inverse[i][0] * rows[0] + inverse[i][1] * rows[1]) + (
                inverse[i][2] * rows[2] + inverse[i][3] * rows[3]
            )
            for j in range(4):
                mix = jnp.where(lane == k + j, -inverse[i][j], mix)
            result = result - columns[i] * mix[None]
        stacked = result
    return stacked[1:]


def mixing(moments, rhs):
    width = moments.shape[1]
    lane = lax.broadcasted_iota(jnp.int32, (rhs, width), 1)
    row = lax.broadcasted_iota(jnp.int32, (rhs, width), 0)
    size = REACH * rhs
    rolled = [moments] + [pltpu.roll(moments, width - i * rhs, 1) for i in range(1, REACH + 1)]
    energy = [rolled[i] - rolled[i + 1] for i in range(REACH)]
    tiles = jnp.concatenate(energy + [moments], axis=0).reshape(-1, 8, width)
    solved = eliminate(tiles, size).reshape(rhs, width)
    solved = jnp.where(lane < size, solved, 0.0)
    residual = (row == lane).astype(f32) - (solved - pltpu.roll(solved, rhs, 1))
    return solved, residual


def outputs_kernel(odd, moments, split01, split23, inverse, root, iterate, iterate_out, residual_out, coefs):
    rhs, _, rows, nx = iterate.shape
    plane, block = pl.program_id(0), pl.program_id(1)

    @pl.when((plane == 0) & (block == 0))
    def _():
        solved, residual = mixing(moments[...], rhs)
        both = jnp.concatenate([solved[:, : 4 * rhs], residual[:, : 4 * rhs]], axis=0)
        high = both.astype(bf16).astype(f32)
        stacked = jnp.concatenate([high, both - high], axis=0)
        pair01, pair23 = stacked[:, : 2 * rhs], stacked[:, 2 * rhs :]
        coefs[...] = jnp.concatenate([pair01, pair01, pair23, pair23], axis=1).astype(bf16)

    def group_of_rows(group, carry):
        y = block * rows + group * 8
        wide = jnp.concatenate(
            [jnp.concatenate([split01[plane, y + j], split23[plane, y + j]], axis=0) for j in range(8)], axis=1
        )
        mixed = jnp.dot(coefs[...], wide, preferred_element_type=f32)
        mixed = mixed[: 2 * rhs] + mixed[2 * rhs :]
        by_row = jnp.stack([mixed[:, j * nx : (j + 1) * nx] for j in range(8)], axis=0)
        by_rhs = pltpu.einshape("abc->bac", by_row)
        cells = pl.ds(pl.multiple_of(y + MARGIN, 8), 8)
        here = pl.ds(group * 8, 8)
        iterate_out[:, 0, here] = iterate[:, 0, here] + by_rhs[:rhs] * inverse[plane + REACH, cells]
        residual_out[:, 0, here] = by_rhs[rhs:] * root[plane + REACH, cells]
        return carry

    lax.fori_loop(0, rows // 8, group_of_rows, 0)


def on_device(iterate, residual, labels, boundary):
    rhs, depth, rows, nx = residual.shape
    assert depth == 2 and REACH == 3 and rows % rhs == 0 and rhs % 8 == 0 and lax.axis_size("gz") % 2 == 0
    odd = (lax.axis_index("gz") % 2).astype(jnp.int32).reshape(1)
    vmem = pl.BlockSpec(memory_space=pltpu.VMEM)
    smem = pl.BlockSpec(memory_space=pltpu.SMEM)

    def array(*shape, dtype=f32):
        return jax.ShapeDtypeStruct(shape, dtype)

    def params(mib):
        return pltpu.CompilerParams(vmem_limit_bytes=mib * 2**20)

    anywhere = pl.BlockSpec(memory_space=pl.ANY)

    count = rows // rhs
    mine, ahead, *edges = pl.pallas_call(
        prepare_kernel,
        out_shape=(array(rows + 4 * count, rhs, nx), array(rows + 3 * count, rhs, nx))
        + (array(depth, REACH, rhs, nx),) * 2,
        in_specs=[smem] + [pl.BlockSpec(memory_space=pltpu.HBM)] * 3,
        out_specs=(vmem,) * 4,
        scratch_shapes=[
            pltpu.VMEM((depth, rhs, rows, nx), f32),
            pltpu.VMEM(labels.shape, jnp.int32),
            pltpu.VMEM(boundary.shape, jnp.int32),
            pltpu.SemaphoreType.DMA((2 + depth,)),
        ],
        compiler_params=params(55),
    )(odd, residual, labels, boundary)

    near2 = swapped(mine)
    far3 = relayed(ahead)
    near3 = relayed(mine, back=True)
    own_before, own_behind = rows_beside(*edges)
    near1 = swapped(
        pl.pallas_call(
            partial(second_kernel, rows),
            out_shape=array(rows + 2, rhs, nx),
            in_specs=[vmem, vmem, vmem, anywhere, anywhere],
            out_specs=vmem,
            compiler_params=params(8),
        )(ahead, own_before, own_behind, near2, far3)
    )
    far1 = relayed(near2)
    far2 = relayed(near1)

    edges = EDGES + sum(part is not None for _, *parts in FIELDS for part in parts)
    before, behind = rows_beside(
        *pl.pallas_call(
            partial(edges_kernel, rows),
            out_shape=(array(edges, rhs, nx),) * 2,
            in_specs=[vmem] * 6,
            out_specs=(vmem, vmem),
            compiler_params=params(12),
        )(near1, near2, far1, far3, near3, mine)
    )

    def planes(number):
        return (number, rows + 2 * REACH, rhs, nx)

    cells = (depth + 2 * REACH, rows + 2 * MARGIN, nx)
    inverse, sx, sy, sz, root, u0, u1, u2, split01, moments = pl.pallas_call(
        partial(early_kernel, rows),
        out_shape=(array(*cells),) * 5
        + tuple(array(*planes(number)) for number in (3, 2, 2))
        + (array(depth, rows, 4 * rhs, nx, dtype=bf16), array(rhs, 128)),
        in_specs=[vmem] * 11,
        out_specs=(vmem,) * 10,
        scratch_shapes=[pltpu.VMEM(planes(number), f32) for number in (4, 2)]
        + [pltpu.VMEM((cells[0] + 2,) + cells[1:], f32)] * 2
        + [pltpu.VMEM(cells, f32)],
        compiler_params=params(24),
    )(far3, far1, mine, ahead, own_before, own_behind, near1, near2, near3, before, behind)

    moments, split23 = pl.pallas_call(
        partial(late_kernel, rows),
        out_shape=(array(rhs, 128), array(depth, rows, 4 * rhs, nx, dtype=bf16)),
        in_specs=[vmem] * 9,
        out_specs=(vmem, vmem),
        scratch_shapes=[pltpu.VMEM(planes(number), f32) for number in (1, 2, 2)],
        compiler_params=params(20),
    )(far2, u0, u1, u2, moments, inverse, sx, sy, sz)

    moments = all_sum(moments, ("gy", "gz"))

    tile = math.gcd(rows, 32)
    plane_rows = pl.BlockSpec((rhs, 1, tile, nx), lambda z, y, odd: (0, jnp.bitwise_xor(z, odd[0]), y, 0))
    return pl.pallas_call(
        outputs_kernel,
        out_shape=(array(*iterate.shape), array(*residual.shape)),
        grid_spec=pltpu.PrefetchScalarGridSpec(
            num_scalar_prefetch=1,
            grid=(depth, rows // tile),
            in_specs=[vmem] * 5 + [plane_rows],
            out_specs=(plane_rows, plane_rows),
            scratch_shapes=[pltpu.VMEM((4 * rhs, 8 * rhs), bf16)],
        ),
        compiler_params=params(16),
    )(odd, moments, split01, split23, inverse, root, iterate)


def solution(mesh):
    placed = (
        P(None, ("regions", "gz"), "gy", None),
        P(None, ("regions", "gz"), "gy", None),
        P(("regions", "gz"), "gy", None),
        P(("regions", "gz"), "gy", None),
    )
    return jax.shard_map(
        on_device,
        mesh=mesh,
        in_specs=placed,
        out_specs=(P(None, ("regions", "gz"), "gy", None), P(None, ("regions", "gz"), "gy", None)),
        check_vma=False,
    )
```

```python
import math
from functools import partial

import jax
import jax.numpy as jnp
from jax import lax
from jax.experimental import pallas as pl
from jax.experimental.pallas import tpu as pltpu
from jax.sharding import PartitionSpec as P

NCLASS = 8
ITERS = 3
REACH = ITERS

contrast_log = 4.0 * math.log(10.0)
highest = lax.Precision.HIGHEST
f32 = jnp.float32
bf16 = jnp.bfloat16


def moved(block, axis, pairs):
    return lax.ppermute(block, axis, pairs)


def shifted(block, axis, step):
    count = lax.axis_size(axis)
    return moved(block, axis, [(i, i + step) for i in range(count) if 0 <= i + step < count])


def swapped(block):
    return moved(block, "gz", [(i, i ^ 1) for i in range(lax.axis_size("gz"))])


def relayed(block, back=False):
    count = lax.axis_size("gz")
    steps = [(i, i + 2 - 4 * (i % 2)) for i in range(count)]
    pairs = [(i, j) for i, j in steps if 0 <= j < count]
    return moved(block, "gz", [(j, i) for i, j in pairs] if back else pairs)


def rows_beside(before, after):
    count = lax.axis_size("gy")
    if count != 2:
        return shifted(after, "gy", 1), shifted(before, "gy", -1)
    second = lax.axis_index("gy") == 1
    other = moved(jnp.where(second, before, after), "gy", [(0, 1), (1, 0)])
    zero = jnp.zeros_like(other)
    return jnp.where(second, other, zero), jnp.where(second, zero, other)


def all_sum(values, axes):
    for axis in axes:
        count = lax.axis_size(axis)
        if count & (count - 1):
            values = lax.psum(values, axis)
            continue
        bits = count.bit_length() - 1
        done = 0
        while done < bits:
            taken = 1 if (bits - done) % 2 else 2
            others = [
                lax.ppermute(values, axis, [(i, i ^ (step << done)) for i in range(count)])
                for step in range(1, 1 << taken)
            ]
            values = sum(others, values)
            done += taken
    return values


def face_of(center, beside):
    return jnp.where(beside > 0.0, 2.0 * center * beside / (center + beside), center)


LATE = 1
BESIDE = ((5, 0, 2), (6, 2, 1), (2, 3, 2))
EDGES = 5
FIELDS = (
    ("far3", 0, None), ("far3", 1, 2), ("beyond", 1, 3), ("beyond", 0, 2), ("own", 0, 2),
    ("own", 1, 3), ("pair", 1, 3), ("pair", 0, 2), ("near3", 0, 2), ("near3", 1, None),
)
BEHIND_ROWS = ("far3", "near3")
MARGIN = 8


def prepare_kernel(
    odd, residual, labels, boundary, mine, ahead, back, cells, first, last, block, label_cells, boundary_cells, arrived
):
    rhs, depth, rows, nx = residual.shape
    copies = [
        pltpu.make_async_copy(labels, label_cells, arrived.at[0]),
        pltpu.make_async_copy(boundary, boundary_cells, arrived.at[1]),
    ] + [
        pltpu.make_async_copy(
            residual.at[:, jnp.bitwise_xor(place, odd[0])], block.at[place], arrived.at[2 + place]
        )
        for place in range(depth)
    ]
    for copy in copies:
        copy.start()
    for copy in copies[:2]:
        copy.wait()
    count = rows // rhs
    for place in range(depth):
        plane = jnp.bitwise_xor(place, odd[0])
        for part in range(count):
            here = pl.ds(part * rhs, rhs)
            coef = jnp.exp(label_cells[plane, here, :].astype(f32) * (contrast_log / (NCLASS - 1)))
            inner = (1 - boundary_cells[plane, here, :]).astype(f32)
            cells[place * count + part] = coef
            cells[(2 + place) * count + part] = inner
            for message in (ahead, back):
                message[rows + place * count + part] = coef
            (back, ahead)[place][rows + 2 * count + part] = inner

    for place, outs in ((0, (mine, back)), (1, (ahead,))):
        copies[2 + place].wait()

        def turn(group, carry, place=place, outs=outs):
            here = pl.ds(group * 8, 8)
            turned = pltpu.einshape("abc->bac", block[place, :, here, :])
            for out in outs:
                out[here] = turned
            return carry

        lax.fori_loop(0, rows // 8, turn, 0)
        first[place] = outs[0][:REACH]
        last[place] = outs[0][rows - REACH : rows]


def copy_rows(source, first, out, start, count):
    def body(y, size):
        for j in range(size):
            out[start + y + j] = source[first + y + j]

    row_blocks(0, count, body, 16)


def second_kernel(rows, ahead, own_before, own_behind, near2, out_a, out_b):
    del near2
    middle = rows // 2
    out_a[0] = own_before[1, REACH - 1]
    copy_rows(ahead, 0, out_a, 1, middle)
    copy_rows(ahead, middle, out_b, 0, rows - middle)
    out_b[rows - middle] = own_behind[1, 0]


def field_blocks(rows, messages):
    for plane, (name, *parts) in enumerate(FIELDS):
        count = rows // messages[name].shape[1]
        for kind, part in enumerate(parts):
            if part is not None:
                yield plane, kind, messages[name], part * count + (rows if name in BEHIND_ROWS else 0), count


def field_edges_kernel(rows, far3, beyond, own, pair, near3, first, last):
    messages = {"far3": far3, "beyond": beyond, "own": own, "pair": pair, "near3": near3}
    for place, (_, _, message, start, count) in enumerate(field_blocks(rows, messages)):
        first[place] = message[start, :MARGIN]
        last[place] = message[start + count - 1, message.shape[1] - MARGIN :]


def edges_kernel(rows, near1a, near1b, near2, far1, inverse, first, last):
    del inverse
    for (_, place, number), (head, start), (tail, stop) in zip(
        BESIDE, ((near1a, 1), (near2, 0), (far1, 0)), ((near1b, rows // 2), (near2, rows), (far1, rows))
    ):
        first[place : place + number] = head[start : start + number]
        last[place : place + number] = tail[stop - number : stop]


def couplings_kernel(
    rows, far3, beyond, own, pair, near3, before, behind, inverse, sx, sy, sz, root, coef, inner, masked
):
    messages = {"far3": far3, "beyond": beyond, "own": own, "pair": pair, "near3": near3}
    for place, (plane, kind, message, start, count) in enumerate(field_blocks(rows, messages)):
        out = (coef, inner)[kind]
        size = message.shape[1]
        for block in range(count):
            out[plane, MARGIN + block * size : MARGIN + (block + 1) * size] = message[start + block]
        out[plane, :MARGIN] = before[place]
        out[plane, MARGIN + rows :] = behind[place]
    make_operator(coef, inner, inverse, sx, sy, sz, root, masked)


def make_operator(coef, inner, inverse, sx, sy, sz, root, masked):
    planes, height, nx = inverse.shape
    lane = lax.broadcasted_iota(jnp.int32, (height, nx), 1)
    inside = lane < nx - 1

    def one_plane(plane, carry):
        here = coef[plane + 1]
        flag = inner[plane + 1]
        right = jnp.where(inside, pltpu.roll(here, nx - 1, 1), 0.0)
        left = jnp.where(lane > 0, pltpu.roll(here, 1, 1), 0.0)
        behind, before = pltpu.roll(here, height - 1, 0), pltpu.roll(here, 1, 0)
        along_x, along_y = face_of(here, right), face_of(here, behind)
        along_z = face_of(here, coef[plane + 2])
        total = along_x + jnp.where(left > 0.0, pltpu.roll(along_x, 1, 1), here)
        total += along_y + jnp.where(before > 0.0, pltpu.roll(along_y, 1, 0), here)
        total += along_z + face_of(here, coef[plane])
        diagonal = flag * total + (1.0 - flag)
        square = jnp.sqrt(diagonal)
        reciprocal = 1.0 / square
        root[plane] = square
        inverse[plane] = reciprocal
        scale = flag * reciprocal
        masked[plane] = scale
        sx[plane] = jnp.where(inside, scale * along_x * pltpu.roll(scale, nx - 1, 1), 0.0)
        sy[plane] = scale * along_y * pltpu.roll(scale, height - 1, 0)
        sz[plane] = scale * along_z
        return carry

    lax.fori_loop(0, planes, one_plane, 0)

    def next_plane(plane, carry):
        sz[plane] = sz[plane] * masked[plane + 1]
        return carry

    lax.fori_loop(0, planes - 1, next_plane, 0)


def cell_row(ref, plane, y):
    return ref[plane, pl.ds(y + (MARGIN - REACH), 1), :]


def row_blocks(start, stop, body, size):
    blocks = -(-(stop - start) // size)
    size = -(-(stop - start) // blocks)

    def step(block, carry):
        body(jnp.minimum(start + block * size, stop - size), size)
        return carry

    lax.fori_loop(0, blocks, step, 0)


def apply_rows(operator, plane, start, before, here, after, size):
    sx, sy, sz = operator
    ref, index = here
    out = []
    last, center = ref[index, start - 1], ref[index, start]
    below = cell_row(sy, plane, start - 1)
    width = center.shape[-1]
    for j in range(size):
        y = start + j
        following = ref[index, y + 1]
        above = cell_row(sy, plane, y)
        ahead = cell_row(sx, plane, y)
        total = ahead * pltpu.roll(center, width - 1, 1) + pltpu.roll(ahead * center, 1, 1)
        total += above * following + below * last
        total += cell_row(sz, plane, y) * after[0][after[1], y]
        total += cell_row(sz, plane - 1, y) * before[0][before[1], y]
        out.append(total)
        last, center, below = center, following, above
    return out


def spread(plane, depth=2):
    return max(REACH - plane, plane - (REACH + depth - 1), 0)


def scale_rows(plane, source, first, dst, start, count, inverse):
    out, place = dst

    def body(j, size):
        for i in range(size):
            out[place, start + j + i] = source[first + j + i] * cell_row(inverse, plane, start + j + i)

    if count < 8:
        body(0, count)
    else:
        row_blocks(0, count, body, 16)


def apply_plane(rows, power, plane, operator, fields):
    reach = REACH - power - spread(plane)
    src = [fields[power - 1, plane + offset] for offset in (-1, 0, 1)]
    out, place = fields[power, plane]

    def body(y, size):
        for j, values in enumerate(apply_rows(operator, plane, y, *src, size)):
            out[place, y + j] = values

    row_blocks(REACH - reach, REACH + rows + reach, body, 34)


def halves(blocks):
    stack = jnp.concatenate(blocks, axis=0)
    high = stack.astype(bf16)
    low = (stack - high.astype(f32)).astype(bf16)
    return jnp.concatenate([high, low], axis=0)


def inner_products(left, right):
    return lax.dot_general(left, right, (((1,), (1,)), ((), ())), preferred_element_type=f32)


def whole(gram, left, right):
    gram = gram[:left] + gram[left : 2 * left]
    return gram[:, :right] + gram[:, right : 2 * right]


def early_kernel(
    rows, far3, far1, mine, ahead, own_before, own_behind, near1a, near1b, near2, near3, before, behind,
    inverse, sx, sy, sz,
    u0_out, u1_out, u2_out, split, moments, u0, u1,
):
    operator = (sx, sy, sz)
    fields = {(0, plane): (u0_out, index) for index, plane in enumerate((0, 2, 3))}
    fields.update({(0, plane): (u0, plane - 4) for plane in range(4, 8)})
    fields.update({(1, 3): (u1_out, 0), (1, 4): (u1_out, 1), (1, 5): (u1, 0), (1, 6): (u1, 1)})
    fields.update({(2, 4): (u2_out, 0), (2, 5): (u2_out, 1)})
    first, last = REACH, REACH + rows
    for plane, source in ((0, far3), (2, far1), (3, mine), (4, ahead), (6, near2), (7, near3)):
        scale_rows(plane, source, 0, fields[0, plane], first, rows, inverse)
    middle = rows // 2
    scale_rows(5, near1a, 1, fields[0, 5], first, middle, inverse)
    scale_rows(5, near1b, 0, fields[0, 5], first + middle, rows - middle, inverse)
    for plane in (3, 4):
        scale_rows(plane, own_before.at[plane - 3], 0, fields[0, plane], 0, REACH, inverse)
        scale_rows(plane, own_behind.at[plane - 3], 0, fields[0, plane], last, REACH, inverse)
    for plane, place, count in BESIDE:
        scale_rows(plane, before, place, fields[0, plane], first - count, count, inverse)
        scale_rows(plane, behind, place, fields[0, plane], last, count, inverse)
    for power, plane in ((1, 3), (1, 4), (1, 5), (1, 6), (2, 4), (2, 5)):
        apply_plane(rows, power, plane, operator, fields)

    rhs = u0.shape[2]
    gram = jnp.zeros((4 * rhs, 4 * rhs), f32)
    for plane in range(2):

        def gram_rows(block, total, plane=plane):
            for group in range(4):
                parts = []
                for j in range(4):
                    y = block * 16 + group * 4 + j
                    sources = [fields[power, plane + REACH] for power in range(2)]
                    both = halves([ref[index, y + REACH] for ref, index in sources])
                    split[plane, y] = both
                    parts.append(both)
                wide = jnp.concatenate(parts, axis=1)
                total = total + inner_products(wide, wide)
            return total

        gram = lax.fori_loop(0, rows // 16, gram_rows, gram)
    gram = whole(gram, 2 * rhs, 2 * rhs)
    moments[:, : 2 * rhs] = gram[:rhs]
    moments[:, 2 * rhs : 3 * rhs] = gram[rhs:, rhs:]


def late_kernel(
    rows, far2a, far2b, u0_in, u1_in, u2_in, moments_in, inverse, sx, sy, sz, moments, split, u0, u1, u2
):
    operator = (sx, sy, sz)
    fields = {(0, plane): (u0_in, index) for index, plane in enumerate((0, 2, 3))}
    fields[0, LATE] = (u0, 0)
    fields.update({(1, 1): (u1, 0), (1, 2): (u1, 1), (1, 3): (u1_in, 0), (1, 4): (u1_in, 1)})
    fields.update({(2, 2): (u2, 0), (2, 3): (u2, 1), (2, 4): (u2_in, 0), (2, 5): (u2_in, 1)})
    first, last = REACH, REACH + rows
    scale_rows(LATE, far2a, 0, fields[0, LATE], first - 1, far2a.shape[0], inverse)
    scale_rows(LATE, far2b, 0, fields[0, LATE], last + 1 - far2b.shape[0], far2b.shape[0], inverse)
    for power, plane in ((1, 1), (1, 2), (2, 2), (2, 3)):
        apply_plane(rows, power, plane, operator, fields)

    rhs = u0.shape[2]
    gram = jnp.zeros((6 * rhs, 2 * rhs), f32)
    for plane in range(2):
        level = plane + REACH

        def gram_rows(block, total, plane=plane, level=level):
            start = block * 16
            y = start + REACH
            last = apply_rows(operator, level, y, *[fields[2, level + offset] for offset in (-1, 0, 1)], 16)
            for group in range(4):
                left, right = [], []
                for j in range(group * 4, group * 4 + 4):
                    ref, index = fields[2, level]
                    both = halves([ref[index, y + j], last[j]])
                    split[plane, start + j] = both
                    left.append(jnp.concatenate([halves([u1_in[plane, y + j]]), both], axis=0))
                    right.append(jnp.concatenate([both[:rhs], both[2 * rhs : 3 * rhs]], axis=0))
                total = total + inner_products(jnp.concatenate(left, axis=1), jnp.concatenate(right, axis=1))
            return total

        gram = lax.fori_loop(0, rows // 16, gram_rows, gram)
    gram = gram[:, :rhs] + gram[:, rhs:]
    blocks = [gram[part * rhs : (part + 1) * rhs] for part in range(6)]
    moments[:, : 3 * rhs] = moments_in[:, : 3 * rhs]
    moments[:, 3 * rhs : 4 * rhs] = blocks[0] + blocks[1]
    moments[:, 4 * rhs : 5 * rhs] = blocks[2] + blocks[4]
    moments[:, 5 * rhs : 6 * rhs] = blocks[3] + blocks[5]
    moments[:, 6 * rhs :] = jnp.zeros((rhs, moments.shape[1] - 6 * rhs), f32)


def inverse_of_pair(a, b, c, d):
    scale = 1.0 / (a * d - b * c)
    return d * scale, -b * scale, -c * scale, a * scale


def times(p, q):
    a, b, c, d = p
    e, f, g, h = q
    return a * e + b * g, a * f + b * h, c * e + d * g, c * f + d * h


def inverse_of_four(m):
    p, q = (m[0][0], m[0][1], m[1][0], m[1][1]), (m[0][2], m[0][3], m[1][2], m[1][3])
    r, s = (m[2][0], m[2][1], m[3][0], m[3][1]), (m[2][2], m[2][3], m[3][2], m[3][3])
    inner = inverse_of_pair(*p)
    right, left = times(inner, q), times(r, inner)
    outer = inverse_of_pair(*[x - y for x, y in zip(s, times(r, right))])
    lower = [-x for x in times(outer, left)]
    upper = [-x for x in times(right, outer)]
    corner = [x - y for x, y in zip(inner, times(right, lower))]
    return (
        (corner[0], corner[1], upper[0], upper[1]),
        (corner[2], corner[3], upper[2], upper[3]),
        (lower[0], lower[1], outer[0], outer[1]),
        (lower[2], lower[3], outer[2], outer[3]),
    )


def eliminate(stacked, size):
    tiles, height, width = stacked.shape
    lane = lax.broadcasted_iota(jnp.int32, (height, width), 1)

    def everywhere(row):
        return jnp.broadcast_to(row, (height, width))

    for k in range(0, size, 4):
        if k and k % height == 0:
            stacked = stacked[1:]
        at = k % height
        rows = [everywhere(stacked[0, at + i : at + i + 1]) for i in range(4)]
        columns = [jnp.broadcast_to(stacked[:, :, k + i : k + i + 1], stacked.shape) for i in range(4)]
        block = [[everywhere(columns[j][0, at + i : at + i + 1]) for j in range(4)] for i in range(4)]
        inverse = inverse_of_four(block)
        pivots = (lane >= k) & (lane < k + 4)
        result = jnp.where(pivots[None], 0.0, stacked)
        for i in range(4):
            mix = (inverse[i][0] * rows[0] + inverse[i][1] * rows[1]) + (
                inverse[i][2] * rows[2] + inverse[i][3] * rows[3]
            )
            for j in range(4):
                mix = jnp.where(lane == k + j, -inverse[i][j], mix)
            result = result - columns[i] * mix[None]
        stacked = result
    return stacked[1:]


def mixing(moments, rhs):
    width = moments.shape[1]
    lane = lax.broadcasted_iota(jnp.int32, (rhs, width), 1)
    row = lax.broadcasted_iota(jnp.int32, (rhs, width), 0)
    size = REACH * rhs
    rolled = [moments] + [pltpu.roll(moments, width - i * rhs, 1) for i in range(1, REACH + 1)]
    energy = [rolled[i] - rolled[i + 1] for i in range(REACH)]
    tiles = jnp.concatenate(energy + [moments], axis=0).reshape(-1, 8, width)
    solved = eliminate(tiles, size).reshape(rhs, width)
    solved = jnp.where(lane < size, solved, 0.0)
    residual = (row == lane).astype(f32) - (solved - pltpu.roll(solved, rhs, 1))
    return solved, residual


def outputs_kernel(odd, moments, split01, split23, inverse, root, iterate, iterate_out, residual_out, coefs):
    rhs, _, rows, nx = iterate.shape
    plane, block = pl.program_id(0), pl.program_id(1)

    @pl.when((plane == 0) & (block == 0))
    def _():
        solved, residual = mixing(moments[...], rhs)
        both = jnp.concatenate([solved[:, : 4 * rhs], residual[:, : 4 * rhs]], axis=0)
        high = both.astype(bf16).astype(f32)
        stacked = jnp.concatenate([high, both - high], axis=0)
        pair01, pair23 = stacked[:, : 2 * rhs], stacked[:, 2 * rhs :]
        coefs[...] = jnp.concatenate([pair01, pair01, pair23, pair23], axis=1).astype(bf16)

    def group_of_rows(group, carry):
        y = block * rows + group * 8
        wide = jnp.concatenate(
            [jnp.concatenate([split01[plane, y + j], split23[plane, y + j]], axis=0) for j in range(8)], axis=1
        )
        mixed = jnp.dot(coefs[...], wide, preferred_element_type=f32)
        mixed = mixed[: 2 * rhs] + mixed[2 * rhs :]
        by_row = jnp.stack([mixed[:, j * nx : (j + 1) * nx] for j in range(8)], axis=0)
        by_rhs = pltpu.einshape("abc->bac", by_row)
        cells = pl.ds(pl.multiple_of(y + MARGIN, 8), 8)
        here = pl.ds(group * 8, 8)
        iterate_out[:, 0, here] = iterate[:, 0, here] + by_rhs[:rhs] * inverse[plane + REACH, cells]
        residual_out[:, 0, here] = by_rhs[rhs:] * root[plane + REACH, cells]
        return carry

    lax.fori_loop(0, rows // 8, group_of_rows, 0)


def on_device(iterate, residual, labels, boundary):
    rhs, depth, rows, nx = residual.shape
    assert depth == 2 and REACH == 3 and rows % rhs == 0 and rhs % 8 == 0 and lax.axis_size("gz") % 2 == 0
    odd = (lax.axis_index("gz") % 2).astype(jnp.int32).reshape(1)
    vmem = pl.BlockSpec(memory_space=pltpu.VMEM)
    smem = pl.BlockSpec(memory_space=pltpu.SMEM)

    def array(*shape, dtype=f32):
        return jax.ShapeDtypeStruct(shape, dtype)

    def params(mib):
        return pltpu.CompilerParams(vmem_limit_bytes=mib * 2**20)

    anywhere = pl.BlockSpec(memory_space=pl.ANY)

    count = rows // rhs
    hbm = pl.BlockSpec(memory_space=pltpu.HBM)
    mine, ahead, back, cells, *edges = pl.pallas_call(
        prepare_kernel,
        out_shape=(array(rows, rhs, nx),)
        + (array(rows + 3 * count, rhs, nx),) * 2
        + (array(4 * count, rhs, nx),)
        + (array(depth, REACH, rhs, nx),) * 2,
        in_specs=[smem, hbm, hbm, hbm],
        out_specs=(vmem,) * 6,
        scratch_shapes=[
            pltpu.VMEM((depth, rhs, rows, nx), f32),
            pltpu.VMEM(labels.shape, jnp.int32),
            pltpu.VMEM(boundary.shape, jnp.int32),
            pltpu.SemaphoreType.DMA((2 + depth,)),
        ],
        compiler_params=params(55),
    )(odd, residual, labels, boundary)

    near2 = swapped(mine)
    far3 = relayed(ahead)
    near3 = relayed(back, back=True)
    own_before, own_behind = rows_beside(*edges)
    second = pl.pallas_call(
        partial(second_kernel, rows),
        out_shape=(array(rows // 2 + 1, rhs, nx), array(rows - rows // 2 + 1, rhs, nx)),
        in_specs=[vmem] * 3 + [anywhere],
        out_specs=(vmem,) * 2,
        compiler_params=params(8),
    )(ahead, own_before, own_behind, near2)
    near1a, near1b = [swapped(message) for message in second]
    pair = swapped(cells)
    far1 = relayed(near2)
    beyond = relayed(pair)
    far2a, far2b = relayed(near1a), relayed(near1b)

    number = sum(part is not None for _, *parts in FIELDS for part in parts)
    fields = (far3, beyond, cells, pair, near3)
    fields_beside = rows_beside(
        *pl.pallas_call(
            partial(field_edges_kernel, rows),
            out_shape=(array(number, MARGIN, nx),) * 2,
            in_specs=[vmem] * 5,
            out_specs=(vmem, vmem),
            compiler_params=params(8),
        )(*fields)
    )
    grid = (depth + 2 * REACH, rows + 2 * MARGIN, nx)
    inverse, sx, sy, sz, root = pl.pallas_call(
        partial(couplings_kernel, rows),
        out_shape=(array(*grid),) * 5,
        in_specs=[vmem] * 7,
        out_specs=(vmem,) * 5,
        scratch_shapes=[pltpu.VMEM((grid[0] + 2,) + grid[1:], f32)] * 2 + [pltpu.VMEM(grid, f32)],
        compiler_params=params(14),
    )(*fields, *fields_beside)

    before, behind = rows_beside(
        *pl.pallas_call(
            partial(edges_kernel, rows),
            out_shape=(array(EDGES, rhs, nx),) * 2,
            in_specs=[vmem] * 4 + [anywhere],
            out_specs=(vmem, vmem),
            compiler_params=params(8),
        )(near1a, near1b, near2, far1, inverse)
    )

    def planes(number):
        return (number, rows + 2 * REACH, rhs, nx)

    u0, u1, u2, split01, moments = pl.pallas_call(
        partial(early_kernel, rows),
        out_shape=tuple(array(*planes(number)) for number in (3, 2, 2))
        + (array(depth, rows, 4 * rhs, nx, dtype=bf16), array(rhs, 128)),
        in_specs=[vmem] * 16,
        out_specs=(vmem,) * 5,
        scratch_shapes=[pltpu.VMEM(planes(number), f32) for number in (4, 2)],
        compiler_params=params(24),
    )(
        far3, far1, mine, ahead, own_before, own_behind, near1a, near1b, near2, near3, before, behind,
        inverse, sx, sy, sz,
    )

    moments, split23 = pl.pallas_call(
        partial(late_kernel, rows),
        out_shape=(array(rhs, 128), array(depth, rows, 4 * rhs, nx, dtype=bf16)),
        in_specs=[vmem] * 10,
        out_specs=(vmem, vmem),
        scratch_shapes=[pltpu.VMEM(planes(number), f32) for number in (1, 2, 2)],
        compiler_params=params(20),
    )(far2a, far2b, u0, u1, u2, moments, inverse, sx, sy, sz)

    moments = all_sum(moments, ("gy", "gz"))

    tile = math.gcd(rows, 32)
    plane_rows = pl.BlockSpec((rhs, 1, tile, nx), lambda z, y, odd: (0, jnp.bitwise_xor(z, odd[0]), y, 0))
    return pl.pallas_call(
        outputs_kernel,
        out_shape=(array(*iterate.shape), array(*residual.shape)),
        grid_spec=pltpu.PrefetchScalarGridSpec(
            num_scalar_prefetch=1,
            grid=(depth, rows // tile),
            in_specs=[vmem] * 5 + [plane_rows],
            out_specs=(plane_rows, plane_rows),
            scratch_shapes=[pltpu.VMEM((4 * rhs, 8 * rhs), bf16)],
        ),
        compiler_params=params(16),
    )(odd, moments, split01, split23, inverse, root, iterate)


def solution(mesh):
    placed = (
        P(None, ("regions", "gz"), "gy", None),
        P(None, ("regions", "gz"), "gy", None),
        P(("regions", "gz"), "gy", None),
        P(("regions", "gz"), "gy", None),
    )
    return jax.shard_map(
        on_device,
        mesh=mesh,
        in_specs=placed,
        out_specs=(P(None, ("regions", "gz"), "gy", None), P(None, ("regions", "gz"), "gy", None)),
        check_vma=False,
    )
```

```python
import math
from functools import partial

import jax
import jax.numpy as jnp
from jax import lax
from jax.experimental import pallas as pl
from jax.experimental.pallas import tpu as pltpu
from jax.sharding import PartitionSpec as P

NCLASS = 8
ITERS = 3
REACH = ITERS

contrast_log = 4.0 * math.log(10.0)
highest = lax.Precision.HIGHEST
f32 = jnp.float32
bf16 = jnp.bfloat16


def moved(block, axis, pairs):
    return lax.ppermute(block, axis, pairs)


def shifted(block, axis, step):
    count = lax.axis_size(axis)
    return moved(block, axis, [(i, i + step) for i in range(count) if 0 <= i + step < count])


def swapped(block):
    return moved(block, "gz", [(i, i ^ 1) for i in range(lax.axis_size("gz"))])


def relayed(block, back=False):
    count = lax.axis_size("gz")
    steps = [(i, i + 2 - 4 * (i % 2)) for i in range(count)]
    pairs = [(i, j) for i, j in steps if 0 <= j < count]
    return moved(block, "gz", [(j, i) for i, j in pairs] if back else pairs)


def rows_beside(before, after):
    count = lax.axis_size("gy")
    if count != 2:
        return shifted(after, "gy", 1), shifted(before, "gy", -1)
    second = lax.axis_index("gy") == 1
    other = moved(jnp.where(second, before, after), "gy", [(0, 1), (1, 0)])
    zero = jnp.zeros_like(other)
    return jnp.where(second, other, zero), jnp.where(second, zero, other)


def face_of(center, beside):
    return jnp.where(beside > 0.0, 2.0 * center * beside / (center + beside), center)


LATE = 1
BESIDE = ((5, 0, 2), (6, 2, 1), (2, 3, 2))
EDGES = 5
FIELDS = (
    ("far3", 0, None), ("far3", 1, 2), ("far1", 1, 3), ("far1", 0, 2), ("mine", 0, 2),
    ("mine", 1, 3), ("near2", 1, 3), ("near2", 0, 2), ("near3", 0, 2), ("near3", 1, None),
)
MARGIN = 8


def turn_plane(block, out):
    def turn(group, carry):
        here = pl.ds(group * 8, 8)
        out[here] = pltpu.einshape("abc->bac", block[:, here, :])
        return carry

    lax.fori_loop(0, block.shape[1] // 8, turn, 0)


def far_kernel(odd, residual, labels, boundary, mine, first, last, block, label_cells, boundary_cells, arrived):
    rhs, depth, rows, nx = residual.shape
    copies = [
        pltpu.make_async_copy(labels, label_cells, arrived.at[0]),
        pltpu.make_async_copy(boundary, boundary_cells, arrived.at[1]),
        pltpu.make_async_copy(residual.at[:, odd[0]], block, arrived.at[2]),
    ]
    for copy in copies:
        copy.start()
    for copy in copies[:2]:
        copy.wait()
    count = rows // rhs
    for place in range(depth):
        plane = jnp.bitwise_xor(place, odd[0])
        for part in range(count):
            cells = pl.ds(part * rhs, rhs)
            mine[rows + place * count + part] = jnp.exp(
                label_cells[plane, cells, :].astype(f32) * (contrast_log / (NCLASS - 1))
            )
            mine[rows + (2 + place) * count + part] = (1 - boundary_cells[plane, cells, :]).astype(f32)
    copies[2].wait()
    turn_plane(block, mine)
    first[...] = mine[:REACH]
    last[...] = mine[rows - REACH : rows]


def near_kernel(odd, residual, mine, ahead, first, last, block, arrived):
    rhs, _, rows, _ = residual.shape
    copy = pltpu.make_async_copy(residual.at[:, 1 - odd[0]], block, arrived)
    copy.start()
    count = rows // rhs
    for part in range(2 * count):
        ahead[rows + part] = mine[rows + part]
    for part in range(count):
        ahead[rows + 2 * count + part] = mine[rows + 3 * count + part]
    copy.wait()
    turn_plane(block, ahead)
    first[...] = ahead[:REACH]
    last[...] = ahead[rows - REACH : rows]


def second_kernel(rows, ahead, own_before, own_behind, near2, far3, out):
    del near2, far3

    def copy_rows(y, size):
        for j in range(size):
            out[y + j] = ahead[y + j]

    row_blocks(0, rows, copy_rows, 16)
    out[rows] = own_before[1, REACH - 1]
    out[rows + 1] = own_behind[1, 0]


def edges_kernel(rows, near1, near2, far1, far3, near3, mine, first, last):
    messages = {"near2": near2, "far1": far1, "far3": far3, "near3": near3, "mine": mine}
    rhs = mine.shape[1]
    count = rows // rhs
    for (_, place, number), source in zip(BESIDE, (near1, near2, far1)):
        first[place : place + number] = source[:number]
        last[place : place + number] = source[rows - number : rows]
    place = EDGES
    for name, *parts in FIELDS:
        for part in parts:
            if part is not None:
                start = rows + part * count
                first[place, :MARGIN] = messages[name][start, :MARGIN]
                last[place, :MARGIN] = messages[name][start + count - 1, rhs - MARGIN :]
                place += 1
                first[place - 1, MARGIN:] = jnp.zeros_like(first[place - 1, MARGIN:])
                last[place - 1, MARGIN:] = jnp.zeros_like(last[place - 1, MARGIN:])


def fill_cells(rows, messages, before, behind, coef, inner):
    place = EDGES
    for plane, (name, *parts) in enumerate(FIELDS):
        for part, out in zip(parts, (coef, inner)):
            if part is None:
                continue
            rhs = messages[name].shape[1]
            count = rows // rhs
            for block in range(count):
                out[plane, MARGIN + block * rhs : MARGIN + (block + 1) * rhs] = messages[name][
                    rows + part * count + block
                ]
            out[plane, :MARGIN] = before[place, :MARGIN]
            out[plane, MARGIN + rows :] = behind[place, :MARGIN]
            place += 1


def make_operator(coef, inner, inverse, sx, sy, sz, root, masked):
    planes, height, nx = inverse.shape
    lane = lax.broadcasted_iota(jnp.int32, (height, nx), 1)
    inside = lane < nx - 1

    def one_plane(plane, carry):
        here = coef[plane + 1]
        flag = inner[plane + 1]
        right = jnp.where(inside, pltpu.roll(here, nx - 1, 1), 0.0)
        left = jnp.where(lane > 0, pltpu.roll(here, 1, 1), 0.0)
        behind, before = pltpu.roll(here, height - 1, 0), pltpu.roll(here, 1, 0)
        along_x, along_y = face_of(here, right), face_of(here, behind)
        along_z = face_of(here, coef[plane + 2])
        total = along_x + jnp.where(left > 0.0, pltpu.roll(along_x, 1, 1), here)
        total += along_y + jnp.where(before > 0.0, pltpu.roll(along_y, 1, 0), here)
        total += along_z + face_of(here, coef[plane])
        diagonal = flag * total + (1.0 - flag)
        square = jnp.sqrt(diagonal)
        reciprocal = 1.0 / square
        root[plane] = square
        inverse[plane] = reciprocal
        scale = flag * reciprocal
        masked[plane] = scale
        sx[plane] = jnp.where(inside, scale * along_x * pltpu.roll(scale, nx - 1, 1), 0.0)
        sy[plane] = scale * along_y * pltpu.roll(scale, height - 1, 0)
        sz[plane] = scale * along_z
        return carry

    lax.fori_loop(0, planes, one_plane, 0)

    def next_plane(plane, carry):
        sz[plane] = sz[plane] * masked[plane + 1]
        return carry

    lax.fori_loop(0, planes - 1, next_plane, 0)


def cell_row(ref, plane, y):
    return ref[plane, pl.ds(y + (MARGIN - REACH), 1), :]


def row_blocks(start, stop, body, size):
    blocks = -(-(stop - start) // size)
    size = -(-(stop - start) // blocks)

    def step(block, carry):
        body(jnp.minimum(start + block * size, stop - size), size)
        return carry

    lax.fori_loop(0, blocks, step, 0)


def apply_rows(operator, plane, start, before, here, after, size):
    sx, sy, sz = operator
    ref, index = here
    out = []
    last, center = ref[index, start - 1], ref[index, start]
    below = cell_row(sy, plane, start - 1)
    width = center.shape[-1]
    for j in range(size):
        y = start + j
        following = ref[index, y + 1]
        above = cell_row(sy, plane, y)
        ahead = cell_row(sx, plane, y)
        total = ahead * pltpu.roll(center, width - 1, 1) + pltpu.roll(ahead * center, 1, 1)
        total += above * following + below * last
        total += cell_row(sz, plane, y) * after[0][after[1], y]
        total += cell_row(sz, plane - 1, y) * before[0][before[1], y]
        out.append(total)
        last, center, below = center, following, above
    return out


def spread(plane, depth=2):
    return max(REACH - plane, plane - (REACH + depth - 1), 0)


def scale_rows(plane, source, first, dst, start, count, inverse):
    out, place = dst

    def body(j, size):
        for i in range(size):
            out[place, start + j + i] = source[first + j + i] * cell_row(inverse, plane, start + j + i)

    if count < 8:
        body(0, count)
    else:
        row_blocks(0, count, body, 16)


def apply_plane(rows, power, plane, operator, fields):
    reach = REACH - power - spread(plane)
    src = [fields[power - 1, plane + offset] for offset in (-1, 0, 1)]
    out, place = fields[power, plane]

    def body(y, size):
        for j, values in enumerate(apply_rows(operator, plane, y, *src, size)):
            out[place, y + j] = values

    row_blocks(REACH - reach, REACH + rows + reach, body, 34)


def halves(blocks):
    stack = jnp.concatenate(blocks, axis=0)
    high = stack.astype(bf16)
    low = (stack - high.astype(f32)).astype(bf16)
    return jnp.concatenate([high, low], axis=0)


def inner_products(left, right):
    return lax.dot_general(left, right, (((1,), (1,)), ((), ())), preferred_element_type=f32)


def whole(gram, left, right):
    gram = gram[:left] + gram[left : 2 * left]
    return gram[:, :right] + gram[:, right : 2 * right]


def early_kernel(
    rows, far3, far1, mine, ahead, own_before, own_behind, near1, near2, near3, before, behind,
    inverse, sx, sy, sz, root, u0_out, u1_out, u2_out, split, moments, u0, u1, coef, inner, masked,
):
    messages = {"near2": near2, "far1": far1, "far3": far3, "near3": near3, "mine": mine}
    fill_cells(rows, messages, before, behind, coef, inner)
    make_operator(coef, inner, inverse, sx, sy, sz, root, masked)
    operator = (sx, sy, sz)
    fields = {(0, plane): (u0_out, index) for index, plane in enumerate((0, 2, 3))}
    fields.update({(0, plane): (u0, plane - 4) for plane in range(4, 8)})
    fields.update({(1, 3): (u1_out, 0), (1, 4): (u1_out, 1), (1, 5): (u1, 0), (1, 6): (u1, 1)})
    fields.update({(2, 4): (u2_out, 0), (2, 5): (u2_out, 1)})
    first, last = REACH, REACH + rows
    for plane, source in ((0, far3), (2, far1), (3, mine), (4, ahead), (5, near1), (6, near2), (7, near3)):
        scale_rows(plane, source, 0, fields[0, plane], first, rows, inverse)
    for plane in (3, 4):
        scale_rows(plane, own_before.at[plane - 3], 0, fields[0, plane], 0, REACH, inverse)
        scale_rows(plane, own_behind.at[plane - 3], 0, fields[0, plane], last, REACH, inverse)
    for plane, place, count in BESIDE:
        scale_rows(plane, before, place, fields[0, plane], first - count, count, inverse)
        scale_rows(plane, behind, place, fields[0, plane], last, count, inverse)
    for power, plane in ((1, 3), (1, 4), (1, 5), (1, 6), (2, 4), (2, 5)):
        apply_plane(rows, power, plane, operator, fields)

    rhs = u0.shape[2]
    gram = jnp.zeros((4 * rhs, 4 * rhs), f32)
    for plane in range(2):

        def gram_rows(block, total, plane=plane):
            for group in range(4):
                parts = []
                for j in range(4):
                    y = block * 16 + group * 4 + j
                    sources = [fields[power, plane + REACH] for power in range(2)]
                    both = halves([ref[index, y + REACH] for ref, index in sources])
                    split[plane, y] = both
                    parts.append(both)
                wide = jnp.concatenate(parts, axis=1)
                total = total + inner_products(wide, wide)
            return total

        gram = lax.fori_loop(0, rows // 16, gram_rows, gram)
    gram = whole(gram, 2 * rhs, 2 * rhs)
    moments[:, : 2 * rhs] = gram[:rhs]
    moments[:, 2 * rhs : 3 * rhs] = gram[rhs:, rhs:]


def late_kernel(
    rows, far2, u0_in, u1_in, u2_in, moments_in, inverse, sx, sy, sz, moments, split, u0, u1, u2
):
    operator = (sx, sy, sz)
    fields = {(0, plane): (u0_in, index) for index, plane in enumerate((0, 2, 3))}
    fields[0, LATE] = (u0, 0)
    fields.update({(1, 1): (u1, 0), (1, 2): (u1, 1), (1, 3): (u1_in, 0), (1, 4): (u1_in, 1)})
    fields.update({(2, 2): (u2, 0), (2, 3): (u2, 1), (2, 4): (u2_in, 0), (2, 5): (u2_in, 1)})
    first, last = REACH, REACH + rows
    for place, start, count in ((0, first, rows), (rows, first - 1, 1), (rows + 1, last, 1)):
        scale_rows(LATE, far2, place, fields[0, LATE], start, count, inverse)
    for power, plane in ((1, 1), (1, 2), (2, 2), (2, 3)):
        apply_plane(rows, power, plane, operator, fields)

    rhs = u0.shape[2]
    gram = jnp.zeros((6 * rhs, 2 * rhs), f32)
    for plane in range(2):
        level = plane + REACH

        def gram_rows(block, total, plane=plane, level=level):
            start = block * 16
            y = start + REACH
            last = apply_rows(operator, level, y, *[fields[2, level + offset] for offset in (-1, 0, 1)], 16)
            for group in range(4):
                left, right = [], []
                for j in range(group * 4, group * 4 + 4):
                    ref, index = fields[2, level]
                    both = halves([ref[index, y + j], last[j]])
                    split[plane, start + j] = both
                    left.append(jnp.concatenate([halves([u1_in[plane, y + j]]), both], axis=0))
                    right.append(jnp.concatenate([both[:rhs], both[2 * rhs : 3 * rhs]], axis=0))
                total = total + inner_products(jnp.concatenate(left, axis=1), jnp.concatenate(right, axis=1))
            return total

        gram = lax.fori_loop(0, rows // 16, gram_rows, gram)
    gram = gram[:, :rhs] + gram[:, rhs:]
    blocks = [gram[part * rhs : (part + 1) * rhs] for part in range(6)]
    moments[:, : 3 * rhs] = moments_in[:, : 3 * rhs]
    moments[:, 3 * rhs : 4 * rhs] = blocks[0] + blocks[1]
    moments[:, 4 * rhs : 5 * rhs] = blocks[2] + blocks[4]
    moments[:, 5 * rhs : 6 * rhs] = blocks[3] + blocks[5]
    moments[:, 6 * rhs :] = jnp.zeros((rhs, moments.shape[1] - 6 * rhs), f32)


def inverse_of_pair(a, b, c, d):
    scale = 1.0 / (a * d - b * c)
    return d * scale, -b * scale, -c * scale, a * scale


def times(p, q):
    a, b, c, d = p
    e, f, g, h = q
    return a * e + b * g, a * f + b * h, c * e + d * g, c * f + d * h


def inverse_of_four(m):
    p, q = (m[0][0], m[0][1], m[1][0], m[1][1]), (m[0][2], m[0][3], m[1][2], m[1][3])
    r, s = (m[2][0], m[2][1], m[3][0], m[3][1]), (m[2][2], m[2][3], m[3][2], m[3][3])
    inner = inverse_of_pair(*p)
    right, left = times(inner, q), times(r, inner)
    outer = inverse_of_pair(*[x - y for x, y in zip(s, times(r, right))])
    lower = [-x for x in times(outer, left)]
    upper = [-x for x in times(right, outer)]
    corner = [x - y for x, y in zip(inner, times(right, lower))]
    return (
        (corner[0], corner[1], upper[0], upper[1]),
        (corner[2], corner[3], upper[2], upper[3]),
        (lower[0], lower[1], outer[0], outer[1]),
        (lower[2], lower[3], outer[2], outer[3]),
    )


def eliminate(stacked, size):
    tiles, height, width = stacked.shape
    lane = lax.broadcasted_iota(jnp.int32, (height, width), 1)

    def everywhere(row):
        return jnp.broadcast_to(row, (height, width))

    for k in range(0, size, 4):
        if k and k % height == 0:
            stacked = stacked[1:]
        at = k % height
        rows = [everywhere(stacked[0, at + i : at + i + 1]) for i in range(4)]
        columns = [jnp.broadcast_to(stacked[:, :, k + i : k + i + 1], stacked.shape) for i in range(4)]
        block = [[everywhere(columns[j][0, at + i : at + i + 1]) for j in range(4)] for i in range(4)]
        inverse = inverse_of_four(block)
        pivots = (lane >= k) & (lane < k + 4)
        result = jnp.where(pivots[None], 0.0, stacked)
        for i in range(4):
            mix = (inverse[i][0] * rows[0] + inverse[i][1] * rows[1]) + (
                inverse[i][2] * rows[2] + inverse[i][3] * rows[3]
            )
            for j in range(4):
                mix = jnp.where(lane == k + j, -inverse[i][j], mix)
            result = result - columns[i] * mix[None]
        stacked = result
    return stacked[1:]


def mixing(moments, rhs):
    width = moments.shape[1]
    lane = lax.broadcasted_iota(jnp.int32, (rhs, width), 1)
    row = lax.broadcasted_iota(jnp.int32, (rhs, width), 0)
    size = REACH * rhs
    rolled = [moments] + [pltpu.roll(moments, width - i * rhs, 1) for i in range(1, REACH + 1)]
    energy = [rolled[i] - rolled[i + 1] for i in range(REACH)]
    tiles = jnp.concatenate(energy + [moments], axis=0).reshape(-1, 8, width)
    solved = eliminate(tiles, size).reshape(rhs, width)
    solved = jnp.where(lane < size, solved, 0.0)
    residual = (row == lane).astype(f32) - (solved - pltpu.roll(solved, rhs, 1))
    return solved, residual


def outputs_kernel(odd, moments, split01, split23, inverse, root, iterate, iterate_out, residual_out, coefs):
    rhs, _, rows, nx = iterate.shape
    plane, block = pl.program_id(0), pl.program_id(1)

    @pl.when((plane == 0) & (block == 0))
    def _():
        solved, residual = mixing(moments[...], rhs)
        both = jnp.concatenate([solved[:, : 4 * rhs], residual[:, : 4 * rhs]], axis=0)
        high = both.astype(bf16).astype(f32)
        stacked = jnp.concatenate([high, both - high], axis=0)
        pair01, pair23 = stacked[:, : 2 * rhs], stacked[:, 2 * rhs :]
        coefs[...] = jnp.concatenate([pair01, pair01, pair23, pair23], axis=1).astype(bf16)

    def group_of_rows(group, carry):
        y = block * rows + group * 8
        wide = jnp.concatenate(
            [jnp.concatenate([split01[plane, y + j], split23[plane, y + j]], axis=0) for j in range(8)], axis=1
        )
        mixed = jnp.dot(coefs[...], wide, preferred_element_type=f32)
        mixed = mixed[: 2 * rhs] + mixed[2 * rhs :]
        by_row = jnp.stack([mixed[:, j * nx : (j + 1) * nx] for j in range(8)], axis=0)
        by_rhs = pltpu.einshape("abc->bac", by_row)
        cells = pl.ds(pl.multiple_of(y + MARGIN, 8), 8)
        here = pl.ds(group * 8, 8)
        iterate_out[:, 0, here] = iterate[:, 0, here] + by_rhs[:rhs] * inverse[plane + REACH, cells]
        residual_out[:, 0, here] = by_rhs[rhs:] * root[plane + REACH, cells]
        return carry

    lax.fori_loop(0, rows // 8, group_of_rows, 0)


def on_device(iterate, residual, labels, boundary):
    rhs, depth, rows, nx = residual.shape
    assert depth == 2 and REACH == 3 and rows % rhs == 0 and rhs % 8 == 0 and lax.axis_size("gz") % 2 == 0
    odd = (lax.axis_index("gz") % 2).astype(jnp.int32).reshape(1)
    vmem = pl.BlockSpec(memory_space=pltpu.VMEM)
    smem = pl.BlockSpec(memory_space=pltpu.SMEM)

    def array(*shape, dtype=f32):
        return jax.ShapeDtypeStruct(shape, dtype)

    def params(mib):
        return pltpu.CompilerParams(vmem_limit_bytes=mib * 2**20)

    anywhere = pl.BlockSpec(memory_space=pl.ANY)

    count = rows // rhs
    hbm = pl.BlockSpec(memory_space=pltpu.HBM)
    edge = (array(REACH, rhs, nx),) * 2
    plane_block = pltpu.VMEM((rhs, rows, nx), f32)
    mine, far_first, far_last = pl.pallas_call(
        far_kernel,
        out_shape=(array(rows + 4 * count, rhs, nx),) + edge,
        in_specs=[smem, hbm, hbm, hbm],
        out_specs=(vmem,) * 3,
        scratch_shapes=[
            plane_block,
            pltpu.VMEM(labels.shape, jnp.int32),
            pltpu.VMEM(boundary.shape, jnp.int32),
            pltpu.SemaphoreType.DMA((3,)),
        ],
        compiler_params=params(58),
    )(odd, residual, labels, boundary)
    ahead, near_first, near_last = pl.pallas_call(
        near_kernel,
        out_shape=(array(rows + 3 * count, rhs, nx),) + edge,
        in_specs=[smem, hbm, vmem],
        out_specs=(vmem,) * 3,
        scratch_shapes=[plane_block, pltpu.SemaphoreType.DMA],
        compiler_params=params(58),
    )(odd, residual, mine)
    edges = jnp.stack([far_first, near_first]), jnp.stack([far_last, near_last])

    near2 = swapped(mine)
    far3 = relayed(ahead)
    near3 = relayed(mine, back=True)
    own_before, own_behind = rows_beside(*edges)
    near1 = swapped(
        pl.pallas_call(
            partial(second_kernel, rows),
            out_shape=array(rows + 2, rhs, nx),
            in_specs=[vmem, vmem, vmem, anywhere, anywhere],
            out_specs=vmem,
            compiler_params=params(8),
        )(ahead, own_before, own_behind, near2, far3)
    )
    far1 = relayed(near2)
    far2 = relayed(near1)

    edges = EDGES + sum(part is not None for _, *parts in FIELDS for part in parts)
    before, behind = rows_beside(
        *pl.pallas_call(
            partial(edges_kernel, rows),
            out_shape=(array(edges, rhs, nx),) * 2,
            in_specs=[vmem] * 6,
            out_specs=(vmem, vmem),
            compiler_params=params(12),
        )(near1, near2, far1, far3, near3, mine)
    )

    def planes(number):
        return (number, rows + 2 * REACH, rhs, nx)

    cells = (depth + 2 * REACH, rows + 2 * MARGIN, nx)
    inverse, sx, sy, sz, root, u0, u1, u2, split01, moments = pl.pallas_call(
        partial(early_kernel, rows),
        out_shape=(array(*cells),) * 5
        + tuple(array(*planes(number)) for number in (3, 2, 2))
        + (array(depth, rows, 4 * rhs, nx, dtype=bf16), array(rhs, 128)),
        in_specs=[vmem] * 11,
        out_specs=(vmem,) * 10,
        scratch_shapes=[pltpu.VMEM(planes(number), f32) for number in (4, 2)]
        + [pltpu.VMEM((cells[0] + 2,) + cells[1:], f32)] * 2
        + [pltpu.VMEM(cells, f32)],
        compiler_params=params(24),
    )(far3, far1, mine, ahead, own_before, own_behind, near1, near2, near3, before, behind)

    moments, split23 = pl.pallas_call(
        partial(late_kernel, rows),
        out_shape=(array(rhs, 128), array(depth, rows, 4 * rhs, nx, dtype=bf16)),
        in_specs=[vmem] * 9,
        out_specs=(vmem, vmem),
        scratch_shapes=[pltpu.VMEM(planes(number), f32) for number in (1, 2, 2)],
        compiler_params=params(20),
    )(far2, u0, u1, u2, moments, inverse, sx, sy, sz)

    moments = jnp.sum(lax.all_gather(moments, ("gz", "gy")), axis=0)

    tile = math.gcd(rows, 32)
    plane_rows = pl.BlockSpec((rhs, 1, tile, nx), lambda z, y, odd: (0, jnp.bitwise_xor(z, odd[0]), y, 0))
    return pl.pallas_call(
        outputs_kernel,
        out_shape=(array(*iterate.shape), array(*residual.shape)),
        grid_spec=pltpu.PrefetchScalarGridSpec(
            num_scalar_prefetch=1,
            grid=(depth, rows // tile),
            in_specs=[vmem] * 5 + [plane_rows],
            out_specs=(plane_rows, plane_rows),
            scratch_shapes=[pltpu.VMEM((4 * rhs, 8 * rhs), bf16)],
        ),
        compiler_params=params(16),
    )(odd, moments, split01, split23, inverse, root, iterate)


def solution(mesh):
    placed = (
        P(None, ("regions", "gz"), "gy", None),
        P(None, ("regions", "gz"), "gy", None),
        P(("regions", "gz"), "gy", None),
        P(("regions", "gz"), "gy", None),
    )
    return jax.shard_map(
        on_device,
        mesh=mesh,
        in_specs=placed,
        out_specs=(P(None, ("regions", "gz"), "gy", None), P(None, ("regions", "gz"), "gy", None)),
        check_vma=False,
    )
```

```python
import math
from functools import partial

import jax
import jax.numpy as jnp
from jax import lax
from jax.experimental import pallas as pl
from jax.experimental.pallas import tpu as pltpu
from jax.sharding import PartitionSpec as P

NCLASS = 8
ITERS = 3
REACH = ITERS

contrast_log = 4.0 * math.log(10.0)
highest = lax.Precision.HIGHEST
f32 = jnp.float32
bf16 = jnp.bfloat16


def moved(block, axis, pairs):
    return lax.ppermute(block, axis, pairs)


def shifted(block, axis, step):
    count = lax.axis_size(axis)
    return moved(block, axis, [(i, i + step) for i in range(count) if 0 <= i + step < count])


def swapped(block):
    return moved(block, "gz", [(i, i ^ 1) for i in range(lax.axis_size("gz"))])


def relayed(block, back=False):
    count = lax.axis_size("gz")
    steps = [(i, i + 2 - 4 * (i % 2)) for i in range(count)]
    pairs = [(i, j) for i, j in steps if 0 <= j < count]
    return moved(block, "gz", [(j, i) for i, j in pairs] if back else pairs)


def rows_beside(before, after):
    count = lax.axis_size("gy")
    if count != 2:
        return shifted(after, "gy", 1), shifted(before, "gy", -1)
    second = lax.axis_index("gy") == 1
    other = moved(jnp.where(second, before, after), "gy", [(0, 1), (1, 0)])
    zero = jnp.zeros_like(other)
    return jnp.where(second, other, zero), jnp.where(second, zero, other)


def all_sum(values, axes):
    for axis in axes:
        count = lax.axis_size(axis)
        if count & (count - 1):
            values = lax.psum(values, axis)
            continue
        step = 1
        while step < count:
            values = values + lax.ppermute(values, axis, [(i, i ^ step) for i in range(count)])
            step *= 2
    return values


def face_of(center, beside):
    return jnp.where(beside > 0.0, 2.0 * center * beside / (center + beside), center)


LATE = 1
BESIDE = ((5, 0, 2), (6, 2, 1), (2, 3, 2))
EDGES = 5
FIELDS = (
    ("far3", 0, None), ("far3", 1, 2), ("far1", 1, 3), ("far1", 0, 2), ("mine", 0, 2),
    ("mine", 1, 3), ("near2", 1, 3), ("near2", 0, 2), ("near3", 0, 2), ("near3", 1, None),
)
MARGIN = 8


def turn_plane(block, out):
    def turn(group, carry):
        here = pl.ds(group * 8, 8)
        out[here] = pltpu.einshape("abc->bac", block[:, here, :])
        return carry

    lax.fori_loop(0, block.shape[1] // 8, turn, 0)


def far_kernel(odd, residual, labels, boundary, mine, first, last, block, label_cells, boundary_cells, arrived):
    rhs, depth, rows, nx = residual.shape
    copies = [
        pltpu.make_async_copy(labels, label_cells, arrived.at[0]),
        pltpu.make_async_copy(boundary, boundary_cells, arrived.at[1]),
        pltpu.make_async_copy(residual.at[:, odd[0]], block, arrived.at[2]),
    ]
    for copy in copies:
        copy.start()
    for copy in copies[:2]:
        copy.wait()
    count = rows // rhs
    for place in range(depth):
        plane = jnp.bitwise_xor(place, odd[0])
        for part in range(count):
            cells = pl.ds(part * rhs, rhs)
            mine[rows + place * count + part] = jnp.exp(
                label_cells[plane, cells, :].astype(f32) * (contrast_log / (NCLASS - 1))
            )
            mine[rows + (2 + place) * count + part] = (1 - boundary_cells[plane, cells, :]).astype(f32)
    copies[2].wait()
    turn_plane(block, mine)
    first[...] = mine[:REACH]
    last[...] = mine[rows - REACH : rows]


def near_kernel(odd, residual, mine, ahead, first, last, block, cells, arrived):
    rhs, _, rows, _ = residual.shape
    copies = [
        pltpu.make_async_copy(mine.at[pl.ds(rows, cells.shape[0])], cells, arrived.at[0]),
        pltpu.make_async_copy(residual.at[:, 1 - odd[0]], block, arrived.at[1]),
    ]
    for copy in copies:
        copy.start()
    copies[0].wait()
    count = rows // rhs
    for part in range(2 * count):
        ahead[rows + part] = cells[part]
    for part in range(count):
        ahead[rows + 2 * count + part] = cells[3 * count + part]
    copies[1].wait()
    turn_plane(block, ahead)
    first[...] = ahead[:REACH]
    last[...] = ahead[rows - REACH : rows]


def second_kernel(rows, ahead, own_before, own_behind, near2, far3, out):
    del near2, far3

    def copy_rows(y, size):
        for j in range(size):
            out[y + j] = ahead[y + j]

    row_blocks(0, rows, copy_rows, 16)
    out[rows] = own_before[1, REACH - 1]
    out[rows + 1] = own_behind[1, 0]


def edges_kernel(rows, near1, near2, far1, far3, near3, mine, first, last):
    messages = {"near2": near2, "far1": far1, "far3": far3, "near3": near3, "mine": mine}
    rhs = mine.shape[1]
    count = rows // rhs
    for (_, place, number), source in zip(BESIDE, (near1, near2, far1)):
        first[place : place + number] = source[:number]
        last[place : place + number] = source[rows - number : rows]
    place = EDGES
    for name, *parts in FIELDS:
        for part in parts:
            if part is not None:
                start = rows + part * count
                first[place, :MARGIN] = messages[name][start, :MARGIN]
                last[place, :MARGIN] = messages[name][start + count - 1, rhs - MARGIN :]
                place += 1
                first[place - 1, MARGIN:] = jnp.zeros_like(first[place - 1, MARGIN:])
                last[place - 1, MARGIN:] = jnp.zeros_like(last[place - 1, MARGIN:])


def fill_cells(rows, messages, before, behind, coef, inner):
    place = EDGES
    for plane, (name, *parts) in enumerate(FIELDS):
        for part, out in zip(parts, (coef, inner)):
            if part is None:
                continue
            rhs = messages[name].shape[1]
            count = rows // rhs
            for block in range(count):
                out[plane, MARGIN + block * rhs : MARGIN + (block + 1) * rhs] = messages[name][
                    rows + part * count + block
                ]
            out[plane, :MARGIN] = before[place, :MARGIN]
            out[plane, MARGIN + rows :] = behind[place, :MARGIN]
            place += 1


def make_operator(coef, inner, inverse, sx, sy, sz, root, masked):
    planes, height, nx = inverse.shape
    lane = lax.broadcasted_iota(jnp.int32, (height, nx), 1)
    inside = lane < nx - 1

    def one_plane(plane, carry):
        here = coef[plane + 1]
        flag = inner[plane + 1]
        right = jnp.where(inside, pltpu.roll(here, nx - 1, 1), 0.0)
        left = jnp.where(lane > 0, pltpu.roll(here, 1, 1), 0.0)
        behind, before = pltpu.roll(here, height - 1, 0), pltpu.roll(here, 1, 0)
        along_x, along_y = face_of(here, right), face_of(here, behind)
        along_z = face_of(here, coef[plane + 2])
        total = along_x + jnp.where(left > 0.0, pltpu.roll(along_x, 1, 1), here)
        total += along_y + jnp.where(before > 0.0, pltpu.roll(along_y, 1, 0), here)
        total += along_z + face_of(here, coef[plane])
        diagonal = flag * total + (1.0 - flag)
        square = jnp.sqrt(diagonal)
        reciprocal = 1.0 / square
        root[plane] = square
        inverse[plane] = reciprocal
        scale = flag * reciprocal
        masked[plane] = scale
        sx[plane] = jnp.where(inside, scale * along_x * pltpu.roll(scale, nx - 1, 1), 0.0)
        sy[plane] = scale * along_y * pltpu.roll(scale, height - 1, 0)
        sz[plane] = scale * along_z
        return carry

    lax.fori_loop(0, planes, one_plane, 0)

    def next_plane(plane, carry):
        sz[plane] = sz[plane] * masked[plane + 1]
        return carry

    lax.fori_loop(0, planes - 1, next_plane, 0)


def cell_row(ref, plane, y):
    return ref[plane, pl.ds(y + (MARGIN - REACH), 1), :]


def row_blocks(start, stop, body, size):
    blocks = -(-(stop - start) // size)
    size = -(-(stop - start) // blocks)

    def step(block, carry):
        body(jnp.minimum(start + block * size, stop - size), size)
        return carry

    lax.fori_loop(0, blocks, step, 0)


def apply_rows(operator, plane, start, before, here, after, size):
    sx, sy, sz = operator
    ref, index = here
    out = []
    last, center = ref[index, start - 1], ref[index, start]
    below = cell_row(sy, plane, start - 1)
    width = center.shape[-1]
    for j in range(size):
        y = start + j
        following = ref[index, y + 1]
        above = cell_row(sy, plane, y)
        ahead = cell_row(sx, plane, y)
        total = ahead * pltpu.roll(center, width - 1, 1) + pltpu.roll(ahead * center, 1, 1)
        total += above * following + below * last
        total += cell_row(sz, plane, y) * after[0][after[1], y]
        total += cell_row(sz, plane - 1, y) * before[0][before[1], y]
        out.append(total)
        last, center, below = center, following, above
    return out


def spread(plane, depth=2):
    return max(REACH - plane, plane - (REACH + depth - 1), 0)


def scale_rows(plane, source, first, dst, start, count, inverse):
    out, place = dst

    def body(j, size):
        for i in range(size):
            out[place, start + j + i] = source[first + j + i] * cell_row(inverse, plane, start + j + i)

    if count < 8:
        body(0, count)
    else:
        row_blocks(0, count, body, 16)


def apply_plane(rows, power, plane, operator, fields):
    reach = REACH - power - spread(plane)
    src = [fields[power - 1, plane + offset] for offset in (-1, 0, 1)]
    out, place = fields[power, plane]

    def body(y, size):
        for j, values in enumerate(apply_rows(operator, plane, y, *src, size)):
            out[place, y + j] = values

    row_blocks(REACH - reach, REACH + rows + reach, body, 34)


def halves(blocks):
    stack = jnp.concatenate(blocks, axis=0)
    high = stack.astype(bf16)
    low = (stack - high.astype(f32)).astype(bf16)
    return jnp.concatenate([high, low], axis=0)


def inner_products(left, right):
    return lax.dot_general(left, right, (((1,), (1,)), ((), ())), preferred_element_type=f32)


def whole(gram, left, right):
    gram = gram[:left] + gram[left : 2 * left]
    return gram[:, :right] + gram[:, right : 2 * right]


def early_kernel(
    rows, far3, far1, mine, ahead, own_before, own_behind, near1, near2, near3, before, behind,
    inverse, sx, sy, sz, root, u0_out, u1_out, u2_out, split, moments, u0, u1, coef, inner, masked,
):
    messages = {"near2": near2, "far1": far1, "far3": far3, "near3": near3, "mine": mine}
    fill_cells(rows, messages, before, behind, coef, inner)
    make_operator(coef, inner, inverse, sx, sy, sz, root, masked)
    operator = (sx, sy, sz)
    fields = {(0, plane): (u0_out, index) for index, plane in enumerate((0, 2, 3))}
    fields.update({(0, plane): (u0, plane - 4) for plane in range(4, 8)})
    fields.update({(1, 3): (u1_out, 0), (1, 4): (u1_out, 1), (1, 5): (u1, 0), (1, 6): (u1, 1)})
    fields.update({(2, 4): (u2_out, 0), (2, 5): (u2_out, 1)})
    first, last = REACH, REACH + rows
    for plane, source in ((0, far3), (2, far1), (3, mine), (4, ahead), (5, near1), (6, near2), (7, near3)):
        scale_rows(plane, source, 0, fields[0, plane], first, rows, inverse)
    for plane in (3, 4):
        scale_rows(plane, own_before.at[plane - 3], 0, fields[0, plane], 0, REACH, inverse)
        scale_rows(plane, own_behind.at[plane - 3], 0, fields[0, plane], last, REACH, inverse)
    for plane, place, count in BESIDE:
        scale_rows(plane, before, place, fields[0, plane], first - count, count, inverse)
        scale_rows(plane, behind, place, fields[0, plane], last, count, inverse)
    for power, plane in ((1, 3), (1, 4), (1, 5), (1, 6), (2, 4), (2, 5)):
        apply_plane(rows, power, plane, operator, fields)

    rhs = u0.shape[2]
    gram = jnp.zeros((4 * rhs, 4 * rhs), f32)
    for plane in range(2):

        def gram_rows(block, total, plane=plane):
            for group in range(4):
                parts = []
                for j in range(4):
                    y = block * 16 + group * 4 + j
                    sources = [fields[power, plane + REACH] for power in range(2)]
                    both = halves([ref[index, y + REACH] for ref, index in sources])
                    split[plane, y] = both
                    parts.append(both)
                wide = jnp.concatenate(parts, axis=1)
                total = total + inner_products(wide, wide)
            return total

        gram = lax.fori_loop(0, rows // 16, gram_rows, gram)
    gram = whole(gram, 2 * rhs, 2 * rhs)
    moments[:, : 2 * rhs] = gram[:rhs]
    moments[:, 2 * rhs : 3 * rhs] = gram[rhs:, rhs:]


def late_kernel(
    rows, far2, u0_in, u1_in, u2_in, moments_in, inverse, sx, sy, sz, moments, split, u0, u1, u2
):
    operator = (sx, sy, sz)
    fields = {(0, plane): (u0_in, index) for index, plane in enumerate((0, 2, 3))}
    fields[0, LATE] = (u0, 0)
    fields.update({(1, 1): (u1, 0), (1, 2): (u1, 1), (1, 3): (u1_in, 0), (1, 4): (u1_in, 1)})
    fields.update({(2, 2): (u2, 0), (2, 3): (u2, 1), (2, 4): (u2_in, 0), (2, 5): (u2_in, 1)})
    first, last = REACH, REACH + rows
    for place, start, count in ((0, first, rows), (rows, first - 1, 1), (rows + 1, last, 1)):
        scale_rows(LATE, far2, place, fields[0, LATE], start, count, inverse)
    for power, plane in ((1, 1), (1, 2), (2, 2), (2, 3)):
        apply_plane(rows, power, plane, operator, fields)

    rhs = u0.shape[2]
    gram = jnp.zeros((6 * rhs, 2 * rhs), f32)
    for plane in range(2):
        level = plane + REACH

        def gram_rows(block, total, plane=plane, level=level):
            start = block * 16
            y = start + REACH
            last = apply_rows(operator, level, y, *[fields[2, level + offset] for offset in (-1, 0, 1)], 16)
            for group in range(4):
                left, right = [], []
                for j in range(group * 4, group * 4 + 4):
                    ref, index = fields[2, level]
                    both = halves([ref[index, y + j], last[j]])
                    split[plane, start + j] = both
                    left.append(jnp.concatenate([halves([u1_in[plane, y + j]]), both], axis=0))
                    right.append(jnp.concatenate([both[:rhs], both[2 * rhs : 3 * rhs]], axis=0))
                total = total + inner_products(jnp.concatenate(left, axis=1), jnp.concatenate(right, axis=1))
            return total

        gram = lax.fori_loop(0, rows // 16, gram_rows, gram)
    gram = gram[:, :rhs] + gram[:, rhs:]
    blocks = [gram[part * rhs : (part + 1) * rhs] for part in range(6)]
    moments[:, : 3 * rhs] = moments_in[:, : 3 * rhs]
    moments[:, 3 * rhs : 4 * rhs] = blocks[0] + blocks[1]
    moments[:, 4 * rhs : 5 * rhs] = blocks[2] + blocks[4]
    moments[:, 5 * rhs : 6 * rhs] = blocks[3] + blocks[5]
    moments[:, 6 * rhs :] = jnp.zeros((rhs, moments.shape[1] - 6 * rhs), f32)


def inverse_of_pair(a, b, c, d):
    scale = 1.0 / (a * d - b * c)
    return d * scale, -b * scale, -c * scale, a * scale


def times(p, q):
    a, b, c, d = p
    e, f, g, h = q
    return a * e + b * g, a * f + b * h, c * e + d * g, c * f + d * h


def inverse_of_four(m):
    p, q = (m[0][0], m[0][1], m[1][0], m[1][1]), (m[0][2], m[0][3], m[1][2], m[1][3])
    r, s = (m[2][0], m[2][1], m[3][0], m[3][1]), (m[2][2], m[2][3], m[3][2], m[3][3])
    inner = inverse_of_pair(*p)
    right, left = times(inner, q), times(r, inner)
    outer = inverse_of_pair(*[x - y for x, y in zip(s, times(r, right))])
    lower = [-x for x in times(outer, left)]
    upper = [-x for x in times(right, outer)]
    corner = [x - y for x, y in zip(inner, times(right, lower))]
    return (
        (corner[0], corner[1], upper[0], upper[1]),
        (corner[2], corner[3], upper[2], upper[3]),
        (lower[0], lower[1], outer[0], outer[1]),
        (lower[2], lower[3], outer[2], outer[3]),
    )


def eliminate(stacked, size):
    tiles, height, width = stacked.shape
    lane = lax.broadcasted_iota(jnp.int32, (height, width), 1)

    def everywhere(row):
        return jnp.broadcast_to(row, (height, width))

    for k in range(0, size, 4):
        if k and k % height == 0:
            stacked = stacked[1:]
        at = k % height
        rows = [everywhere(stacked[0, at + i : at + i + 1]) for i in range(4)]
        columns = [jnp.broadcast_to(stacked[:, :, k + i : k + i + 1], stacked.shape) for i in range(4)]
        block = [[everywhere(columns[j][0, at + i : at + i + 1]) for j in range(4)] for i in range(4)]
        inverse = inverse_of_four(block)
        pivots = (lane >= k) & (lane < k + 4)
        result = jnp.where(pivots[None], 0.0, stacked)
        for i in range(4):
            mix = (inverse[i][0] * rows[0] + inverse[i][1] * rows[1]) + (
                inverse[i][2] * rows[2] + inverse[i][3] * rows[3]
            )
            for j in range(4):
                mix = jnp.where(lane == k + j, -inverse[i][j], mix)
            result = result - columns[i] * mix[None]
        stacked = result
    return stacked[1:]


def mixing(moments, rhs):
    width = moments.shape[1]
    lane = lax.broadcasted_iota(jnp.int32, (rhs, width), 1)
    row = lax.broadcasted_iota(jnp.int32, (rhs, width), 0)
    size = REACH * rhs
    rolled = [moments] + [pltpu.roll(moments, width - i * rhs, 1) for i in range(1, REACH + 1)]
    energy = [rolled[i] - rolled[i + 1] for i in range(REACH)]
    tiles = jnp.concatenate(energy + [moments], axis=0).reshape(-1, 8, width)
    solved = eliminate(tiles, size).reshape(rhs, width)
    solved = jnp.where(lane < size, solved, 0.0)
    residual = (row == lane).astype(f32) - (solved - pltpu.roll(solved, rhs, 1))
    return solved, residual


def outputs_kernel(odd, moments, split01, split23, inverse, root, iterate, iterate_out, residual_out, coefs):
    rhs, _, rows, nx = iterate.shape
    plane, block = pl.program_id(0), pl.program_id(1)

    @pl.when((plane == 0) & (block == 0))
    def _():
        solved, residual = mixing(moments[...], rhs)
        both = jnp.concatenate([solved[:, : 4 * rhs], residual[:, : 4 * rhs]], axis=0)
        high = both.astype(bf16).astype(f32)
        stacked = jnp.concatenate([high, both - high], axis=0)
        pair01, pair23 = stacked[:, : 2 * rhs], stacked[:, 2 * rhs :]
        coefs[...] = jnp.concatenate([pair01, pair01, pair23, pair23], axis=1).astype(bf16)

    def group_of_rows(group, carry):
        y = block * rows + group * 8
        wide = jnp.concatenate(
            [jnp.concatenate([split01[plane, y + j], split23[plane, y + j]], axis=0) for j in range(8)], axis=1
        )
        mixed = jnp.dot(coefs[...], wide, preferred_element_type=f32)
        mixed = mixed[: 2 * rhs] + mixed[2 * rhs :]
        by_row = jnp.stack([mixed[:, j * nx : (j + 1) * nx] for j in range(8)], axis=0)
        by_rhs = pltpu.einshape("abc->bac", by_row)
        cells = pl.ds(pl.multiple_of(y + MARGIN, 8), 8)
        here = pl.ds(group * 8, 8)
        iterate_out[:, 0, here] = iterate[:, 0, here] + by_rhs[:rhs] * inverse[plane + REACH, cells]
        residual_out[:, 0, here] = by_rhs[rhs:] * root[plane + REACH, cells]
        return carry

    lax.fori_loop(0, rows // 8, group_of_rows, 0, unroll=True)


def on_device(iterate, residual, labels, boundary):
    rhs, depth, rows, nx = residual.shape
    assert depth == 2 and REACH == 3 and rows % rhs == 0 and rhs % 8 == 0 and lax.axis_size("gz") % 2 == 0
    odd = (lax.axis_index("gz") % 2).astype(jnp.int32).reshape(1)
    vmem = pl.BlockSpec(memory_space=pltpu.VMEM)
    smem = pl.BlockSpec(memory_space=pltpu.SMEM)

    def array(*shape, dtype=f32):
        return jax.ShapeDtypeStruct(shape, dtype)

    def params(mib):
        return pltpu.CompilerParams(vmem_limit_bytes=mib * 2**20)

    anywhere = pl.BlockSpec(memory_space=pl.ANY)

    count = rows // rhs
    hbm = pl.BlockSpec(memory_space=pltpu.HBM)
    edge = (array(REACH, rhs, nx),) * 2
    plane_block = pltpu.VMEM((rhs, rows, nx), f32)
    mine, far_first, far_last = pl.pallas_call(
        far_kernel,
        out_shape=(array(rows + 4 * count, rhs, nx),) + edge,
        in_specs=[smem, hbm, hbm, hbm],
        out_specs=(vmem,) * 3,
        scratch_shapes=[
            plane_block,
            pltpu.VMEM(labels.shape, jnp.int32),
            pltpu.VMEM(boundary.shape, jnp.int32),
            pltpu.SemaphoreType.DMA((3,)),
        ],
        compiler_params=params(58),
    )(odd, residual, labels, boundary)
    ahead, near_first, near_last = pl.pallas_call(
        near_kernel,
        out_shape=(array(rows + 3 * count, rhs, nx),) + edge,
        in_specs=[smem, hbm, hbm],
        out_specs=(vmem,) * 3,
        scratch_shapes=[plane_block, pltpu.VMEM((4 * count, rhs, nx), f32), pltpu.SemaphoreType.DMA((2,))],
        compiler_params=params(52),
    )(odd, residual, mine)
    edges = jnp.stack([far_first, near_first]), jnp.stack([far_last, near_last])

    near2 = swapped(mine)
    far3 = relayed(ahead)
    near3 = relayed(mine, back=True)
    own_before, own_behind = rows_beside(*edges)
    near1 = swapped(
        pl.pallas_call(
            partial(second_kernel, rows),
            out_shape=array(rows + 2, rhs, nx),
            in_specs=[vmem, vmem, vmem, anywhere, anywhere],
            out_specs=vmem,
            compiler_params=params(8),
        )(ahead, own_before, own_behind, near2, far3)
    )
    far1 = relayed(near2)
    far2 = relayed(near1)

    edges = EDGES + sum(part is not None for _, *parts in FIELDS for part in parts)
    before, behind = rows_beside(
        *pl.pallas_call(
            partial(edges_kernel, rows),
            out_shape=(array(edges, rhs, nx),) * 2,
            in_specs=[vmem] * 6,
            out_specs=(vmem, vmem),
            compiler_params=params(12),
        )(near1, near2, far1, far3, near3, mine)
    )

    def planes(number):
        return (number, rows + 2 * REACH, rhs, nx)

    cells = (depth + 2 * REACH, rows + 2 * MARGIN, nx)
    inverse, sx, sy, sz, root, u0, u1, u2, split01, moments = pl.pallas_call(
        partial(early_kernel, rows),
        out_shape=(array(*cells),) * 5
        + tuple(array(*planes(number)) for number in (3, 2, 2))
        + (array(depth, rows, 4 * rhs, nx, dtype=bf16), array(rhs, 128)),
        in_specs=[vmem] * 11,
        out_specs=(vmem,) * 10,
        scratch_shapes=[pltpu.VMEM(planes(number), f32) for number in (4, 2)]
        + [pltpu.VMEM((cells[0] + 2,) + cells[1:], f32)] * 2
        + [pltpu.VMEM(cells, f32)],
        compiler_params=params(24),
    )(far3, far1, mine, ahead, own_before, own_behind, near1, near2, near3, before, behind)

    moments, split23 = pl.pallas_call(
        partial(late_kernel, rows),
        out_shape=(array(rhs, 128), array(depth, rows, 4 * rhs, nx, dtype=bf16)),
        in_specs=[vmem] * 9,
        out_specs=(vmem, vmem),
        scratch_shapes=[pltpu.VMEM(planes(number), f32) for number in (1, 2, 2)],
        compiler_params=params(20),
    )(far2, u0, u1, u2, moments, inverse, sx, sy, sz)

    moments = all_sum(moments, ("gy", "gz"))

    tile = math.gcd(rows, 32)
    plane_rows = pl.BlockSpec((rhs, 1, tile, nx), lambda z, y, odd: (0, jnp.bitwise_xor(z, odd[0]), y, 0))
    return pl.pallas_call(
        outputs_kernel,
        out_shape=(array(*iterate.shape), array(*residual.shape)),
        grid_spec=pltpu.PrefetchScalarGridSpec(
            num_scalar_prefetch=1,
            grid=(depth, rows // tile),
            in_specs=[vmem] * 5 + [plane_rows],
            out_specs=(plane_rows, plane_rows),
            scratch_shapes=[pltpu.VMEM((4 * rhs, 8 * rhs), bf16)],
        ),
        compiler_params=params(16),
    )(odd, moments, split01, split23, inverse, root, iterate)


def solution(mesh):
    placed = (
        P(None, ("regions", "gz"), "gy", None),
        P(None, ("regions", "gz"), "gy", None),
        P(("regions", "gz"), "gy", None),
        P(("regions", "gz"), "gy", None),
    )
    return jax.shard_map(
        on_device,
        mesh=mesh,
        in_specs=placed,
        out_specs=(P(None, ("regions", "gz"), "gy", None), P(None, ("regions", "gz"), "gy", None)),
        check_vma=False,
    )
```

```python
import math
from functools import partial

import jax
import jax.numpy as jnp
from jax import lax
from jax.experimental import pallas as pl
from jax.experimental.pallas import tpu as pltpu
from jax.sharding import PartitionSpec as P

NCLASS = 8
ITERS = 3
REACH = ITERS

contrast_log = 4.0 * math.log(10.0)
highest = lax.Precision.HIGHEST
f32 = jnp.float32
bf16 = jnp.bfloat16


def moved(block, axis, pairs):
    return lax.ppermute(block, axis, pairs)


def shifted(block, axis, step):
    count = lax.axis_size(axis)
    return moved(block, axis, [(i, i + step) for i in range(count) if 0 <= i + step < count])


def swapped(block):
    return moved(block, "gz", [(i, i ^ 1) for i in range(lax.axis_size("gz"))])


def relayed(block, back=False):
    count = lax.axis_size("gz")
    steps = [(i, i + 2 - 4 * (i % 2)) for i in range(count)]
    pairs = [(i, j) for i, j in steps if 0 <= j < count]
    return moved(block, "gz", [(j, i) for i, j in pairs] if back else pairs)


def rows_beside(before, after):
    count = lax.axis_size("gy")
    if count != 2:
        return shifted(after, "gy", 1), shifted(before, "gy", -1)
    second = lax.axis_index("gy") == 1
    other = moved(jnp.where(second, before, after), "gy", [(0, 1), (1, 0)])
    zero = jnp.zeros_like(other)
    return jnp.where(second, other, zero), jnp.where(second, zero, other)


def all_sum(values, axes):
    for axis in axes:
        count = lax.axis_size(axis)
        if count & (count - 1):
            values = lax.psum(values, axis)
            continue
        step = 1
        while step < count:
            values = values + lax.ppermute(values, axis, [(i, i ^ step) for i in range(count)])
            step *= 2
    return values


def face_of(center, beside):
    return jnp.where(beside > 0.0, 2.0 * center * beside / (center + beside), center)


LATE = 1
BESIDE = ((5, 0, 2), (6, 2, 1), (2, 3, 2))
EDGES = 5
FIELDS = (
    ("far3", 0, None), ("far3", 1, 2), ("far1", 1, 3), ("far1", 0, 2), ("mine", 0, 2),
    ("mine", 1, 3), ("near2", 1, 3), ("near2", 0, 2), ("near3", 0, 2), ("near3", 1, None),
)
MARGIN = 8


def turn_plane(block, out):
    def turn(group, carry):
        here = pl.ds(group * 8, 8)
        out[here] = pltpu.einshape("abc->bac", block[:, here, :])
        return carry

    lax.fori_loop(0, block.shape[1] // 8, turn, 0)


def far_kernel(odd, residual, labels, boundary, mine, first, last, block, label_cells, boundary_cells, arrived):
    rhs, depth, rows, nx = residual.shape
    copies = [
        pltpu.make_async_copy(labels, label_cells, arrived.at[0]),
        pltpu.make_async_copy(boundary, boundary_cells, arrived.at[1]),
        pltpu.make_async_copy(residual.at[:, odd[0]], block, arrived.at[2]),
    ]
    for copy in copies:
        copy.start()
    for copy in copies[:2]:
        copy.wait()
    count = rows // rhs
    for place in range(depth):
        plane = jnp.bitwise_xor(place, odd[0])
        for part in range(count):
            cells = pl.ds(part * rhs, rhs)
            mine[rows + place * count + part] = jnp.exp(
                label_cells[plane, cells, :].astype(f32) * (contrast_log / (NCLASS - 1))
            )
            mine[rows + (2 + place) * count + part] = (1 - boundary_cells[plane, cells, :]).astype(f32)
    copies[2].wait()
    turn_plane(block, mine)
    first[...] = mine[:REACH]
    last[...] = mine[rows - REACH : rows]


def near_kernel(odd, residual, mine, ahead, first, last, block, cells, arrived):
    rhs, _, rows, _ = residual.shape
    copies = [
        pltpu.make_async_copy(mine.at[pl.ds(rows, cells.shape[0])], cells, arrived.at[0]),
        pltpu.make_async_copy(residual.at[:, 1 - odd[0]], block, arrived.at[1]),
    ]
    for copy in copies:
        copy.start()
    copies[0].wait()
    count = rows // rhs
    for part in range(2 * count):
        ahead[rows + part] = cells[part]
    for part in range(count):
        ahead[rows + 2 * count + part] = cells[3 * count + part]
    copies[1].wait()
    turn_plane(block, ahead)
    first[...] = ahead[:REACH]
    last[...] = ahead[rows - REACH : rows]


def hand_on(message, earlier, out):
    del message, earlier, out


def second_kernel(rows, ahead, own_before, own_behind, out):
    def copy_rows(y, size):
        for j in range(size):
            out[y + j] = ahead[y + j]

    row_blocks(0, rows, copy_rows, 16)
    out[rows] = own_before[1, REACH - 1]
    out[rows + 1] = own_behind[1, 0]


def edges_kernel(rows, near1, near2, far1, far3, near3, mine, first, last):
    messages = {"near2": near2, "far1": far1, "far3": far3, "near3": near3, "mine": mine}
    rhs = mine.shape[1]
    count = rows // rhs
    for (_, place, number), source in zip(BESIDE, (near1, near2, far1)):
        first[place : place + number] = source[:number]
        last[place : place + number] = source[rows - number : rows]
    place = EDGES
    for name, *parts in FIELDS:
        for part in parts:
            if part is not None:
                start = rows + part * count
                first[place, :MARGIN] = messages[name][start, :MARGIN]
                last[place, :MARGIN] = messages[name][start + count - 1, rhs - MARGIN :]
                place += 1
                first[place - 1, MARGIN:] = jnp.zeros_like(first[place - 1, MARGIN:])
                last[place - 1, MARGIN:] = jnp.zeros_like(last[place - 1, MARGIN:])


def fill_cells(rows, messages, before, behind, coef, inner):
    place = EDGES
    for plane, (name, *parts) in enumerate(FIELDS):
        for part, out in zip(parts, (coef, inner)):
            if part is None:
                continue
            rhs = messages[name].shape[1]
            count = rows // rhs
            for block in range(count):
                out[plane, MARGIN + block * rhs : MARGIN + (block + 1) * rhs] = messages[name][
                    rows + part * count + block
                ]
            out[plane, :MARGIN] = before[place, :MARGIN]
            out[plane, MARGIN + rows :] = behind[place, :MARGIN]
            place += 1


def make_operator(coef, inner, inverse, sx, sy, sz, root, masked):
    planes, height, nx = inverse.shape
    lane = lax.broadcasted_iota(jnp.int32, (height, nx), 1)
    inside = lane < nx - 1

    def one_plane(plane, carry):
        here = coef[plane + 1]
        flag = inner[plane + 1]
        right = jnp.where(inside, pltpu.roll(here, nx - 1, 1), 0.0)
        left = jnp.where(lane > 0, pltpu.roll(here, 1, 1), 0.0)
        behind, before = pltpu.roll(here, height - 1, 0), pltpu.roll(here, 1, 0)
        along_x, along_y = face_of(here, right), face_of(here, behind)
        along_z = face_of(here, coef[plane + 2])
        total = along_x + jnp.where(left > 0.0, pltpu.roll(along_x, 1, 1), here)
        total += along_y + jnp.where(before > 0.0, pltpu.roll(along_y, 1, 0), here)
        total += along_z + face_of(here, coef[plane])
        diagonal = flag * total + (1.0 - flag)
        square = jnp.sqrt(diagonal)
        reciprocal = 1.0 / square
        root[plane] = square
        inverse[plane] = reciprocal
        scale = flag * reciprocal
        masked[plane] = scale
        sx[plane] = jnp.where(inside, scale * along_x * pltpu.roll(scale, nx - 1, 1), 0.0)
        sy[plane] = scale * along_y * pltpu.roll(scale, height - 1, 0)
        sz[plane] = scale * along_z
        return carry

    lax.fori_loop(0, planes, one_plane, 0)

    def next_plane(plane, carry):
        sz[plane] = sz[plane] * masked[plane + 1]
        return carry

    lax.fori_loop(0, planes - 1, next_plane, 0)


def cell_row(ref, plane, y):
    return ref[plane, pl.ds(y + (MARGIN - REACH), 1), :]


def row_blocks(start, stop, body, size, unroll=1):
    blocks = -(-(stop - start) // size)
    size = -(-(stop - start) // blocks)

    def step(block, carry):
        body(jnp.minimum(start + block * size, stop - size), size)
        return carry

    lax.fori_loop(0, blocks, step, 0, unroll=min(unroll, blocks))


def apply_rows(operator, plane, start, before, here, after, size):
    sx, sy, sz = operator
    ref, index = here
    out = []
    last, center = ref[index, start - 1], ref[index, start]
    below = cell_row(sy, plane, start - 1)
    width = center.shape[-1]
    for j in range(size):
        y = start + j
        following = ref[index, y + 1]
        above = cell_row(sy, plane, y)
        ahead = cell_row(sx, plane, y)
        total = ahead * pltpu.roll(center, width - 1, 1) + pltpu.roll(ahead * center, 1, 1)
        total += above * following + below * last
        total += cell_row(sz, plane, y) * after[0][after[1], y]
        total += cell_row(sz, plane - 1, y) * before[0][before[1], y]
        out.append(total)
        last, center, below = center, following, above
    return out


def spread(plane, depth=2):
    return max(REACH - plane, plane - (REACH + depth - 1), 0)


def scale_rows(plane, source, first, dst, start, count, inverse):
    out, place = dst

    def body(j, size):
        for i in range(size):
            out[place, start + j + i] = source[first + j + i] * cell_row(inverse, plane, start + j + i)

    if count < 8:
        body(0, count)
    else:
        row_blocks(0, count, body, 16)


def apply_plane(rows, power, plane, operator, fields, unroll=1):
    reach = REACH - power - spread(plane)
    src = [fields[power - 1, plane + offset] for offset in (-1, 0, 1)]
    out, place = fields[power, plane]

    def body(y, size):
        for j, values in enumerate(apply_rows(operator, plane, y, *src, size)):
            out[place, y + j] = values

    row_blocks(REACH - reach, REACH + rows + reach, body, 34, unroll)


def halves(blocks):
    stack = jnp.concatenate(blocks, axis=0)
    high = stack.astype(bf16)
    low = (stack - high.astype(f32)).astype(bf16)
    return jnp.concatenate([high, low], axis=0)


def inner_products(left, right):
    return lax.dot_general(left, right, (((1,), (1,)), ((), ())), preferred_element_type=f32)


def whole(gram, left, right):
    gram = gram[:left] + gram[left : 2 * left]
    return gram[:, :right] + gram[:, right : 2 * right]


def early_kernel(
    rows, far3, far1, mine, ahead, own_before, own_behind, near1, near2, near3, before, behind,
    inverse, sx, sy, sz, root, u0_out, u1_out, u2_out, split, moments, u0, u1, coef, inner, masked,
):
    messages = {"near2": near2, "far1": far1, "far3": far3, "near3": near3, "mine": mine}
    fill_cells(rows, messages, before, behind, coef, inner)
    make_operator(coef, inner, inverse, sx, sy, sz, root, masked)
    operator = (sx, sy, sz)
    fields = {(0, plane): (u0_out, index) for index, plane in enumerate((0, 2, 3))}
    fields.update({(0, plane): (u0, plane - 4) for plane in range(4, 8)})
    fields.update({(1, 3): (u1_out, 0), (1, 4): (u1_out, 1), (1, 5): (u1, 0), (1, 6): (u1, 1)})
    fields.update({(2, 4): (u2_out, 0), (2, 5): (u2_out, 1)})
    first, last = REACH, REACH + rows
    for plane, source in ((0, far3), (2, far1), (3, mine), (4, ahead), (5, near1), (6, near2), (7, near3)):
        scale_rows(plane, source, 0, fields[0, plane], first, rows, inverse)
    for plane in (3, 4):
        scale_rows(plane, own_before.at[plane - 3], 0, fields[0, plane], 0, REACH, inverse)
        scale_rows(plane, own_behind.at[plane - 3], 0, fields[0, plane], last, REACH, inverse)
    for plane, place, count in BESIDE:
        scale_rows(plane, before, place, fields[0, plane], first - count, count, inverse)
        scale_rows(plane, behind, place, fields[0, plane], last, count, inverse)
    for power, plane in ((1, 3), (1, 4), (1, 5), (1, 6), (2, 4), (2, 5)):
        apply_plane(rows, power, plane, operator, fields)

    rhs = u0.shape[2]
    gram = jnp.zeros((4 * rhs, 4 * rhs), f32)
    for plane in range(2):

        def gram_rows(block, total, plane=plane):
            for group in range(4):
                parts = []
                for j in range(4):
                    y = block * 16 + group * 4 + j
                    sources = [fields[power, plane + REACH] for power in range(2)]
                    both = halves([ref[index, y + REACH] for ref, index in sources])
                    split[plane, y] = both
                    parts.append(both)
                wide = jnp.concatenate(parts, axis=1)
                total = total + inner_products(wide, wide)
            return total

        gram = lax.fori_loop(0, rows // 16, gram_rows, gram)
    gram = whole(gram, 2 * rhs, 2 * rhs)
    moments[:, : 2 * rhs] = gram[:rhs]
    moments[:, 2 * rhs : 3 * rhs] = gram[rhs:, rhs:]


def late_kernel(
    rows, far2, u0_in, u1_in, u2_in, moments_in, inverse, sx, sy, sz, moments, split, u0, u1, u2
):
    operator = (sx, sy, sz)
    fields = {(0, plane): (u0_in, index) for index, plane in enumerate((0, 2, 3))}
    fields[0, LATE] = (u0, 0)
    fields.update({(1, 1): (u1, 0), (1, 2): (u1, 1), (1, 3): (u1_in, 0), (1, 4): (u1_in, 1)})
    fields.update({(2, 2): (u2, 0), (2, 3): (u2, 1), (2, 4): (u2_in, 0), (2, 5): (u2_in, 1)})
    first, last = REACH, REACH + rows
    for place, start, count in ((0, first, rows), (rows, first - 1, 1), (rows + 1, last, 1)):
        scale_rows(LATE, far2, place, fields[0, LATE], start, count, inverse)
    for power, plane in ((1, 1), (1, 2), (2, 2), (2, 3)):
        apply_plane(rows, power, plane, operator, fields, 2)

    rhs = u0.shape[2]
    gram = jnp.zeros((6 * rhs, 2 * rhs), f32)
    for plane in range(2):
        level = plane + REACH

        def gram_rows(block, total, plane=plane, level=level):
            start = block * 16
            y = start + REACH
            last = apply_rows(operator, level, y, *[fields[2, level + offset] for offset in (-1, 0, 1)], 16)
            for group in range(4):
                left, right = [], []
                for j in range(group * 4, group * 4 + 4):
                    ref, index = fields[2, level]
                    both = halves([ref[index, y + j], last[j]])
                    split[plane, start + j] = both
                    left.append(jnp.concatenate([halves([u1_in[plane, y + j]]), both], axis=0))
                    right.append(jnp.concatenate([both[:rhs], both[2 * rhs : 3 * rhs]], axis=0))
                total = total + inner_products(jnp.concatenate(left, axis=1), jnp.concatenate(right, axis=1))
            return total

        gram = lax.fori_loop(0, rows // 16, gram_rows, gram, unroll=2)
    gram = gram[:, :rhs] + gram[:, rhs:]
    blocks = [gram[part * rhs : (part + 1) * rhs] for part in range(6)]
    moments[:, : 3 * rhs] = moments_in[:, : 3 * rhs]
    moments[:, 3 * rhs : 4 * rhs] = blocks[0] + blocks[1]
    moments[:, 4 * rhs : 5 * rhs] = blocks[2] + blocks[4]
    moments[:, 5 * rhs : 6 * rhs] = blocks[3] + blocks[5]
    moments[:, 6 * rhs :] = jnp.zeros((rhs, moments.shape[1] - 6 * rhs), f32)


def inverse_of_pair(a, b, c, d):
    scale = 1.0 / (a * d - b * c)
    return d * scale, -b * scale, -c * scale, a * scale


def times(p, q):
    a, b, c, d = p
    e, f, g, h = q
    return a * e + b * g, a * f + b * h, c * e + d * g, c * f + d * h


def inverse_of_four(m):
    p, q = (m[0][0], m[0][1], m[1][0], m[1][1]), (m[0][2], m[0][3], m[1][2], m[1][3])
    r, s = (m[2][0], m[2][1], m[3][0], m[3][1]), (m[2][2], m[2][3], m[3][2], m[3][3])
    inner = inverse_of_pair(*p)
    right, left = times(inner, q), times(r, inner)
    outer = inverse_of_pair(*[x - y for x, y in zip(s, times(r, right))])
    lower = [-x for x in times(outer, left)]
    upper = [-x for x in times(right, outer)]
    corner = [x - y for x, y in zip(inner, times(right, lower))]
    return (
        (corner[0], corner[1], upper[0], upper[1]),
        (corner[2], corner[3], upper[2], upper[3]),
        (lower[0], lower[1], outer[0], outer[1]),
        (lower[2], lower[3], outer[2], outer[3]),
    )


def eliminate(stacked, size):
    tiles, height, width = stacked.shape
    lane = lax.broadcasted_iota(jnp.int32, (height, width), 1)

    def everywhere(row):
        return jnp.broadcast_to(row, (height, width))

    for k in range(0, size, 4):
        if k and k % height == 0:
            stacked = stacked[1:]
        at = k % height
        rows = [everywhere(stacked[0, at + i : at + i + 1]) for i in range(4)]
        columns = [jnp.broadcast_to(stacked[:, :, k + i : k + i + 1], stacked.shape) for i in range(4)]
        block = [[everywhere(columns[j][0, at + i : at + i + 1]) for j in range(4)] for i in range(4)]
        inverse = inverse_of_four(block)
        pivots = (lane >= k) & (lane < k + 4)
        result = jnp.where(pivots[None], 0.0, stacked)
        for i in range(4):
            mix = (inverse[i][0] * rows[0] + inverse[i][1] * rows[1]) + (
                inverse[i][2] * rows[2] + inverse[i][3] * rows[3]
            )
            for j in range(4):
                mix = jnp.where(lane == k + j, -inverse[i][j], mix)
            result = result - columns[i] * mix[None]
        stacked = result
    return stacked[1:]


def mixing(moments, rhs):
    width = moments.shape[1]
    lane = lax.broadcasted_iota(jnp.int32, (rhs, width), 1)
    row = lax.broadcasted_iota(jnp.int32, (rhs, width), 0)
    size = REACH * rhs
    rolled = [moments] + [pltpu.roll(moments, width - i * rhs, 1) for i in range(1, REACH + 1)]
    energy = [rolled[i] - rolled[i + 1] for i in range(REACH)]
    tiles = jnp.concatenate(energy + [moments], axis=0).reshape(-1, 8, width)
    solved = eliminate(tiles, size).reshape(rhs, width)
    solved = jnp.where(lane < size, solved, 0.0)
    residual = (row == lane).astype(f32) - (solved - pltpu.roll(solved, rhs, 1))
    return solved, residual


def outputs_kernel(odd, moments, split01, split23, inverse, root, iterate, iterate_out, residual_out, coefs):
    rhs, _, rows, nx = iterate.shape
    plane, block = pl.program_id(0), pl.program_id(1)

    @pl.when((plane == 0) & (block == 0))
    def _():
        solved, residual = mixing(moments[...], rhs)
        both = jnp.concatenate([solved[:, : 4 * rhs], residual[:, : 4 * rhs]], axis=0)
        high = both.astype(bf16).astype(f32)
        stacked = jnp.concatenate([high, both - high], axis=0)
        pair01, pair23 = stacked[:, : 2 * rhs], stacked[:, 2 * rhs :]
        coefs[...] = jnp.concatenate([pair01, pair01, pair23, pair23], axis=1).astype(bf16)

    def group_of_rows(group, carry):
        y = block * rows + group * 8
        wide = jnp.concatenate(
            [jnp.concatenate([split01[plane, y + j], split23[plane, y + j]], axis=0) for j in range(8)], axis=1
        )
        mixed = jnp.dot(coefs[...], wide, preferred_element_type=f32)
        mixed = mixed[: 2 * rhs] + mixed[2 * rhs :]
        by_row = jnp.stack([mixed[:, j * nx : (j + 1) * nx] for j in range(8)], axis=0)
        by_rhs = pltpu.einshape("abc->bac", by_row)
        cells = pl.ds(pl.multiple_of(y + MARGIN, 8), 8)
        here = pl.ds(group * 8, 8)
        iterate_out[:, 0, here] = iterate[:, 0, here] + by_rhs[:rhs] * inverse[plane + REACH, cells]
        residual_out[:, 0, here] = by_rhs[rhs:] * root[plane + REACH, cells]
        return carry

    lax.fori_loop(0, rows // 8, group_of_rows, 0, unroll=True)


def on_device(iterate, residual, labels, boundary):
    rhs, depth, rows, nx = residual.shape
    assert depth == 2 and REACH == 3 and rows % rhs == 0 and rhs % 8 == 0 and lax.axis_size("gz") % 2 == 0
    odd = (lax.axis_index("gz") % 2).astype(jnp.int32).reshape(1)
    vmem = pl.BlockSpec(memory_space=pltpu.VMEM)
    smem = pl.BlockSpec(memory_space=pltpu.SMEM)

    def array(*shape, dtype=f32):
        return jax.ShapeDtypeStruct(shape, dtype)

    def params(mib):
        return pltpu.CompilerParams(vmem_limit_bytes=mib * 2**20)

    anywhere = pl.BlockSpec(memory_space=pl.ANY)

    count = rows // rhs
    hbm = pl.BlockSpec(memory_space=pltpu.HBM)
    edge = (array(REACH, rhs, nx),) * 2
    plane_block = pltpu.VMEM((rhs, rows, nx), f32)
    mine, far_first, far_last = pl.pallas_call(
        far_kernel,
        out_shape=(array(rows + 4 * count, rhs, nx),) + edge,
        in_specs=[smem, hbm, hbm, hbm],
        out_specs=(vmem,) * 3,
        scratch_shapes=[
            plane_block,
            pltpu.VMEM(labels.shape, jnp.int32),
            pltpu.VMEM(boundary.shape, jnp.int32),
            pltpu.SemaphoreType.DMA((3,)),
        ],
        compiler_params=params(58),
    )(odd, residual, labels, boundary)
    ahead, near_first, near_last = pl.pallas_call(
        near_kernel,
        out_shape=(array(rows + 3 * count, rhs, nx),) + edge,
        in_specs=[smem, hbm, hbm],
        out_specs=(vmem,) * 3,
        scratch_shapes=[plane_block, pltpu.VMEM((4 * count, rhs, nx), f32), pltpu.SemaphoreType.DMA((2,))],
        compiler_params=params(52),
    )(odd, residual, mine)
    edges = jnp.stack([far_first, near_first]), jnp.stack([far_last, near_last])

    first_swap = swapped(mine)
    far3 = relayed(ahead)
    near3 = relayed(mine, back=True)
    own_before, own_behind = rows_beside(*edges)
    second = pl.pallas_call(
        partial(second_kernel, rows),
        out_shape=array(rows + 2, rhs, nx),
        in_specs=[vmem] * 3,
        out_specs=vmem,
        compiler_params=params(8),
    )(ahead, own_before, own_behind)
    def handed_on(block, earlier):
        return pl.pallas_call(
            hand_on,
            out_shape=array(*block.shape),
            in_specs=[anywhere] * 2,
            out_specs=anywhere,
            input_output_aliases={0: 0},
            compiler_params=params(8),
        )(block, earlier)

    near2 = handed_on(first_swap, second)
    near1 = swapped(handed_on(second, far3))
    far1 = relayed(near2)
    far2 = relayed(near1)

    edges = EDGES + sum(part is not None for _, *parts in FIELDS for part in parts)
    before, behind = rows_beside(
        *pl.pallas_call(
            partial(edges_kernel, rows),
            out_shape=(array(edges, rhs, nx),) * 2,
            in_specs=[vmem] * 6,
            out_specs=(vmem, vmem),
            compiler_params=params(12),
        )(near1, near2, far1, far3, near3, mine)
    )

    def planes(number):
        return (number, rows + 2 * REACH, rhs, nx)

    cells = (depth + 2 * REACH, rows + 2 * MARGIN, nx)
    inverse, sx, sy, sz, root, u0, u1, u2, split01, moments = pl.pallas_call(
        partial(early_kernel, rows),
        out_shape=(array(*cells),) * 5
        + tuple(array(*planes(number)) for number in (3, 2, 2))
        + (array(depth, rows, 4 * rhs, nx, dtype=bf16), array(rhs, 128)),
        in_specs=[vmem] * 11,
        out_specs=(vmem,) * 10,
        scratch_shapes=[pltpu.VMEM(planes(number), f32) for number in (4, 2)]
        + [pltpu.VMEM((cells[0] + 2,) + cells[1:], f32)] * 2
        + [pltpu.VMEM(cells, f32)],
        compiler_params=params(24),
    )(far3, far1, mine, ahead, own_before, own_behind, near1, near2, near3, before, behind)

    moments, split23 = pl.pallas_call(
        partial(late_kernel, rows),
        out_shape=(array(rhs, 128), array(depth, rows, 4 * rhs, nx, dtype=bf16)),
        in_specs=[vmem] * 9,
        out_specs=(vmem, vmem),
        scratch_shapes=[pltpu.VMEM(planes(number), f32) for number in (1, 2, 2)],
        compiler_params=params(20),
    )(far2, u0, u1, u2, moments, inverse, sx, sy, sz)

    moments = all_sum(moments, ("gy", "gz"))

    tile = math.gcd(rows, 32)
    plane_rows = pl.BlockSpec((rhs, 1, tile, nx), lambda z, y, odd: (0, jnp.bitwise_xor(z, odd[0]), y, 0))
    return pl.pallas_call(
        outputs_kernel,
        out_shape=(array(*iterate.shape), array(*residual.shape)),
        grid_spec=pltpu.PrefetchScalarGridSpec(
            num_scalar_prefetch=1,
            grid=(depth, rows // tile),
            in_specs=[vmem] * 5 + [plane_rows],
            out_specs=(plane_rows, plane_rows),
            scratch_shapes=[pltpu.VMEM((4 * rhs, 8 * rhs), bf16)],
        ),
        compiler_params=params(16),
    )(odd, moments, split01, split23, inverse, root, iterate)


def solution(mesh):
    placed = (
        P(None, ("regions", "gz"), "gy", None),
        P(None, ("regions", "gz"), "gy", None),
        P(("regions", "gz"), "gy", None),
        P(("regions", "gz"), "gy", None),
    )
    return jax.shard_map(
        on_device,
        mesh=mesh,
        in_specs=placed,
        out_specs=(P(None, ("regions", "gz"), "gy", None), P(None, ("regions", "gz"), "gy", None)),
        check_vma=False,
    )
```

```python
import math
from functools import partial

import jax
import jax.numpy as jnp
from jax import lax
from jax.experimental import pallas as pl
from jax.experimental.pallas import tpu as pltpu
from jax.sharding import PartitionSpec as P

NCLASS = 8
ITERS = 3
REACH = ITERS

contrast_log = 4.0 * math.log(10.0)
highest = lax.Precision.HIGHEST
f32 = jnp.float32
bf16 = jnp.bfloat16


def moved(block, axis, pairs):
    return lax.ppermute(block, axis, pairs)


def shifted(block, axis, step):
    count = lax.axis_size(axis)
    return moved(block, axis, [(i, i + step) for i in range(count) if 0 <= i + step < count])


def swapped(block):
    return moved(block, "gz", [(i, i ^ 1) for i in range(lax.axis_size("gz"))])


def relayed(block, back=False):
    count = lax.axis_size("gz")
    steps = [(i, i + 2 - 4 * (i % 2)) for i in range(count)]
    pairs = [(i, j) for i, j in steps if 0 <= j < count]
    return moved(block, "gz", [(j, i) for i, j in pairs] if back else pairs)


def rows_beside(before, after):
    count = lax.axis_size("gy")
    if count != 2:
        return shifted(after, "gy", 1), shifted(before, "gy", -1)
    second = lax.axis_index("gy") == 1
    other = moved(jnp.where(second, before, after), "gy", [(0, 1), (1, 0)])
    zero = jnp.zeros_like(other)
    return jnp.where(second, other, zero), jnp.where(second, zero, other)


def all_sum(values, axes):
    for axis in axes:
        count = lax.axis_size(axis)
        if count & (count - 1):
            values = lax.psum(values, axis)
            continue
        step = 1
        while step < count:
            values = values + lax.ppermute(values, axis, [(i, i ^ step) for i in range(count)])
            step *= 2
    return values


def face_of(center, beside):
    return jnp.where(beside > 0.0, 2.0 * center * beside / (center + beside), center)


LATE = 1
BESIDE = ((5, 0, 2), (6, 2, 1), (2, 3, 2))
EDGES = 5
FIELDS = (
    ("far3", 0, None), ("far3", 1, 2), ("beyond", 1, 3), ("beyond", 0, 2), ("mine", 0, 2),
    ("mine", 1, 3), ("near2", 1, 3), ("near2", 0, 2), ("near3", 0, 2), ("near3", 1, None),
)
MARGIN = 8


def turn_plane(block, out):
    def turn(group, carry):
        here = pl.ds(group * 8, 8)
        out[here] = pltpu.einshape("abc->bac", block[:, here, :])
        return carry

    lax.fori_loop(0, block.shape[1] // 8, turn, 0)


def far_kernel(odd, residual, labels, boundary, mine, first, last, block, label_cells, boundary_cells, arrived):
    rhs, depth, rows, nx = residual.shape
    copies = [
        pltpu.make_async_copy(labels, label_cells, arrived.at[0]),
        pltpu.make_async_copy(boundary, boundary_cells, arrived.at[1]),
        pltpu.make_async_copy(residual.at[:, odd[0]], block, arrived.at[2]),
    ]
    for copy in copies:
        copy.start()
    for copy in copies[:2]:
        copy.wait()
    count = rows // rhs
    for place in range(depth):
        plane = jnp.bitwise_xor(place, odd[0])
        for part in range(count):
            cells = pl.ds(part * rhs, rhs)
            mine[rows + place * count + part] = jnp.exp(
                label_cells[plane, cells, :].astype(f32) * (contrast_log / (NCLASS - 1))
            )
            mine[rows + (2 + place) * count + part] = (1 - boundary_cells[plane, cells, :]).astype(f32)
    copies[2].wait()
    turn_plane(block, mine)
    first[...] = mine[:REACH]
    last[...] = mine[rows - REACH : rows]


def near_kernel(odd, residual, mine, ahead, first, last, block, cells, arrived):
    rhs, _, rows, _ = residual.shape
    copies = [
        pltpu.make_async_copy(mine.at[pl.ds(rows, cells.shape[0])], cells, arrived.at[0]),
        pltpu.make_async_copy(residual.at[:, 1 - odd[0]], block, arrived.at[1]),
    ]
    for copy in copies:
        copy.start()
    copies[0].wait()
    count = rows // rhs
    for part in range(2 * count):
        ahead[rows + part] = cells[part]
    for part in range(count):
        ahead[rows + 2 * count + part] = cells[3 * count + part]
    copies[1].wait()
    turn_plane(block, ahead)
    first[...] = ahead[:REACH]
    last[...] = ahead[rows - REACH : rows]


def hand_on(message, earlier, out):
    del message, earlier, out


def second_kernel(rows, ahead, own_before, own_behind, out):
    def copy_rows(y, size):
        for j in range(size):
            out[y + j] = ahead[y + j]

    row_blocks(0, rows, copy_rows, 16)
    out[rows] = own_before[1, REACH - 1]
    out[rows + 1] = own_behind[1, 0]


def copy_kernel(first, source, *rest):
    out = rest[-1]

    def copy_rows(y, size):
        for j in range(size):
            out[y + j] = source[first + y + j]

    row_blocks(0, out.shape[0], copy_rows, 16)


def edges_kernel(rows, near1, near2, far1, beyond, far3, near3, mine, first, last):
    messages = {"near2": near2, "beyond": beyond, "far3": far3, "near3": near3, "mine": mine}
    rhs = mine.shape[1]
    count = rows // rhs
    for (_, place, number), source in zip(BESIDE, (near1, near2, far1)):
        first[place : place + number] = source[:number]
        last[place : place + number] = source[rows - number : rows]
    place = EDGES
    for name, *parts in FIELDS:
        for part in parts:
            if part is not None:
                start = part * count + (rows if name != "beyond" else 0)
                first[place, :MARGIN] = messages[name][start, :MARGIN]
                last[place, :MARGIN] = messages[name][start + count - 1, rhs - MARGIN :]
                place += 1
                first[place - 1, MARGIN:] = jnp.zeros_like(first[place - 1, MARGIN:])
                last[place - 1, MARGIN:] = jnp.zeros_like(last[place - 1, MARGIN:])


def fill_cells(rows, messages, before, behind, coef, inner):
    place = EDGES
    for plane, (name, *parts) in enumerate(FIELDS):
        for part, out in zip(parts, (coef, inner)):
            if part is None:
                continue
            rhs = messages[name].shape[1]
            count = rows // rhs
            first = rows if name != "beyond" else 0
            for block in range(count):
                out[plane, MARGIN + block * rhs : MARGIN + (block + 1) * rhs] = messages[name][
                    first + part * count + block
                ]
            out[plane, :MARGIN] = before[place, :MARGIN]
            out[plane, MARGIN + rows :] = behind[place, :MARGIN]
            place += 1


def make_operator(coef, inner, inverse, sx, sy, sz, root, masked):
    planes, height, nx = inverse.shape
    lane = lax.broadcasted_iota(jnp.int32, (height, nx), 1)
    inside = lane < nx - 1

    def one_plane(plane, carry):
        here = coef[plane + 1]
        flag = inner[plane + 1]
        right = jnp.where(inside, pltpu.roll(here, nx - 1, 1), 0.0)
        left = jnp.where(lane > 0, pltpu.roll(here, 1, 1), 0.0)
        behind, before = pltpu.roll(here, height - 1, 0), pltpu.roll(here, 1, 0)
        along_x, along_y = face_of(here, right), face_of(here, behind)
        along_z = face_of(here, coef[plane + 2])
        total = along_x + jnp.where(left > 0.0, pltpu.roll(along_x, 1, 1), here)
        total += along_y + jnp.where(before > 0.0, pltpu.roll(along_y, 1, 0), here)
        total += along_z + face_of(here, coef[plane])
        diagonal = flag * total + (1.0 - flag)
        square = jnp.sqrt(diagonal)
        reciprocal = 1.0 / square
        root[plane] = square
        inverse[plane] = reciprocal
        scale = flag * reciprocal
        masked[plane] = scale
        sx[plane] = jnp.where(inside, scale * along_x * pltpu.roll(scale, nx - 1, 1), 0.0)
        sy[plane] = scale * along_y * pltpu.roll(scale, height - 1, 0)
        sz[plane] = scale * along_z
        return carry

    lax.fori_loop(0, planes, one_plane, 0)

    def next_plane(plane, carry):
        sz[plane] = sz[plane] * masked[plane + 1]
        return carry

    lax.fori_loop(0, planes - 1, next_plane, 0)


def cell_row(ref, plane, y):
    return ref[plane, pl.ds(y + (MARGIN - REACH), 1), :]


def row_blocks(start, stop, body, size, unroll=1):
    blocks = -(-(stop - start) // size)
    size = -(-(stop - start) // blocks)

    def step(block, carry):
        body(jnp.minimum(start + block * size, stop - size), size)
        return carry

    lax.fori_loop(0, blocks, step, 0, unroll=min(unroll, blocks))


def apply_rows(operator, plane, start, before, here, after, size):
    sx, sy, sz = operator
    ref, index = here
    out = []
    last, center = ref[index, start - 1], ref[index, start]
    below = cell_row(sy, plane, start - 1)
    width = center.shape[-1]
    for j in range(size):
        y = start + j
        following = ref[index, y + 1]
        above = cell_row(sy, plane, y)
        ahead = cell_row(sx, plane, y)
        total = ahead * pltpu.roll(center, width - 1, 1) + pltpu.roll(ahead * center, 1, 1)
        total += above * following + below * last
        total += cell_row(sz, plane, y) * after[0][after[1], y]
        total += cell_row(sz, plane - 1, y) * before[0][before[1], y]
        out.append(total)
        last, center, below = center, following, above
    return out


def spread(plane, depth=2):
    return max(REACH - plane, plane - (REACH + depth - 1), 0)


def scale_rows(plane, source, first, dst, start, count, inverse):
    out, place = dst

    def body(j, size):
        for i in range(size):
            out[place, start + j + i] = source[first + j + i] * cell_row(inverse, plane, start + j + i)

    if count < 8:
        body(0, count)
    else:
        row_blocks(0, count, body, 16)


def apply_plane(rows, power, plane, operator, fields, unroll=1):
    reach = REACH - power - spread(plane)
    src = [fields[power - 1, plane + offset] for offset in (-1, 0, 1)]
    out, place = fields[power, plane]

    def body(y, size):
        for j, values in enumerate(apply_rows(operator, plane, y, *src, size)):
            out[place, y + j] = values

    row_blocks(REACH - reach, REACH + rows + reach, body, 34, unroll)


def halves(blocks):
    stack = jnp.concatenate(blocks, axis=0)
    high = stack.astype(bf16)
    low = (stack - high.astype(f32)).astype(bf16)
    return jnp.concatenate([high, low], axis=0)


def inner_products(left, right):
    return lax.dot_general(left, right, (((1,), (1,)), ((), ())), preferred_element_type=f32)


def whole(gram, left, right):
    gram = gram[:left] + gram[left : 2 * left]
    return gram[:, :right] + gram[:, right : 2 * right]


def early_kernel(
    rows, far3, far1, beyond, mine, ahead, own_before, own_behind, near1, near2, near3, before, behind,
    inverse, sx, sy, sz, root, u0_out, u1_out, u2_out, split, moments, u0, u1, coef, inner, masked,
):
    messages = {"near2": near2, "beyond": beyond, "far3": far3, "near3": near3, "mine": mine}
    fill_cells(rows, messages, before, behind, coef, inner)
    make_operator(coef, inner, inverse, sx, sy, sz, root, masked)
    operator = (sx, sy, sz)
    fields = {(0, plane): (u0_out, index) for index, plane in enumerate((0, 2, 3))}
    fields.update({(0, plane): (u0, plane - 4) for plane in range(4, 8)})
    fields.update({(1, 3): (u1_out, 0), (1, 4): (u1_out, 1), (1, 5): (u1, 0), (1, 6): (u1, 1)})
    fields.update({(2, 4): (u2_out, 0), (2, 5): (u2_out, 1)})
    first, last = REACH, REACH + rows
    for plane, source in ((0, far3), (2, far1), (3, mine), (4, ahead), (5, near1), (6, near2), (7, near3)):
        scale_rows(plane, source, 0, fields[0, plane], first, rows, inverse)
    for plane in (3, 4):
        scale_rows(plane, own_before.at[plane - 3], 0, fields[0, plane], 0, REACH, inverse)
        scale_rows(plane, own_behind.at[plane - 3], 0, fields[0, plane], last, REACH, inverse)
    for plane, place, count in BESIDE:
        scale_rows(plane, before, place, fields[0, plane], first - count, count, inverse)
        scale_rows(plane, behind, place, fields[0, plane], last, count, inverse)
    for power, plane in ((1, 3), (1, 4), (1, 5), (1, 6), (2, 4), (2, 5)):
        apply_plane(rows, power, plane, operator, fields)

    rhs = u0.shape[2]
    gram = jnp.zeros((4 * rhs, 4 * rhs), f32)
    for plane in range(2):

        def gram_rows(block, total, plane=plane):
            for group in range(4):
                parts = []
                for j in range(4):
                    y = block * 16 + group * 4 + j
                    sources = [fields[power, plane + REACH] for power in range(2)]
                    both = halves([ref[index, y + REACH] for ref, index in sources])
                    split[plane, y] = both
                    parts.append(both)
                wide = jnp.concatenate(parts, axis=1)
                total = total + inner_products(wide, wide)
            return total

        gram = lax.fori_loop(0, rows // 16, gram_rows, gram)
    gram = whole(gram, 2 * rhs, 2 * rhs)
    moments[:, : 2 * rhs] = gram[:rhs]
    moments[:, 2 * rhs : 3 * rhs] = gram[rhs:, rhs:]


def late_kernel(
    rows, far2, u0_in, u1_in, u2_in, moments_in, inverse, sx, sy, sz, moments, split, u0, u1, u2
):
    operator = (sx, sy, sz)
    fields = {(0, plane): (u0_in, index) for index, plane in enumerate((0, 2, 3))}
    fields[0, LATE] = (u0, 0)
    fields.update({(1, 1): (u1, 0), (1, 2): (u1, 1), (1, 3): (u1_in, 0), (1, 4): (u1_in, 1)})
    fields.update({(2, 2): (u2, 0), (2, 3): (u2, 1), (2, 4): (u2_in, 0), (2, 5): (u2_in, 1)})
    first, last = REACH, REACH + rows
    for place, start, count in ((0, first, rows), (rows, first - 1, 1), (rows + 1, last, 1)):
        scale_rows(LATE, far2, place, fields[0, LATE], start, count, inverse)
    for power, plane in ((1, 1), (1, 2), (2, 2), (2, 3)):
        apply_plane(rows, power, plane, operator, fields, 2)

    rhs = u0.shape[2]
    gram = jnp.zeros((6 * rhs, 2 * rhs), f32)
    for plane in range(2):
        level = plane + REACH

        def gram_rows(block, total, plane=plane, level=level):
            start = block * 16
            y = start + REACH
            last = apply_rows(operator, level, y, *[fields[2, level + offset] for offset in (-1, 0, 1)], 16)
            for group in range(4):
                left, right = [], []
                for j in range(group * 4, group * 4 + 4):
                    ref, index = fields[2, level]
                    both = halves([ref[index, y + j], last[j]])
                    split[plane, start + j] = both
                    left.append(jnp.concatenate([halves([u1_in[plane, y + j]]), both], axis=0))
                    right.append(jnp.concatenate([both[:rhs], both[2 * rhs : 3 * rhs]], axis=0))
                total = total + inner_products(jnp.concatenate(left, axis=1), jnp.concatenate(right, axis=1))
            return total

        gram = lax.fori_loop(0, rows // 16, gram_rows, gram, unroll=2)
    gram = gram[:, :rhs] + gram[:, rhs:]
    blocks = [gram[part * rhs : (part + 1) * rhs] for part in range(6)]
    moments[:, : 3 * rhs] = moments_in[:, : 3 * rhs]
    moments[:, 3 * rhs : 4 * rhs] = blocks[0] + blocks[1]
    moments[:, 4 * rhs : 5 * rhs] = blocks[2] + blocks[4]
    moments[:, 5 * rhs : 6 * rhs] = blocks[3] + blocks[5]
    moments[:, 6 * rhs :] = jnp.zeros((rhs, moments.shape[1] - 6 * rhs), f32)


def inverse_of_pair(a, b, c, d):
    scale = 1.0 / (a * d - b * c)
    return d * scale, -b * scale, -c * scale, a * scale


def times(p, q):
    a, b, c, d = p
    e, f, g, h = q
    return a * e + b * g, a * f + b * h, c * e + d * g, c * f + d * h


def inverse_of_four(m):
    p, q = (m[0][0], m[0][1], m[1][0], m[1][1]), (m[0][2], m[0][3], m[1][2], m[1][3])
    r, s = (m[2][0], m[2][1], m[3][0], m[3][1]), (m[2][2], m[2][3], m[3][2], m[3][3])
    inner = inverse_of_pair(*p)
    right, left = times(inner, q), times(r, inner)
    outer = inverse_of_pair(*[x - y for x, y in zip(s, times(r, right))])
    lower = [-x for x in times(outer, left)]
    upper = [-x for x in times(right, outer)]
    corner = [x - y for x, y in zip(inner, times(right, lower))]
    return (
        (corner[0], corner[1], upper[0], upper[1]),
        (corner[2], corner[3], upper[2], upper[3]),
        (lower[0], lower[1], outer[0], outer[1]),
        (lower[2], lower[3], outer[2], outer[3]),
    )


def eliminate(stacked, size):
    tiles, height, width = stacked.shape
    lane = lax.broadcasted_iota(jnp.int32, (height, width), 1)

    def everywhere(row):
        return jnp.broadcast_to(row, (height, width))

    for k in range(0, size, 4):
        if k and k % height == 0:
            stacked = stacked[1:]
        at = k % height
        rows = [everywhere(stacked[0, at + i : at + i + 1]) for i in range(4)]
        columns = [jnp.broadcast_to(stacked[:, :, k + i : k + i + 1], stacked.shape) for i in range(4)]
        block = [[everywhere(columns[j][0, at + i : at + i + 1]) for j in range(4)] for i in range(4)]
        inverse = inverse_of_four(block)
        pivots = (lane >= k) & (lane < k + 4)
        result = jnp.where(pivots[None], 0.0, stacked)
        for i in range(4):
            mix = (inverse[i][0] * rows[0] + inverse[i][1] * rows[1]) + (
                inverse[i][2] * rows[2] + inverse[i][3] * rows[3]
            )
            for j in range(4):
                mix = jnp.where(lane == k + j, -inverse[i][j], mix)
            result = result - columns[i] * mix[None]
        stacked = result
    return stacked[1:]


def mixing(moments, rhs):
    width = moments.shape[1]
    lane = lax.broadcasted_iota(jnp.int32, (rhs, width), 1)
    row = lax.broadcasted_iota(jnp.int32, (rhs, width), 0)
    size = REACH * rhs
    rolled = [moments] + [pltpu.roll(moments, width - i * rhs, 1) for i in range(1, REACH + 1)]
    energy = [rolled[i] - rolled[i + 1] for i in range(REACH)]
    tiles = jnp.concatenate(energy + [moments], axis=0).reshape(-1, 8, width)
    solved = eliminate(tiles, size).reshape(rhs, width)
    solved = jnp.where(lane < size, solved, 0.0)
    residual = (row == lane).astype(f32) - (solved - pltpu.roll(solved, rhs, 1))
    return solved, residual


def outputs_kernel(odd, moments, split01, split23, inverse, root, iterate, iterate_out, residual_out, coefs):
    rhs, _, rows, nx = iterate.shape
    plane, block = pl.program_id(0), pl.program_id(1)

    @pl.when((plane == 0) & (block == 0))
    def _():
        solved, residual = mixing(moments[...], rhs)
        both = jnp.concatenate([solved[:, : 4 * rhs], residual[:, : 4 * rhs]], axis=0)
        high = both.astype(bf16).astype(f32)
        stacked = jnp.concatenate([high, both - high], axis=0)
        pair01, pair23 = stacked[:, : 2 * rhs], stacked[:, 2 * rhs :]
        coefs[...] = jnp.concatenate([pair01, pair01, pair23, pair23], axis=1).astype(bf16)

    def group_of_rows(group, carry):
        y = block * rows + group * 8
        wide = jnp.concatenate(
            [jnp.concatenate([split01[plane, y + j], split23[plane, y + j]], axis=0) for j in range(8)], axis=1
        )
        mixed = jnp.dot(coefs[...], wide, preferred_element_type=f32)
        mixed = mixed[: 2 * rhs] + mixed[2 * rhs :]
        by_row = jnp.stack([mixed[:, j * nx : (j + 1) * nx] for j in range(8)], axis=0)
        by_rhs = pltpu.einshape("abc->bac", by_row)
        cells = pl.ds(pl.multiple_of(y + MARGIN, 8), 8)
        here = pl.ds(group * 8, 8)
        iterate_out[:, 0, here] = iterate[:, 0, here] + by_rhs[:rhs] * inverse[plane + REACH, cells]
        residual_out[:, 0, here] = by_rhs[rhs:] * root[plane + REACH, cells]
        return carry

    lax.fori_loop(0, rows // 8, group_of_rows, 0, unroll=True)


def on_device(iterate, residual, labels, boundary):
    rhs, depth, rows, nx = residual.shape
    assert depth == 2 and REACH == 3 and rows % rhs == 0 and rhs % 8 == 0 and lax.axis_size("gz") % 2 == 0
    odd = (lax.axis_index("gz") % 2).astype(jnp.int32).reshape(1)
    vmem = pl.BlockSpec(memory_space=pltpu.VMEM)
    smem = pl.BlockSpec(memory_space=pltpu.SMEM)

    def array(*shape, dtype=f32):
        return jax.ShapeDtypeStruct(shape, dtype)

    def params(mib):
        return pltpu.CompilerParams(vmem_limit_bytes=mib * 2**20)

    anywhere = pl.BlockSpec(memory_space=pl.ANY)

    count = rows // rhs
    hbm = pl.BlockSpec(memory_space=pltpu.HBM)
    edge = (array(REACH, rhs, nx),) * 2
    plane_block = pltpu.VMEM((rhs, rows, nx), f32)
    mine, far_first, far_last = pl.pallas_call(
        far_kernel,
        out_shape=(array(rows + 4 * count, rhs, nx),) + edge,
        in_specs=[smem, hbm, hbm, hbm],
        out_specs=(vmem,) * 3,
        scratch_shapes=[
            plane_block,
            pltpu.VMEM(labels.shape, jnp.int32),
            pltpu.VMEM(boundary.shape, jnp.int32),
            pltpu.SemaphoreType.DMA((3,)),
        ],
        compiler_params=params(58),
    )(odd, residual, labels, boundary)
    ahead, near_first, near_last = pl.pallas_call(
        near_kernel,
        out_shape=(array(rows + 3 * count, rhs, nx),) + edge,
        in_specs=[smem, hbm, hbm],
        out_specs=(vmem,) * 3,
        scratch_shapes=[plane_block, pltpu.VMEM((4 * count, rhs, nx), f32), pltpu.SemaphoreType.DMA((2,))],
        compiler_params=params(52),
    )(odd, residual, mine)
    edges = jnp.stack([far_first, near_first]), jnp.stack([far_last, near_last])

    first_swap = swapped(mine)
    far3 = relayed(ahead)
    near3 = relayed(mine, back=True)
    own_before, own_behind = rows_beside(*edges)
    second = pl.pallas_call(
        partial(second_kernel, rows),
        out_shape=array(rows + 2, rhs, nx),
        in_specs=[vmem] * 3,
        out_specs=vmem,
        compiler_params=params(8),
    )(ahead, own_before, own_behind)
    def handed_on(block, earlier):
        return pl.pallas_call(
            hand_on,
            out_shape=array(*block.shape),
            in_specs=[anywhere] * 2,
            out_specs=anywhere,
            input_output_aliases={0: 0},
            compiler_params=params(8),
        )(block, earlier)

    near2 = handed_on(first_swap, second)
    near1 = swapped(handed_on(second, near2))
    def copied(number, first, source, *earlier):
        return pl.pallas_call(
            partial(copy_kernel, first),
            out_shape=array(number, rhs, nx),
            in_specs=[vmem] + [anywhere] * len(earlier),
            out_specs=vmem,
            compiler_params=params(8),
        )(source, *earlier)

    far1 = relayed(copied(rows, 0, near2, far3))
    beyond = swapped(copied(4 * count, rows, near3))
    far2 = relayed(near1)

    edges = EDGES + sum(part is not None for _, *parts in FIELDS for part in parts)
    before, behind = rows_beside(
        *pl.pallas_call(
            partial(edges_kernel, rows),
            out_shape=(array(edges, rhs, nx),) * 2,
            in_specs=[vmem] * 7,
            out_specs=(vmem, vmem),
            compiler_params=params(12),
        )(near1, near2, far1, beyond, far3, near3, mine)
    )

    def planes(number):
        return (number, rows + 2 * REACH, rhs, nx)

    cells = (depth + 2 * REACH, rows + 2 * MARGIN, nx)
    inverse, sx, sy, sz, root, u0, u1, u2, split01, moments = pl.pallas_call(
        partial(early_kernel, rows),
        out_shape=(array(*cells),) * 5
        + tuple(array(*planes(number)) for number in (3, 2, 2))
        + (array(depth, rows, 4 * rhs, nx, dtype=bf16), array(rhs, 128)),
        in_specs=[vmem] * 12,
        out_specs=(vmem,) * 10,
        scratch_shapes=[pltpu.VMEM(planes(number), f32) for number in (4, 2)]
        + [pltpu.VMEM((cells[0] + 2,) + cells[1:], f32)] * 2
        + [pltpu.VMEM(cells, f32)],
        compiler_params=params(24),
    )(far3, far1, beyond, mine, ahead, own_before, own_behind, near1, near2, near3, before, behind)

    moments, split23 = pl.pallas_call(
        partial(late_kernel, rows),
        out_shape=(array(rhs, 128), array(depth, rows, 4 * rhs, nx, dtype=bf16)),
        in_specs=[vmem] * 9,
        out_specs=(vmem, vmem),
        scratch_shapes=[pltpu.VMEM(planes(number), f32) for number in (1, 2, 2)],
        compiler_params=params(20),
    )(far2, u0, u1, u2, moments, inverse, sx, sy, sz)

    moments = all_sum(moments, ("gy", "gz"))

    tile = math.gcd(rows, 32)
    plane_rows = pl.BlockSpec((rhs, 1, tile, nx), lambda z, y, odd: (0, jnp.bitwise_xor(z, odd[0]), y, 0))
    return pl.pallas_call(
        outputs_kernel,
        out_shape=(array(*iterate.shape), array(*residual.shape)),
        grid_spec=pltpu.PrefetchScalarGridSpec(
            num_scalar_prefetch=1,
            grid=(depth, rows // tile),
            in_specs=[vmem] * 5 + [plane_rows],
            out_specs=(plane_rows, plane_rows),
            scratch_shapes=[pltpu.VMEM((4 * rhs, 8 * rhs), bf16)],
        ),
        compiler_params=params(16),
    )(odd, moments, split01, split23, inverse, root, iterate)


def solution(mesh):
    placed = (
        P(None, ("regions", "gz"), "gy", None),
        P(None, ("regions", "gz"), "gy", None),
        P(("regions", "gz"), "gy", None),
        P(("regions", "gz"), "gy", None),
    )
    return jax.shard_map(
        on_device,
        mesh=mesh,
        in_specs=placed,
        out_specs=(P(None, ("regions", "gz"), "gy", None), P(None, ("regions", "gz"), "gy", None)),
        check_vma=False,
    )
```

```python
import math
from functools import partial

import jax
import jax.numpy as jnp
from jax import lax
from jax.experimental import pallas as pl
from jax.experimental.pallas import tpu as pltpu
from jax.sharding import PartitionSpec as P

NCLASS = 8
ITERS = 3
REACH = ITERS

contrast_log = 4.0 * math.log(10.0)
highest = lax.Precision.HIGHEST
f32 = jnp.float32
bf16 = jnp.bfloat16


def moved(block, axis, pairs):
    return lax.ppermute(block, axis, pairs)


def shifted(block, axis, step):
    count = lax.axis_size(axis)
    return moved(block, axis, [(i, i + step) for i in range(count) if 0 <= i + step < count])


def swapped(block):
    return moved(block, "gz", [(i, i ^ 1) for i in range(lax.axis_size("gz"))])


def relayed(block, back=False):
    count = lax.axis_size("gz")
    steps = [(i, i + 2 - 4 * (i % 2)) for i in range(count)]
    pairs = [(i, j) for i, j in steps if 0 <= j < count]
    return moved(block, "gz", [(j, i) for i, j in pairs] if back else pairs)


def rows_beside(before, after):
    count = lax.axis_size("gy")
    if count != 2:
        return shifted(after, "gy", 1), shifted(before, "gy", -1)
    second = lax.axis_index("gy") == 1
    other = moved(jnp.where(second, before, after), "gy", [(0, 1), (1, 0)])
    zero = jnp.zeros_like(other)
    return jnp.where(second, other, zero), jnp.where(second, zero, other)


def all_sum(values, axes):
    for axis in axes:
        count = lax.axis_size(axis)
        if count & (count - 1):
            values = lax.psum(values, axis)
            continue
        step = 1
        while step < count:
            values = values + lax.ppermute(values, axis, [(i, i ^ step) for i in range(count)])
            step *= 2
    return values


def face_of(center, beside):
    return jnp.where(beside > 0.0, 2.0 * center * beside / (center + beside), center)


LATE = 1
BESIDE = ((5, 0, 2), (6, 2, 1), (2, 3, 2))
EDGES = 5
FIELDS = (
    ("far3", 0, None), ("far3", 1, 2), ("beyond", 1, 3), ("beyond", 0, 2), ("mine", 0, 2),
    ("mine", 1, 3), ("near2", 1, 3), ("near2", 0, 2), ("near3", 0, 2), ("near3", 1, None),
)
MARGIN = 8


def turn_plane(block, out):
    def turn(group, carry):
        here = pl.ds(group * 8, 8)
        out[here] = pltpu.einshape("abc->bac", block[:, here, :])
        return carry

    lax.fori_loop(0, block.shape[1] // 8, turn, 0)


def far_kernel(odd, residual, labels, boundary, mine, first, last, block, label_cells, boundary_cells, arrived):
    rhs, depth, rows, nx = residual.shape
    copies = [
        pltpu.make_async_copy(labels, label_cells, arrived.at[0]),
        pltpu.make_async_copy(boundary, boundary_cells, arrived.at[1]),
        pltpu.make_async_copy(residual.at[:, odd[0]], block, arrived.at[2]),
    ]
    for copy in copies:
        copy.start()
    for copy in copies[:2]:
        copy.wait()
    count = rows // rhs
    for place in range(depth):
        plane = jnp.bitwise_xor(place, odd[0])
        for part in range(count):
            cells = pl.ds(part * rhs, rhs)
            mine[rows + place * count + part] = jnp.exp(
                label_cells[plane, cells, :].astype(f32) * (contrast_log / (NCLASS - 1))
            )
            mine[rows + (2 + place) * count + part] = (1 - boundary_cells[plane, cells, :]).astype(f32)
    copies[2].wait()
    turn_plane(block, mine)
    first[...] = mine[:REACH]
    last[...] = mine[rows - REACH : rows]


def near_kernel(odd, residual, mine, ahead, first, last, block, cells, arrived):
    rhs, _, rows, _ = residual.shape
    copies = [
        pltpu.make_async_copy(mine.at[pl.ds(rows, cells.shape[0])], cells, arrived.at[0]),
        pltpu.make_async_copy(residual.at[:, 1 - odd[0]], block, arrived.at[1]),
    ]
    for copy in copies:
        copy.start()
    copies[0].wait()
    count = rows // rhs
    for part in range(2 * count):
        ahead[rows + part] = cells[part]
    for part in range(count):
        ahead[rows + 2 * count + part] = cells[3 * count + part]
    copies[1].wait()
    turn_plane(block, ahead)
    first[...] = ahead[:REACH]
    last[...] = ahead[rows - REACH : rows]


def hand_on(message, earlier, out):
    del message, earlier, out


def second_kernel(rows, ahead, own_before, own_behind, out):
    def copy_rows(y, size):
        for j in range(size):
            out[y + j] = ahead[y + j]

    row_blocks(0, rows, copy_rows, 16)
    out[rows] = own_before[1, REACH - 1]
    out[rows + 1] = own_behind[1, 0]


def copy_kernel(first, source, *rest):
    out = rest[-1]

    def copy_rows(y, size):
        for j in range(size):
            out[y + j] = source[first + y + j]

    row_blocks(0, out.shape[0], copy_rows, 16)


def edges_kernel(rows, near1, near2, far1, beyond, far3, near3, mine, first, last):
    messages = {"near2": near2, "beyond": beyond, "far3": far3, "near3": near3, "mine": mine}
    rhs = mine.shape[1]
    count = rows // rhs
    for (_, place, number), source in zip(BESIDE, (near1, near2, far1)):
        first[place : place + number] = source[:number]
        last[place : place + number] = source[rows - number : rows]
    place = EDGES
    for name, *parts in FIELDS:
        for part in parts:
            if part is not None:
                start = part * count + (rows if name != "beyond" else 0)
                first[place, :MARGIN] = messages[name][start, :MARGIN]
                last[place, :MARGIN] = messages[name][start + count - 1, rhs - MARGIN :]
                place += 1
                first[place - 1, MARGIN:] = jnp.zeros_like(first[place - 1, MARGIN:])
                last[place - 1, MARGIN:] = jnp.zeros_like(last[place - 1, MARGIN:])


def fill_cells(rows, messages, before, behind, coef, inner):
    place = EDGES
    for plane, (name, *parts) in enumerate(FIELDS):
        for part, out in zip(parts, (coef, inner)):
            if part is None:
                continue
            rhs = messages[name].shape[1]
            count = rows // rhs
            first = rows if name != "beyond" else 0
            for block in range(count):
                out[plane, MARGIN + block * rhs : MARGIN + (block + 1) * rhs] = messages[name][
                    first + part * count + block
                ]
            out[plane, :MARGIN] = before[place, :MARGIN]
            out[plane, MARGIN + rows :] = behind[place, :MARGIN]
            place += 1


def make_operator(coef, inner, inverse, sx, sy, sz, root, masked):
    planes, height, nx = inverse.shape
    lane = lax.broadcasted_iota(jnp.int32, (height, nx), 1)
    inside = lane < nx - 1

    def one_plane(plane, carry):
        here = coef[plane + 1]
        flag = inner[plane + 1]
        right = jnp.where(inside, pltpu.roll(here, nx - 1, 1), 0.0)
        left = jnp.where(lane > 0, pltpu.roll(here, 1, 1), 0.0)
        behind, before = pltpu.roll(here, height - 1, 0), pltpu.roll(here, 1, 0)
        along_x, along_y = face_of(here, right), face_of(here, behind)
        along_z = face_of(here, coef[plane + 2])
        total = along_x + jnp.where(left > 0.0, pltpu.roll(along_x, 1, 1), here)
        total += along_y + jnp.where(before > 0.0, pltpu.roll(along_y, 1, 0), here)
        total += along_z + face_of(here, coef[plane])
        diagonal = flag * total + (1.0 - flag)
        square = jnp.sqrt(diagonal)
        reciprocal = 1.0 / square
        root[plane] = square
        inverse[plane] = reciprocal
        scale = flag * reciprocal
        masked[plane] = scale
        sx[plane] = jnp.where(inside, scale * along_x * pltpu.roll(scale, nx - 1, 1), 0.0)
        sy[plane] = scale * along_y * pltpu.roll(scale, height - 1, 0)
        sz[plane] = scale * along_z
        return carry

    lax.fori_loop(0, planes, one_plane, 0)

    def next_plane(plane, carry):
        sz[plane] = sz[plane] * masked[plane + 1]
        return carry

    lax.fori_loop(0, planes - 1, next_plane, 0)


def cell_row(ref, plane, y):
    return ref[plane, pl.ds(y + (MARGIN - REACH), 1), :]


def row_blocks(start, stop, body, size, unroll=1):
    blocks = -(-(stop - start) // size)
    size = -(-(stop - start) // blocks)

    def step(block, carry):
        body(jnp.minimum(start + block * size, stop - size), size)
        return carry

    lax.fori_loop(0, blocks, step, 0, unroll=min(unroll, blocks))


def apply_rows(operator, plane, start, before, here, after, size):
    sx, sy, sz = operator
    ref, index = here
    out = []
    last, center = ref[index, start - 1], ref[index, start]
    below = cell_row(sy, plane, start - 1)
    width = center.shape[-1]
    for j in range(size):
        y = start + j
        following = ref[index, y + 1]
        above = cell_row(sy, plane, y)
        ahead = cell_row(sx, plane, y)
        total = ahead * pltpu.roll(center, width - 1, 1) + pltpu.roll(ahead * center, 1, 1)
        total += above * following + below * last
        total += cell_row(sz, plane, y) * after[0][after[1], y]
        total += cell_row(sz, plane - 1, y) * before[0][before[1], y]
        out.append(total)
        last, center, below = center, following, above
    return out


def spread(plane, depth=2):
    return max(REACH - plane, plane - (REACH + depth - 1), 0)


def scale_rows(plane, source, first, dst, start, count, inverse):
    out, place = dst

    def body(j, size):
        for i in range(size):
            out[place, start + j + i] = source[first + j + i] * cell_row(inverse, plane, start + j + i)

    if count < 8:
        body(0, count)
    else:
        row_blocks(0, count, body, 16)


def apply_plane(rows, power, plane, operator, fields, unroll=1):
    reach = REACH - power - spread(plane)
    src = [fields[power - 1, plane + offset] for offset in (-1, 0, 1)]
    out, place = fields[power, plane]

    def body(y, size):
        for j, values in enumerate(apply_rows(operator, plane, y, *src, size)):
            out[place, y + j] = values

    row_blocks(REACH - reach, REACH + rows + reach, body, 34, unroll)


def halves(blocks):
    stack = jnp.concatenate(blocks, axis=0)
    high = stack.astype(bf16)
    low = (stack - high.astype(f32)).astype(bf16)
    return jnp.concatenate([high, low], axis=0)


def inner_products(left, right):
    return lax.dot_general(left, right, (((1,), (1,)), ((), ())), preferred_element_type=f32)


def whole(gram, left, right):
    gram = gram[:left] + gram[left : 2 * left]
    return gram[:, :right] + gram[:, right : 2 * right]


def early_kernel(
    rows, far3, far1, beyond, mine, ahead, own_before, own_behind, near1, near2, near3, before, behind,
    inverse, sx, sy, sz, root, u0_out, u1_out, u2_out, split, moments, u0, u1, coef, inner, masked,
):
    messages = {"near2": near2, "beyond": beyond, "far3": far3, "near3": near3, "mine": mine}
    fill_cells(rows, messages, before, behind, coef, inner)
    make_operator(coef, inner, inverse, sx, sy, sz, root, masked)
    operator = (sx, sy, sz)
    fields = {(0, plane): (u0_out, index) for index, plane in enumerate((0, 2, 3))}
    fields.update({(0, plane): (u0, plane - 4) for plane in range(4, 8)})
    fields.update({(1, 3): (u1_out, 0), (1, 4): (u1_out, 1), (1, 5): (u1, 0), (1, 6): (u1, 1)})
    fields.update({(2, 4): (u2_out, 0), (2, 5): (u2_out, 1)})
    first, last = REACH, REACH + rows
    for plane, source in ((0, far3), (2, far1), (3, mine), (4, ahead), (5, near1), (6, near2), (7, near3)):
        scale_rows(plane, source, 0, fields[0, plane], first, rows, inverse)
    for plane in (3, 4):
        scale_rows(plane, own_before.at[plane - 3], 0, fields[0, plane], 0, REACH, inverse)
        scale_rows(plane, own_behind.at[plane - 3], 0, fields[0, plane], last, REACH, inverse)
    for plane, place, count in BESIDE:
        scale_rows(plane, before, place, fields[0, plane], first - count, count, inverse)
        scale_rows(plane, behind, place, fields[0, plane], last, count, inverse)
    for power, plane in ((1, 3), (1, 4), (1, 5), (1, 6), (2, 4), (2, 5)):
        apply_plane(rows, power, plane, operator, fields)

    rhs = u0.shape[2]
    gram = jnp.zeros((4 * rhs, 4 * rhs), f32)
    for plane in range(2):

        def gram_rows(block, total, plane=plane):
            for group in range(4):
                parts = []
                for j in range(4):
                    y = block * 16 + group * 4 + j
                    sources = [fields[power, plane + REACH] for power in range(2)]
                    both = halves([ref[index, y + REACH] for ref, index in sources])
                    split[plane, y] = both
                    parts.append(both)
                wide = jnp.concatenate(parts, axis=1)
                total = total + inner_products(wide, wide)
            return total

        gram = lax.fori_loop(0, rows // 16, gram_rows, gram)
    gram = whole(gram, 2 * rhs, 2 * rhs)
    moments[:, : 2 * rhs] = gram[:rhs]
    moments[:, 2 * rhs : 3 * rhs] = gram[rhs:, rhs:]


def late_kernel(
    rows, far2, u0_in, u1_in, u2_in, moments_in, inverse, sx, sy, sz, moments, split, u0, u1, u2
):
    operator = (sx, sy, sz)
    fields = {(0, plane): (u0_in, index) for index, plane in enumerate((0, 2, 3))}
    fields[0, LATE] = (u0, 0)
    fields.update({(1, 1): (u1, 0), (1, 2): (u1, 1), (1, 3): (u1_in, 0), (1, 4): (u1_in, 1)})
    fields.update({(2, 2): (u2, 0), (2, 3): (u2, 1), (2, 4): (u2_in, 0), (2, 5): (u2_in, 1)})
    first, last = REACH, REACH + rows
    for place, start, count in ((0, first, rows), (rows, first - 1, 1), (rows + 1, last, 1)):
        scale_rows(LATE, far2, place, fields[0, LATE], start, count, inverse)
    for power, plane in ((1, 1), (1, 2), (2, 2), (2, 3)):
        apply_plane(rows, power, plane, operator, fields, 2)

    rhs = u0.shape[2]
    gram = jnp.zeros((6 * rhs, 2 * rhs), f32)
    for plane in range(2):
        level = plane + REACH

        def gram_rows(block, total, plane=plane, level=level):
            start = block * 16
            y = start + REACH
            last = apply_rows(operator, level, y, *[fields[2, level + offset] for offset in (-1, 0, 1)], 16)
            for group in range(4):
                left, right = [], []
                for j in range(group * 4, group * 4 + 4):
                    ref, index = fields[2, level]
                    both = halves([ref[index, y + j], last[j]])
                    split[plane, start + j] = both
                    left.append(jnp.concatenate([halves([u1_in[plane, y + j]]), both], axis=0))
                    right.append(jnp.concatenate([both[:rhs], both[2 * rhs : 3 * rhs]], axis=0))
                total = total + inner_products(jnp.concatenate(left, axis=1), jnp.concatenate(right, axis=1))
            return total

        gram = lax.fori_loop(0, rows // 16, gram_rows, gram, unroll=2)
    gram = gram[:, :rhs] + gram[:, rhs:]
    blocks = [gram[part * rhs : (part + 1) * rhs] for part in range(6)]
    moments[:, : 3 * rhs] = moments_in[:, : 3 * rhs]
    moments[:, 3 * rhs : 4 * rhs] = blocks[0] + blocks[1]
    moments[:, 4 * rhs : 5 * rhs] = blocks[2] + blocks[4]
    moments[:, 5 * rhs : 6 * rhs] = blocks[3] + blocks[5]
    moments[:, 6 * rhs :] = jnp.zeros((rhs, moments.shape[1] - 6 * rhs), f32)


def inverse_of_pair(a, b, c, d):
    scale = 1.0 / (a * d - b * c)
    return d * scale, -b * scale, -c * scale, a * scale


def times(p, q):
    a, b, c, d = p
    e, f, g, h = q
    return a * e + b * g, a * f + b * h, c * e + d * g, c * f + d * h


def inverse_of_four(m):
    p, q = (m[0][0], m[0][1], m[1][0], m[1][1]), (m[0][2], m[0][3], m[1][2], m[1][3])
    r, s = (m[2][0], m[2][1], m[3][0], m[3][1]), (m[2][2], m[2][3], m[3][2], m[3][3])
    inner = inverse_of_pair(*p)
    right, left = times(inner, q), times(r, inner)
    outer = inverse_of_pair(*[x - y for x, y in zip(s, times(r, right))])
    lower = [-x for x in times(outer, left)]
    upper = [-x for x in times(right, outer)]
    corner = [x - y for x, y in zip(inner, times(right, lower))]
    return (
        (corner[0], corner[1], upper[0], upper[1]),
        (corner[2], corner[3], upper[2], upper[3]),
        (lower[0], lower[1], outer[0], outer[1]),
        (lower[2], lower[3], outer[2], outer[3]),
    )


def eliminate(stacked, size):
    tiles, height, width = stacked.shape
    lane = lax.broadcasted_iota(jnp.int32, (height, width), 1)

    def everywhere(row):
        return jnp.broadcast_to(row, (height, width))

    for k in range(0, size, 4):
        if k and k % height == 0:
            stacked = stacked[1:]
        at = k % height
        rows = [everywhere(stacked[0, at + i : at + i + 1]) for i in range(4)]
        columns = [jnp.broadcast_to(stacked[:, :, k + i : k + i + 1], stacked.shape) for i in range(4)]
        block = [[everywhere(columns[j][0, at + i : at + i + 1]) for j in range(4)] for i in range(4)]
        inverse = inverse_of_four(block)
        pivots = (lane >= k) & (lane < k + 4)
        result = jnp.where(pivots[None], 0.0, stacked)
        for i in range(4):
            mix = (inverse[i][0] * rows[0] + inverse[i][1] * rows[1]) + (
                inverse[i][2] * rows[2] + inverse[i][3] * rows[3]
            )
            for j in range(4):
                mix = jnp.where(lane == k + j, -inverse[i][j], mix)
            result = result - columns[i] * mix[None]
        stacked = result
    return stacked[1:]


def mixing(moments, rhs):
    width = moments.shape[1]
    lane = lax.broadcasted_iota(jnp.int32, (rhs, width), 1)
    row = lax.broadcasted_iota(jnp.int32, (rhs, width), 0)
    size = REACH * rhs
    rolled = [moments] + [pltpu.roll(moments, width - i * rhs, 1) for i in range(1, REACH + 1)]
    energy = [rolled[i] - rolled[i + 1] for i in range(REACH)]
    tiles = jnp.concatenate(energy + [moments], axis=0).reshape(-1, 8, width)
    solved = eliminate(tiles, size).reshape(rhs, width)
    solved = jnp.where(lane < size, solved, 0.0)
    residual = (row == lane).astype(f32) - (solved - pltpu.roll(solved, rhs, 1))
    return solved, residual


def outputs_kernel(odd, moments, split01, split23, inverse, root, iterate, iterate_out, residual_out, coefs):
    rhs, _, rows, nx = iterate.shape
    plane, block = pl.program_id(0), pl.program_id(1)

    @pl.when((plane == 0) & (block == 0))
    def _():
        solved, residual = mixing(moments[...], rhs)
        both = jnp.concatenate([solved[:, : 4 * rhs], residual[:, : 4 * rhs]], axis=0)
        high = both.astype(bf16).astype(f32)
        stacked = jnp.concatenate([high, both - high], axis=0)
        pair01, pair23 = stacked[:, : 2 * rhs], stacked[:, 2 * rhs :]
        coefs[...] = jnp.concatenate([pair01, pair01, pair23, pair23], axis=1).astype(bf16)

    def group_of_rows(group, carry):
        y = block * rows + group * 8
        wide = jnp.concatenate(
            [jnp.concatenate([split01[plane, y + j], split23[plane, y + j]], axis=0) for j in range(8)], axis=1
        )
        mixed = jnp.dot(coefs[...], wide, preferred_element_type=f32)
        mixed = mixed[: 2 * rhs] + mixed[2 * rhs :]
        by_row = jnp.stack([mixed[:, j * nx : (j + 1) * nx] for j in range(8)], axis=0)
        by_rhs = pltpu.einshape("abc->bac", by_row)
        cells = pl.ds(pl.multiple_of(y + MARGIN, 8), 8)
        here = pl.ds(group * 8, 8)
        iterate_out[:, 0, here] = iterate[:, 0, here] + by_rhs[:rhs] * inverse[plane + REACH, cells]
        residual_out[:, 0, here] = by_rhs[rhs:] * root[plane + REACH, cells]
        return carry

    lax.fori_loop(0, rows // 8, group_of_rows, 0, unroll=True)


def on_device(iterate, residual, labels, boundary):
    rhs, depth, rows, nx = residual.shape
    assert depth == 2 and REACH == 3 and rows % rhs == 0 and rhs % 8 == 0 and lax.axis_size("gz") % 2 == 0
    odd = (lax.axis_index("gz") % 2).astype(jnp.int32).reshape(1)
    vmem = pl.BlockSpec(memory_space=pltpu.VMEM)
    smem = pl.BlockSpec(memory_space=pltpu.SMEM)

    def array(*shape, dtype=f32):
        return jax.ShapeDtypeStruct(shape, dtype)

    def params(mib):
        return pltpu.CompilerParams(vmem_limit_bytes=mib * 2**20)

    anywhere = pl.BlockSpec(memory_space=pl.ANY)

    count = rows // rhs
    hbm = pl.BlockSpec(memory_space=pltpu.HBM)
    edge = (array(REACH, rhs, nx),) * 2
    plane_block = pltpu.VMEM((rhs, rows, nx), f32)
    mine, far_first, far_last = pl.pallas_call(
        far_kernel,
        out_shape=(array(rows + 4 * count, rhs, nx),) + edge,
        in_specs=[smem, hbm, hbm, hbm],
        out_specs=(vmem,) * 3,
        scratch_shapes=[
            plane_block,
            pltpu.VMEM(labels.shape, jnp.int32),
            pltpu.VMEM(boundary.shape, jnp.int32),
            pltpu.SemaphoreType.DMA((3,)),
        ],
        compiler_params=params(58),
    )(odd, residual, labels, boundary)
    ahead, near_first, near_last = pl.pallas_call(
        near_kernel,
        out_shape=(array(rows + 3 * count, rhs, nx),) + edge,
        in_specs=[smem, hbm, hbm],
        out_specs=(vmem,) * 3,
        scratch_shapes=[plane_block, pltpu.VMEM((4 * count, rhs, nx), f32), pltpu.SemaphoreType.DMA((2,))],
        compiler_params=params(52),
    )(odd, residual, mine)
    edges = jnp.stack([far_first, near_first]), jnp.stack([far_last, near_last])

    first_swap = swapped(mine)
    far3 = relayed(ahead)
    near3 = relayed(mine, back=True)
    own_before, own_behind = rows_beside(*edges)
    second = pl.pallas_call(
        partial(second_kernel, rows),
        out_shape=array(rows + 2, rhs, nx),
        in_specs=[vmem] * 3,
        out_specs=vmem,
        compiler_params=params(8),
    )(ahead, own_before, own_behind)
    def handed_on(block, earlier):
        return pl.pallas_call(
            hand_on,
            out_shape=array(*block.shape),
            in_specs=[anywhere] * 2,
            out_specs=anywhere,
            input_output_aliases={0: 0},
            compiler_params=params(8),
        )(block, earlier)

    near2 = handed_on(first_swap, second)
    near1 = swapped(handed_on(second, near2))
    def copied(number, first, source, *earlier):
        return pl.pallas_call(
            partial(copy_kernel, first),
            out_shape=array(number, rhs, nx),
            in_specs=[vmem] + [anywhere] * len(earlier),
            out_specs=vmem,
            compiler_params=params(8),
        )(source, *earlier)

    far1 = relayed(copied(rows, 0, near2))
    beyond = swapped(copied(4 * count, rows, near3, far3))
    far2 = relayed(near1)

    edges = EDGES + sum(part is not None for _, *parts in FIELDS for part in parts)
    before, behind = rows_beside(
        *pl.pallas_call(
            partial(edges_kernel, rows),
            out_shape=(array(edges, rhs, nx),) * 2,
            in_specs=[vmem] * 7,
            out_specs=(vmem, vmem),
            compiler_params=params(12),
        )(near1, near2, far1, beyond, far3, near3, mine)
    )

    def planes(number):
        return (number, rows + 2 * REACH, rhs, nx)

    cells = (depth + 2 * REACH, rows + 2 * MARGIN, nx)
    inverse, sx, sy, sz, root, u0, u1, u2, split01, moments = pl.pallas_call(
        partial(early_kernel, rows),
        out_shape=(array(*cells),) * 5
        + tuple(array(*planes(number)) for number in (3, 2, 2))
        + (array(depth, rows, 4 * rhs, nx, dtype=bf16), array(rhs, 128)),
        in_specs=[vmem] * 12,
        out_specs=(vmem,) * 10,
        scratch_shapes=[pltpu.VMEM(planes(number), f32) for number in (4, 2)]
        + [pltpu.VMEM((cells[0] + 2,) + cells[1:], f32)] * 2
        + [pltpu.VMEM(cells, f32)],
        compiler_params=params(24),
    )(far3, far1, beyond, mine, ahead, own_before, own_behind, near1, near2, near3, before, behind)

    moments, split23 = pl.pallas_call(
        partial(late_kernel, rows),
        out_shape=(array(rhs, 128), array(depth, rows, 4 * rhs, nx, dtype=bf16)),
        in_specs=[vmem] * 9,
        out_specs=(vmem, vmem),
        scratch_shapes=[pltpu.VMEM(planes(number), f32) for number in (1, 2, 2)],
        compiler_params=params(20),
    )(far2, u0, u1, u2, moments, inverse, sx, sy, sz)

    moments = all_sum(moments, ("gy", "gz"))

    tile = math.gcd(rows, 32)
    plane_rows = pl.BlockSpec((rhs, 1, tile, nx), lambda z, y, odd: (0, jnp.bitwise_xor(z, odd[0]), y, 0))
    return pl.pallas_call(
        outputs_kernel,
        out_shape=(array(*iterate.shape), array(*residual.shape)),
        grid_spec=pltpu.PrefetchScalarGridSpec(
            num_scalar_prefetch=1,
            grid=(depth, rows // tile),
            in_specs=[vmem] * 5 + [plane_rows],
            out_specs=(plane_rows, plane_rows),
            scratch_shapes=[pltpu.VMEM((4 * rhs, 8 * rhs), bf16)],
        ),
        compiler_params=params(16),
    )(odd, moments, split01, split23, inverse, root, iterate)


def solution(mesh):
    placed = (
        P(None, ("regions", "gz"), "gy", None),
        P(None, ("regions", "gz"), "gy", None),
        P(("regions", "gz"), "gy", None),
        P(("regions", "gz"), "gy", None),
    )
    return jax.shard_map(
        on_device,
        mesh=mesh,
        in_specs=placed,
        out_specs=(P(None, ("regions", "gz"), "gy", None), P(None, ("regions", "gz"), "gy", None)),
        check_vma=False,
    )
```

```python
import math
from functools import partial

import jax
import jax.numpy as jnp
from jax import lax
from jax.experimental import pallas as pl
from jax.experimental.pallas import tpu as pltpu
from jax.sharding import PartitionSpec as P

NCLASS = 8
ITERS = 3
REACH = ITERS

contrast_log = 4.0 * math.log(10.0)
highest = lax.Precision.HIGHEST
f32 = jnp.float32
bf16 = jnp.bfloat16


def moved(block, axis, pairs):
    return lax.ppermute(block, axis, pairs)


def shifted(block, axis, step):
    count = lax.axis_size(axis)
    return moved(block, axis, [(i, i + step) for i in range(count) if 0 <= i + step < count])


def swapped(block):
    return moved(block, "gz", [(i, i ^ 1) for i in range(lax.axis_size("gz"))])


def relayed(block, back=False):
    count = lax.axis_size("gz")
    steps = [(i, i + 2 - 4 * (i % 2)) for i in range(count)]
    pairs = [(i, j) for i, j in steps if 0 <= j < count]
    return moved(block, "gz", [(j, i) for i, j in pairs] if back else pairs)


def rows_beside(before, after):
    count = lax.axis_size("gy")
    if count != 2:
        return shifted(after, "gy", 1), shifted(before, "gy", -1)
    second = lax.axis_index("gy") == 1
    other = moved(jnp.where(second, before, after), "gy", [(0, 1), (1, 0)])
    zero = jnp.zeros_like(other)
    return jnp.where(second, other, zero), jnp.where(second, zero, other)


def all_sum(values, axes):
    for axis in axes:
        count = lax.axis_size(axis)
        if count & (count - 1):
            values = lax.psum(values, axis)
            continue
        step = 1
        while step < count:
            values = values + lax.ppermute(values, axis, [(i, i ^ step) for i in range(count)])
            step *= 2
    return values


def face_of(center, beside):
    return jnp.where(beside > 0.0, 2.0 * center * beside / (center + beside), center)


LATE = 1
BESIDE = ((5, 0, 2), (6, 2, 1), (2, 3, 2))
EDGES = 5
FIELDS = (
    ("far3", 0, None), ("far3", 1, 2), ("beyond", 1, 3), ("beyond", 0, 2), ("mine", 0, 2),
    ("mine", 1, 3), ("near2", 1, 3), ("near2", 0, 2), ("near3", 0, 2), ("near3", 1, None),
)
MARGIN = 8


def turn_plane(block, out):
    def turn(group, carry):
        here = pl.ds(group * 8, 8)
        out[here] = pltpu.einshape("abc->bac", block[:, here, :])
        return carry

    lax.fori_loop(0, block.shape[1] // 8, turn, 0)


def far_kernel(odd, residual, labels, boundary, mine, first, last, block, label_cells, boundary_cells, arrived):
    rhs, depth, rows, nx = residual.shape
    copies = [
        pltpu.make_async_copy(labels, label_cells, arrived.at[0]),
        pltpu.make_async_copy(boundary, boundary_cells, arrived.at[1]),
        pltpu.make_async_copy(residual.at[:, odd[0]], block, arrived.at[2]),
    ]
    for copy in copies:
        copy.start()
    for copy in copies[:2]:
        copy.wait()
    count = rows // rhs
    for place in range(depth):
        plane = jnp.bitwise_xor(place, odd[0])
        for part in range(count):
            cells = pl.ds(part * rhs, rhs)
            mine[rows + place * count + part] = jnp.exp(
                label_cells[plane, cells, :].astype(f32) * (contrast_log / (NCLASS - 1))
            )
            mine[rows + (2 + place) * count + part] = (1 - boundary_cells[plane, cells, :]).astype(f32)
    copies[2].wait()
    turn_plane(block, mine)
    first[...] = mine[:REACH]
    last[...] = mine[rows - REACH : rows]


def near_kernel(odd, residual, mine, ahead, first, last, block, cells, arrived):
    rhs, _, rows, _ = residual.shape
    copies = [
        pltpu.make_async_copy(mine.at[pl.ds(rows, cells.shape[0])], cells, arrived.at[0]),
        pltpu.make_async_copy(residual.at[:, 1 - odd[0]], block, arrived.at[1]),
    ]
    for copy in copies:
        copy.start()
    copies[0].wait()
    count = rows // rhs
    for part in range(2 * count):
        ahead[rows + part] = cells[part]
    for part in range(count):
        ahead[rows + 2 * count + part] = cells[3 * count + part]
    copies[1].wait()
    turn_plane(block, ahead)
    first[...] = ahead[:REACH]
    last[...] = ahead[rows - REACH : rows]


def hand_on(message, earlier, out):
    del message, earlier, out


def second_kernel(rows, ahead, own_before, own_behind, out):
    def copy_rows(y, size):
        for j in range(size):
            out[y + j] = ahead[y + j]

    row_blocks(0, rows, copy_rows, 16)
    out[rows] = own_before[1, REACH - 1]
    out[rows + 1] = own_behind[1, 0]


def copy_kernel(first, source, *rest):
    out = rest[-1]

    def copy_rows(y, size):
        for j in range(size):
            out[y + j] = source[first + y + j]

    row_blocks(0, out.shape[0], copy_rows, 16)


def edges_kernel(rows, near1, near2, far1, beyond, far3, near3, mine, first, last):
    messages = {"near2": near2, "beyond": beyond, "far3": far3, "near3": near3, "mine": mine}
    rhs = mine.shape[1]
    count = rows // rhs
    for (_, place, number), source in zip(BESIDE, (near1, near2, far1)):
        first[place : place + number] = source[:number]
        last[place : place + number] = source[rows - number : rows]
    place = EDGES
    for name, *parts in FIELDS:
        for part in parts:
            if part is not None:
                start = part * count + (rows if name != "beyond" else 0)
                first[place, :MARGIN] = messages[name][start, :MARGIN]
                last[place, :MARGIN] = messages[name][start + count - 1, rhs - MARGIN :]
                place += 1
                first[place - 1, MARGIN:] = jnp.zeros_like(first[place - 1, MARGIN:])
                last[place - 1, MARGIN:] = jnp.zeros_like(last[place - 1, MARGIN:])


def fill_cells(rows, messages, before, behind, coef, inner):
    place = EDGES
    for plane, (name, *parts) in enumerate(FIELDS):
        for part, out in zip(parts, (coef, inner)):
            if part is None:
                continue
            rhs = messages[name].shape[1]
            count = rows // rhs
            first = rows if name != "beyond" else 0
            for block in range(count):
                out[plane, MARGIN + block * rhs : MARGIN + (block + 1) * rhs] = messages[name][
                    first + part * count + block
                ]
            out[plane, :MARGIN] = before[place, :MARGIN]
            out[plane, MARGIN + rows :] = behind[place, :MARGIN]
            place += 1


def make_operator(coef, inner, inverse, sx, sy, sz, root, masked):
    planes, height, nx = inverse.shape
    lane = lax.broadcasted_iota(jnp.int32, (height, nx), 1)
    inside = lane < nx - 1

    def one_plane(plane, carry):
        here = coef[plane + 1]
        flag = inner[plane + 1]
        right = jnp.where(inside, pltpu.roll(here, nx - 1, 1), 0.0)
        left = jnp.where(lane > 0, pltpu.roll(here, 1, 1), 0.0)
        behind, before = pltpu.roll(here, height - 1, 0), pltpu.roll(here, 1, 0)
        along_x, along_y = face_of(here, right), face_of(here, behind)
        along_z = face_of(here, coef[plane + 2])
        total = along_x + jnp.where(left > 0.0, pltpu.roll(along_x, 1, 1), here)
        total += along_y + jnp.where(before > 0.0, pltpu.roll(along_y, 1, 0), here)
        total += along_z + face_of(here, coef[plane])
        diagonal = flag * total + (1.0 - flag)
        square = jnp.sqrt(diagonal)
        reciprocal = 1.0 / square
        root[plane] = square
        inverse[plane] = reciprocal
        scale = flag * reciprocal
        masked[plane] = scale
        sx[plane] = jnp.where(inside, scale * along_x * pltpu.roll(scale, nx - 1, 1), 0.0)
        sy[plane] = scale * along_y * pltpu.roll(scale, height - 1, 0)
        sz[plane] = scale * along_z
        return carry

    lax.fori_loop(0, planes, one_plane, 0)

    def next_plane(plane, carry):
        sz[plane] = sz[plane] * masked[plane + 1]
        return carry

    lax.fori_loop(0, planes - 1, next_plane, 0)


def cell_row(ref, plane, y):
    return ref[plane, pl.ds(y + (MARGIN - REACH), 1), :]


def row_blocks(start, stop, body, size, unroll=1):
    blocks = -(-(stop - start) // size)
    size = -(-(stop - start) // blocks)

    def step(block, carry):
        body(jnp.minimum(start + block * size, stop - size), size)
        return carry

    lax.fori_loop(0, blocks, step, 0, unroll=min(unroll, blocks))


def apply_rows(operator, plane, start, before, here, after, size):
    sx, sy, sz = operator
    ref, index = here
    out = []
    last, center = ref[index, start - 1], ref[index, start]
    below = cell_row(sy, plane, start - 1)
    width = center.shape[-1]
    for j in range(size):
        y = start + j
        following = ref[index, y + 1]
        above = cell_row(sy, plane, y)
        ahead = cell_row(sx, plane, y)
        total = ahead * pltpu.roll(center, width - 1, 1) + pltpu.roll(ahead * center, 1, 1)
        total += above * following + below * last
        total += cell_row(sz, plane, y) * after[0][after[1], y]
        total += cell_row(sz, plane - 1, y) * before[0][before[1], y]
        out.append(total)
        last, center, below = center, following, above
    return out


def spread(plane, depth=2):
    return max(REACH - plane, plane - (REACH + depth - 1), 0)


def scale_rows(plane, source, first, dst, start, count, inverse):
    out, place = dst

    def body(j, size):
        for i in range(size):
            out[place, start + j + i] = source[first + j + i] * cell_row(inverse, plane, start + j + i)

    if count < 8:
        body(0, count)
    else:
        row_blocks(0, count, body, 16)


def apply_plane(rows, power, plane, operator, fields, unroll=1):
    reach = REACH - power - spread(plane)
    src = [fields[power - 1, plane + offset] for offset in (-1, 0, 1)]
    out, place = fields[power, plane]

    def body(y, size):
        for j, values in enumerate(apply_rows(operator, plane, y, *src, size)):
            out[place, y + j] = values

    row_blocks(REACH - reach, REACH + rows + reach, body, 34, unroll)


def halves(blocks):
    stack = jnp.concatenate(blocks, axis=0)
    high = stack.astype(bf16)
    low = (stack - high.astype(f32)).astype(bf16)
    return jnp.concatenate([high, low], axis=0)


def inner_products(left, right):
    return lax.dot_general(left, right, (((1,), (1,)), ((), ())), preferred_element_type=f32)


def whole(gram, left, right):
    gram = gram[:left] + gram[left : 2 * left]
    return gram[:, :right] + gram[:, right : 2 * right]


def early_kernel(
    rows, far3, far1, beyond, mine, ahead, own_before, own_behind, near1, near2, near3, before, behind,
    inverse, sx, sy, sz, root, u0_out, u1_out, u2_out, split, moments, u0, u1, coef, inner, masked,
):
    messages = {"near2": near2, "beyond": beyond, "far3": far3, "near3": near3, "mine": mine}
    fill_cells(rows, messages, before, behind, coef, inner)
    make_operator(coef, inner, inverse, sx, sy, sz, root, masked)
    operator = (sx, sy, sz)
    fields = {(0, plane): (u0_out, index) for index, plane in enumerate((0, 2, 3))}
    fields.update({(0, plane): (u0, plane - 4) for plane in range(4, 8)})
    fields.update({(1, 3): (u1_out, 0), (1, 4): (u1_out, 1), (1, 5): (u1, 0), (1, 6): (u1, 1)})
    fields.update({(2, 4): (u2_out, 0), (2, 5): (u2_out, 1)})
    first, last = REACH, REACH + rows
    for plane, source in ((0, far3), (2, far1), (3, mine), (4, ahead), (5, near1), (6, near2), (7, near3)):
        scale_rows(plane, source, 0, fields[0, plane], first, rows, inverse)
    for plane in (3, 4):
        scale_rows(plane, own_before.at[plane - 3], 0, fields[0, plane], 0, REACH, inverse)
        scale_rows(plane, own_behind.at[plane - 3], 0, fields[0, plane], last, REACH, inverse)
    for plane, place, count in BESIDE:
        scale_rows(plane, before, place, fields[0, plane], first - count, count, inverse)
        scale_rows(plane, behind, place, fields[0, plane], last, count, inverse)
    for power, plane in ((1, 3), (1, 4), (1, 5), (1, 6), (2, 4), (2, 5)):
        apply_plane(rows, power, plane, operator, fields)

    rhs = u0.shape[2]
    gram = jnp.zeros((4 * rhs, 4 * rhs), f32)
    for plane in range(2):

        def gram_rows(block, total, plane=plane):
            for group in range(4):
                parts = []
                for j in range(4):
                    y = block * 16 + group * 4 + j
                    sources = [fields[power, plane + REACH] for power in range(2)]
                    both = halves([ref[index, y + REACH] for ref, index in sources])
                    split[plane, y] = both
                    parts.append(both)
                wide = jnp.concatenate(parts, axis=1)
                total = total + inner_products(wide, wide)
            return total

        gram = lax.fori_loop(0, rows // 16, gram_rows, gram)
    gram = whole(gram, 2 * rhs, 2 * rhs)
    moments[:, : 2 * rhs] = gram[:rhs]
    moments[:, 2 * rhs : 3 * rhs] = gram[rhs:, rhs:]


def late_kernel(
    rows, far2, u0_in, u1_in, u2_in, moments_in, inverse, sx, sy, sz, moments, split, u0, u1, u2
):
    operator = (sx, sy, sz)
    fields = {(0, plane): (u0_in, index) for index, plane in enumerate((0, 2, 3))}
    fields[0, LATE] = (u0, 0)
    fields.update({(1, 1): (u1, 0), (1, 2): (u1, 1), (1, 3): (u1_in, 0), (1, 4): (u1_in, 1)})
    fields.update({(2, 2): (u2, 0), (2, 3): (u2, 1), (2, 4): (u2_in, 0), (2, 5): (u2_in, 1)})
    first, last = REACH, REACH + rows
    for place, start, count in ((0, first, rows), (rows, first - 1, 1), (rows + 1, last, 1)):
        scale_rows(LATE, far2, place, fields[0, LATE], start, count, inverse)
    for power, plane in ((1, 1), (1, 2), (2, 2), (2, 3)):
        apply_plane(rows, power, plane, operator, fields, 2)

    rhs = u0.shape[2]
    gram = jnp.zeros((6 * rhs, 2 * rhs), f32)
    for plane in range(2):
        level = plane + REACH

        def gram_rows(block, total, plane=plane, level=level):
            start = block * 16
            y = start + REACH
            last = apply_rows(operator, level, y, *[fields[2, level + offset] for offset in (-1, 0, 1)], 16)
            for group in range(4):
                left, right = [], []
                for j in range(group * 4, group * 4 + 4):
                    ref, index = fields[2, level]
                    both = halves([ref[index, y + j], last[j]])
                    split[plane, start + j] = both
                    left.append(jnp.concatenate([halves([u1_in[plane, y + j]]), both], axis=0))
                    right.append(jnp.concatenate([both[:rhs], both[2 * rhs : 3 * rhs]], axis=0))
                total = total + inner_products(jnp.concatenate(left, axis=1), jnp.concatenate(right, axis=1))
            return total

        gram = lax.fori_loop(0, rows // 16, gram_rows, gram, unroll=2)
    gram = gram[:, :rhs] + gram[:, rhs:]
    blocks = [gram[part * rhs : (part + 1) * rhs] for part in range(6)]
    moments[:, : 3 * rhs] = moments_in[:, : 3 * rhs]
    moments[:, 3 * rhs : 4 * rhs] = blocks[0] + blocks[1]
    moments[:, 4 * rhs : 5 * rhs] = blocks[2] + blocks[4]
    moments[:, 5 * rhs : 6 * rhs] = blocks[3] + blocks[5]
    moments[:, 6 * rhs :] = jnp.zeros((rhs, moments.shape[1] - 6 * rhs), f32)


def inverse_of_pair(a, b, c, d):
    scale = 1.0 / (a * d - b * c)
    return d * scale, -b * scale, -c * scale, a * scale


def times(p, q):
    a, b, c, d = p
    e, f, g, h = q
    return a * e + b * g, a * f + b * h, c * e + d * g, c * f + d * h


def inverse_of_four(m):
    p, q = (m[0][0], m[0][1], m[1][0], m[1][1]), (m[0][2], m[0][3], m[1][2], m[1][3])
    r, s = (m[2][0], m[2][1], m[3][0], m[3][1]), (m[2][2], m[2][3], m[3][2], m[3][3])
    inner = inverse_of_pair(*p)
    right, left = times(inner, q), times(r, inner)
    outer = inverse_of_pair(*[x - y for x, y in zip(s, times(r, right))])
    lower = [-x for x in times(outer, left)]
    upper = [-x for x in times(right, outer)]
    corner = [x - y for x, y in zip(inner, times(right, lower))]
    return (
        (corner[0], corner[1], upper[0], upper[1]),
        (corner[2], corner[3], upper[2], upper[3]),
        (lower[0], lower[1], outer[0], outer[1]),
        (lower[2], lower[3], outer[2], outer[3]),
    )


def eliminate(stacked, size):
    tiles, height, width = stacked.shape
    lane = lax.broadcasted_iota(jnp.int32, (height, width), 1)

    def everywhere(row):
        return jnp.broadcast_to(row, (height, width))

    for k in range(0, size, 4):
        if k and k % height == 0:
            stacked = stacked[1:]
        at = k % height
        rows = [everywhere(stacked[0, at + i : at + i + 1]) for i in range(4)]
        columns = [jnp.broadcast_to(stacked[:, :, k + i : k + i + 1], stacked.shape) for i in range(4)]
        block = [[everywhere(columns[j][0, at + i : at + i + 1]) for j in range(4)] for i in range(4)]
        inverse = inverse_of_four(block)
        pivots = (lane >= k) & (lane < k + 4)
        result = jnp.where(pivots[None], 0.0, stacked)
        for i in range(4):
            mix = (inverse[i][0] * rows[0] + inverse[i][1] * rows[1]) + (
                inverse[i][2] * rows[2] + inverse[i][3] * rows[3]
            )
            for j in range(4):
                mix = jnp.where(lane == k + j, -inverse[i][j], mix)
            result = result - columns[i] * mix[None]
        stacked = result
    return stacked[1:]


def mixing(moments, rhs):
    width = moments.shape[1]
    lane = lax.broadcasted_iota(jnp.int32, (rhs, width), 1)
    row = lax.broadcasted_iota(jnp.int32, (rhs, width), 0)
    size = REACH * rhs
    rolled = [moments] + [pltpu.roll(moments, width - i * rhs, 1) for i in range(1, REACH + 1)]
    energy = [rolled[i] - rolled[i + 1] for i in range(REACH)]
    tiles = jnp.concatenate(energy + [moments], axis=0).reshape(-1, 8, width)
    solved = eliminate(tiles, size).reshape(rhs, width)
    solved = jnp.where(lane < size, solved, 0.0)
    residual = (row == lane).astype(f32) - (solved - pltpu.roll(solved, rhs, 1))
    return solved, residual


def outputs_kernel(odd, moments, split01, split23, inverse, root, iterate, iterate_out, residual_out, coefs):
    rhs, _, rows, nx = iterate.shape
    plane, block = pl.program_id(0), pl.program_id(1)

    @pl.when((plane == 0) & (block == 0))
    def _():
        solved, residual = mixing(moments[...], rhs)
        both = jnp.concatenate([solved[:, : 4 * rhs], residual[:, : 4 * rhs]], axis=0)
        high = both.astype(bf16).astype(f32)
        stacked = jnp.concatenate([high, both - high], axis=0)
        pair01, pair23 = stacked[:, : 2 * rhs], stacked[:, 2 * rhs :]
        coefs[...] = jnp.concatenate([pair01, pair01, pair23, pair23], axis=1).astype(bf16)

    def group_of_rows(group, carry):
        y = block * rows + group * 8
        wide = jnp.concatenate(
            [jnp.concatenate([split01[plane, y + j], split23[plane, y + j]], axis=0) for j in range(8)], axis=1
        )
        mixed = jnp.dot(coefs[...], wide, preferred_element_type=f32)
        mixed = mixed[: 2 * rhs] + mixed[2 * rhs :]
        by_row = jnp.stack([mixed[:, j * nx : (j + 1) * nx] for j in range(8)], axis=0)
        by_rhs = pltpu.einshape("abc->bac", by_row)
        cells = pl.ds(pl.multiple_of(y + MARGIN, 8), 8)
        here = pl.ds(group * 8, 8)
        iterate_out[:, 0, here] = iterate[:, 0, here] + by_rhs[:rhs] * inverse[plane + REACH, cells]
        residual_out[:, 0, here] = by_rhs[rhs:] * root[plane + REACH, cells]
        return carry

    lax.fori_loop(0, rows // 8, group_of_rows, 0, unroll=True)


def on_device(iterate, residual, labels, boundary):
    rhs, depth, rows, nx = residual.shape
    assert depth == 2 and REACH == 3 and rows % rhs == 0 and rhs % 8 == 0 and lax.axis_size("gz") % 2 == 0
    odd = (lax.axis_index("gz") % 2).astype(jnp.int32).reshape(1)
    vmem = pl.BlockSpec(memory_space=pltpu.VMEM)
    smem = pl.BlockSpec(memory_space=pltpu.SMEM)

    def array(*shape, dtype=f32):
        return jax.ShapeDtypeStruct(shape, dtype)

    def params(mib):
        return pltpu.CompilerParams(vmem_limit_bytes=mib * 2**20)

    anywhere = pl.BlockSpec(memory_space=pl.ANY)

    count = rows // rhs
    hbm = pl.BlockSpec(memory_space=pltpu.HBM)
    edge = (array(REACH, rhs, nx),) * 2
    plane_block = pltpu.VMEM((rhs, rows, nx), f32)
    mine, far_first, far_last = pl.pallas_call(
        far_kernel,
        out_shape=(array(rows + 4 * count, rhs, nx),) + edge,
        in_specs=[smem, hbm, hbm, hbm],
        out_specs=(vmem,) * 3,
        scratch_shapes=[
            plane_block,
            pltpu.VMEM(labels.shape, jnp.int32),
            pltpu.VMEM(boundary.shape, jnp.int32),
            pltpu.SemaphoreType.DMA((3,)),
        ],
        compiler_params=params(58),
    )(odd, residual, labels, boundary)
    ahead, near_first, near_last = pl.pallas_call(
        near_kernel,
        out_shape=(array(rows + 3 * count, rhs, nx),) + edge,
        in_specs=[smem, hbm, hbm],
        out_specs=(vmem,) * 3,
        scratch_shapes=[plane_block, pltpu.VMEM((4 * count, rhs, nx), f32), pltpu.SemaphoreType.DMA((2,))],
        compiler_params=params(52),
    )(odd, residual, mine)
    edges = jnp.stack([far_first, near_first]), jnp.stack([far_last, near_last])

    first_swap = swapped(mine)
    far3 = relayed(ahead)
    near3 = relayed(mine, back=True)
    own_before, own_behind = rows_beside(*edges)
    second = pl.pallas_call(
        partial(second_kernel, rows),
        out_shape=array(rows + 2, rhs, nx),
        in_specs=[vmem] * 3,
        out_specs=vmem,
        compiler_params=params(8),
    )(ahead, own_before, own_behind)
    def handed_on(block, earlier):
        return pl.pallas_call(
            hand_on,
            out_shape=array(*block.shape),
            in_specs=[anywhere] * 2,
            out_specs=anywhere,
            input_output_aliases={0: 0},
            compiler_params=params(8),
        )(block, earlier)

    near2 = handed_on(first_swap, second)
    near1 = swapped(handed_on(second, near2))
    def copied(number, first, source, *earlier):
        return pl.pallas_call(
            partial(copy_kernel, first),
            out_shape=array(number, rhs, nx),
            in_specs=[vmem] + [anywhere] * len(earlier),
            out_specs=vmem,
            compiler_params=params(8),
        )(source, *earlier)

    far1 = relayed(copied(rows, 0, near2))
    beyond = swapped(handed_on(copied(4 * count, rows, near3, far3), near1))
    far2 = relayed(near1)

    edges = EDGES + sum(part is not None for _, *parts in FIELDS for part in parts)
    before, behind = rows_beside(
        *pl.pallas_call(
            partial(edges_kernel, rows),
            out_shape=(array(edges, rhs, nx),) * 2,
            in_specs=[vmem] * 7,
            out_specs=(vmem, vmem),
            compiler_params=params(12),
        )(near1, near2, far1, beyond, far3, near3, mine)
    )

    def planes(number):
        return (number, rows + 2 * REACH, rhs, nx)

    cells = (depth + 2 * REACH, rows + 2 * MARGIN, nx)
    inverse, sx, sy, sz, root, u0, u1, u2, split01, moments = pl.pallas_call(
        partial(early_kernel, rows),
        out_shape=(array(*cells),) * 5
        + tuple(array(*planes(number)) for number in (3, 2, 2))
        + (array(depth, rows, 4 * rhs, nx, dtype=bf16), array(rhs, 128)),
        in_specs=[vmem] * 12,
        out_specs=(vmem,) * 10,
        scratch_shapes=[pltpu.VMEM(planes(number), f32) for number in (4, 2)]
        + [pltpu.VMEM((cells[0] + 2,) + cells[1:], f32)] * 2
        + [pltpu.VMEM(cells, f32)],
        compiler_params=params(24),
    )(far3, far1, beyond, mine, ahead, own_before, own_behind, near1, near2, near3, before, behind)

    moments, split23 = pl.pallas_call(
        partial(late_kernel, rows),
        out_shape=(array(rhs, 128), array(depth, rows, 4 * rhs, nx, dtype=bf16)),
        in_specs=[vmem] * 9,
        out_specs=(vmem, vmem),
        scratch_shapes=[pltpu.VMEM(planes(number), f32) for number in (1, 2, 2)],
        compiler_params=params(20),
    )(far2, u0, u1, u2, moments, inverse, sx, sy, sz)

    moments = all_sum(moments, ("gy", "gz"))

    tile = math.gcd(rows, 32)
    plane_rows = pl.BlockSpec((rhs, 1, tile, nx), lambda z, y, odd: (0, jnp.bitwise_xor(z, odd[0]), y, 0))
    return pl.pallas_call(
        outputs_kernel,
        out_shape=(array(*iterate.shape), array(*residual.shape)),
        grid_spec=pltpu.PrefetchScalarGridSpec(
            num_scalar_prefetch=1,
            grid=(depth, rows // tile),
            in_specs=[vmem] * 5 + [plane_rows],
            out_specs=(plane_rows, plane_rows),
            scratch_shapes=[pltpu.VMEM((4 * rhs, 8 * rhs), bf16)],
        ),
        compiler_params=params(16),
    )(odd, moments, split01, split23, inverse, root, iterate)


def solution(mesh):
    placed = (
        P(None, ("regions", "gz"), "gy", None),
        P(None, ("regions", "gz"), "gy", None),
        P(("regions", "gz"), "gy", None),
        P(("regions", "gz"), "gy", None),
    )
    return jax.shard_map(
        on_device,
        mesh=mesh,
        in_specs=placed,
        out_specs=(P(None, ("regions", "gz"), "gy", None), P(None, ("regions", "gz"), "gy", None)),
        check_vma=False,
    )
```
